32 devices in a mesh: row: 8 (over z, x), col: 4 (over y, core).
Axes of the slice: x: 2, y: 2, z: 4, core: 2. Of those that a mesh axis runs over, the one named last changes fastest.
Arguments:
- pair: bfloat16 [320, 320, 128], P('row', 'col'), may hold values from -6 to 6
- token_mask: int32 [320], replicated, may hold values from 0 to 1, as said below
- chain_ids: int32 [320], replicated, may hold values from 0 to 7, never falling along the last dimension, each value on 1 to 80 neighbouring positions
- chain_bias: float32 [128], replicated, may hold values from -4 to 4
- in_weights: bfloat16 [2, 128, 640], replicated, may hold values from -0.5 to 0.5
- out_weights: bfloat16 [2, 128, 128], replicated, may hold values from -0.5 to 0.5
Outputs:
- pair_out: bfloat16 [320, 320, 128], P('row', 'col')
The draws below stay inside these ranges and needn't reach their ends.
Inputs may be any that keep to these rules, and one draw needn't show every extreme that they name: token_mask is 0 on a run of padding at the end that always includes the last token; some tokens before it may be 0 as well. chain_ids never falls along the tokens.
All inputs are finite; a program needn't handle non-finite values.
Results may differ from the reference program's by a relative error of at most 0.015.
Values may be sent and summed in bfloat16 or wider, within the bound.
No kernel may reach another device: no remote copies, remote signals or barrier semaphores. Data moves between devices by JAX's collectives and lax.ppermute only.
A program may use at most 128 MiB of HBM per device.

```python
import math
import jax
import jax.numpy as jnp
import numpy as np
from jax import lax

CHANNELS = 128
TOK_ROW = 40
CHAINS = 8
TOKENS = 320
TILE_COL = 80


def draw_token_mask(key, part):
    key = jax.random.fold_in(key, 3)
    length_key, hole_key = jax.random.split(key)
    length = jax.random.randint(length_key, (), TOKENS - TOKENS // 8, TOKENS)
    holes = jax.random.randint(hole_key, (TOKENS,), 0, 16)
    kept = (jnp.arange(TOKENS) < length) & (holes != 0)
    return kept.astype(jnp.int32)


def block_levels(rng, dims, cuts, smallest, high):
    loudness, own = 1.0, jax.random.fold_in(rng, 6)
    for dim, blocks in cuts:
        draws = jnp.exp(jax.random.uniform(jax.random.fold_in(own, dim), (blocks,), jnp.float32, smallest / len(cuts), high / len(cuts)))
        loudness = loudness * jnp.repeat(draws, dims[dim] // blocks).reshape([-1 if axis == dim else 1 for axis in range(len(dims))])
    return loudness


def profile(number_of, total, reach, slope):
    weights = [(1 << 20) // math.isqrt(grade ** slope) + 1 for grade in range(2, number_of + 1)]
    spare, holding = total - reach - (number_of - 1), [1] * (number_of - 1)
    while spare > 0:
        free = [i for i in range(number_of - 1) if holding[i] < reach]
        mass, left = sum([weights[i] for i in free]), spare
        for i in free:
            more = min(reach - holding[i], max(1, left * weights[i] // mass), spare)
            holding[i] = holding[i] + more
            spare = spare - more
    return np.array([reach] + holding)


def ragged_sizes(stream_key, amount, total, limit, skew):
    if amount == 2:
        one = jax.random.randint(stream_key, (), max(1, total - limit), min(limit, total - 1) + 1)
        return jnp.stack([one, total - one])
    sizes = jnp.asarray(profile(amount, total, limit, skew), jnp.int32)
    pairs = (amount - 1) // 2
    giver, taker = sizes[1:1 + 2 * pairs:2], sizes[2:2 + 2 * pairs:2]
    margin = jnp.minimum(giver - 1, limit - taker)
    moved = jax.random.randint(jax.random.fold_in(stream_key, 1), (pairs,), 0, 1 << 20) % (margin + 1)
    sizes = sizes.at[1:1 + 2 * pairs:2].set(giver - moved).at[2:2 + 2 * pairs:2].set(taker + moved)
    return sizes[jax.random.permutation(jax.random.fold_in(stream_key, 2), amount)]


def gaussian(rng, shape, deviation, reach, cuts=(), kind=jnp.bfloat16):
    result = jax.random.normal(rng, shape, jnp.float32) * deviation
    if len(cuts) > 0:
        result = block_levels(rng, shape, cuts, -0.22, 0.18) * result
    return jnp.clip(result, min=-reach, max=reach).astype(kind)


def setup_inputs(seed: int = 0) -> dict:
    key_of = jax.random.split(jax.random.key(seed), 7)
    return {
        "pair": gaussian(key_of[0], (TOKENS, TOKENS, CHANNELS), 1.0, 6.0, ((0, 8), (1, 4))),
        "token_mask": draw_token_mask(jax.random.fold_in(key_of[6], 71), 0),
        "chain_ids": jnp.searchsorted(jnp.cumsum(ragged_sizes(key_of[2], CHAINS, TOKENS, TOKENS // 4, 1)), jnp.arange(TOKENS), side="right").astype(jnp.int32),
        "chain_bias": gaussian(key_of[3], (CHANNELS,), 1.0, 4.0, (), jnp.float32),
        "in_weights": gaussian(key_of[4], (2, CHANNELS, 5 * CHANNELS), CHANNELS ** -0.5, 0.5),
        "out_weights": gaussian(key_of[5], (2, CHANNELS, CHANNELS), CHANNELS ** -0.5, 0.5),
    }


def layer_norm(values):
    center = values - lax.optimization_barrier(jnp.mean(values, axis=-1, keepdims=True))
    spread = lax.optimization_barrier(jnp.mean(center * center, axis=-1, keepdims=True))
    return center * lax.rsqrt(spread + 1e-05)

def rounded(values):
    return lax.optimization_barrier(values.astype(jnp.bfloat16)).astype(jnp.float32)

def reference(pair, token_mask, chain_ids, chain_bias, in_weights, out_weights):
    valid = token_mask.astype(jnp.float32)
    pair_mask = valid[:, None] * valid[None, :]
    same_chain = (chain_ids[:, None] == chain_ids[None, :]).astype(jnp.float32)
    field = pair.astype(jnp.float32) + same_chain[:, :, None] * chain_bias
    for direction in range(2):
        normed = layer_norm(field).astype(jnp.bfloat16)
        projected = jnp.dot(normed.reshape(-1, CHANNELS), in_weights[direction], preferred_element_type=jnp.float32)
        projected = projected.reshape(TOKENS, TOKENS, 5 * CHANNELS)
        width = CHANNELS
        first = (jax.nn.sigmoid(projected[..., :width]) * projected[..., width:2 * width] * pair_mask[:, :, None]).astype(jnp.bfloat16)
        second = (jax.nn.sigmoid(projected[..., 2 * width:3 * width]) * projected[..., 3 * width:4 * width] * pair_mask[:, :, None]).astype(jnp.bfloat16)
        gate_value = jax.nn.sigmoid(projected[..., 4 * width:])
        first_wide = first.astype(jnp.float32)
        second_wide = second.astype(jnp.float32)
        summed = jnp.zeros((TOKENS, TOKENS, CHANNELS), jnp.float32)
        if direction == 0:
            block = TILE_COL
            for index in range(TOKENS // block):
                lo = index * block
                part = jnp.einsum('ikc,jkc->ijc', first_wide[:, lo:lo + block], second_wide[:, lo:lo + block], precision=lax.Precision.HIGHEST)
                summed = summed + rounded(part)
        else:
            block = TOK_ROW
            for index in range(TOKENS // block):
                lo = index * block
                part = jnp.einsum('kic,kjc->ijc', first_wide[lo:lo + block], second_wide[lo:lo + block], precision=lax.Precision.HIGHEST)
                summed = summed + rounded(part)
        normed_sum = layer_norm(summed).astype(jnp.bfloat16)
        output = jnp.dot(normed_sum.reshape(-1, CHANNELS), out_weights[direction], preferred_element_type=jnp.float32)
        field = field + gate_value * output.reshape(TOKENS, TOKENS, CHANNELS)
    return field.astype(jnp.bfloat16)
```

```python
import functools

import jax
import jax.numpy as jnp
from jax import lax
from jax.experimental import pallas as pl
from jax.experimental.pallas import tpu as pltpu
from jax.sharding import PartitionSpec as P

LANES = 128
SUB = 8
F32 = jnp.float32
BF16 = jnp.bfloat16


def layer_norm(values, axis=-1):
    center = values - jnp.mean(values, axis=axis, keepdims=True)
    spread = jnp.mean(center * center, axis=axis, keepdims=True)
    return center * lax.rsqrt(spread + 1e-05)


def matmul(left, right, dims):
    return lax.dot_general(left, right, (dims, ((), ())), preferred_element_type=F32)


def identity(size, scale):
    row = lax.broadcasted_iota(jnp.int32, (size, size), 0)
    col = lax.broadcasted_iota(jnp.int32, (size, size), 1)
    return jnp.where(row == col, scale, 0.0).astype(BF16)


def column(row_ref):
    width = row_ref.shape[1]
    return jnp.broadcast_to(row_ref[...], (width, width)).T[:, 0:1]


def first_field(pair_ref, eye, bias_col, same, group, lanes):
    rows = pair_ref[group * lanes : (group + 1) * lanes, :]
    return matmul(eye, rows, ((1,), (1,))) + bias_col * same


def transposed(weights, scale):
    eye = identity(weights.shape[1], scale)
    return matmul(eye, weights, ((1,), (1,))).astype(BF16)


def interleaved(first, second, share):
    width = first.shape[1]
    both = jnp.concatenate([first, second], axis=1)
    row = lax.broadcasted_iota(jnp.int32, (2 * width, 1), 0)
    col = lax.broadcasted_iota(jnp.int32, (2 * width, 2 * width), 1)
    owner, place = row // (2 * share), row % (2 * share)
    source = owner * share + place % share + jnp.where(place >= share, width, 0)
    pick = jnp.where(col == source, 0.5, 0.0).astype(BF16)
    return matmul(pick, both, ((1,), (1,))).astype(BF16)


def load_in_weights(weights, share):
    width = weights.shape[0]
    blocks = [weights[:, k * width : (k + 1) * width] for k in range(5)]
    return (
        interleaved(blocks[0], blocks[2], share),
        interleaved(blocks[1], blocks[3], share),
        transposed(blocks[4], 0.5),
    )


def token_vectors(tokens, row_start, col_start, rows, cols):
    groups = rows // SUB
    wide = tokens.shape[1]
    many = jnp.broadcast_to(tokens.astype(F32), (SUB, wide))
    lane = lax.broadcasted_iota(jnp.int32, (1, SUB * cols), 1)
    at_row = jnp.zeros_like(lane)
    for step in range(1, SUB):
        at_row = at_row + jnp.where(lane >= step * cols, 1, 0)
    at_col = lane - at_row * cols
    key = lax.broadcasted_iota(jnp.int32, (LANES, SUB * cols), 0)
    pick_row = jnp.where(key == at_row, 1.0, 0.0).astype(BF16)
    pick_col = jnp.where(key == at_col, 1.0, 0.0).astype(BF16)

    def window(start):
        return pltpu.roll(many, wide - start, 1)[:, :LANES]

    by_col = matmul(window(col_start).astype(BF16), pick_col, ((1,), (0,)))[0:1]
    windows = [window(row_start + group * SUB)[0:1] for group in range(groups)]
    windows.append(jnp.zeros((-groups % SUB, LANES), F32))
    by_row = matmul(jnp.concatenate(windows, axis=0).astype(BF16), pick_row, ((1,), (0,)))
    by_row = by_row.astype(jnp.int32)
    by_col = by_col.astype(jnp.int32)
    masks = (by_row & by_col & 1).astype(F32)
    sames = jnp.where((by_row >> 1) == (by_col >> 1), 1.0, 0.0)
    return masks, sames


def send_inputs(field, mask, in_t, group, share, sent_ref, gate_ref):
    width = field.shape[0]
    lanes = field.shape[1]
    pieces = lanes // LANES
    normed = layer_norm(field, 0).astype(BF16)
    gates_t, values_t, out_gate_t = in_t
    gates = jnp.tanh(matmul(gates_t, normed, ((1,), (0,))))
    values = matmul(values_t, normed, ((1,), (0,)))
    sent = (gates * values + values) * mask
    gate = jnp.tanh(matmul(out_gate_t, normed, ((1,), (0,))))
    gate_ref[:, group * lanes : (group + 1) * lanes] = gate
    for owner in range(width // share):
        block = sent[owner * 2 * share : (owner + 1) * 2 * share]
        lines = [block[:, piece * LANES : (piece + 1) * LANES] for piece in range(pieces)]
        sent_ref[owner, group] = jnp.concatenate(lines, axis=0).astype(BF16)


def start_kernel(share, rows, cols, mask_hbm, chain_hbm, pair_hbm, bias_hbm, w_hbm,
                 sent_hbm, gate_hbm, mask_same_hbm, sent_ref, gate_ref, mask_same_ref,
                 pair_ref, w_ref, bias_ref, valid_ref, chain_ref, sems):
    lanes = SUB * cols
    groups = rows // SUB
    width = pair_ref.shape[1]
    count = mask_hbm.shape[0]
    copies = [
        pltpu.make_async_copy(mask_hbm, valid_ref.at[0], sems.at[0]),
        pltpu.make_async_copy(chain_hbm, chain_ref.at[0], sems.at[1]),
        pltpu.make_async_copy(w_hbm.at[0], w_ref, sems.at[2]),
        pltpu.make_async_copy(bias_hbm, bias_ref.at[0], sems.at[3]),
    ]
    for group in range(groups):
        at = pl.ds(group * lanes, lanes)
        copies.append(pltpu.make_async_copy(pair_hbm.at[at], pair_ref.at[at], sems.at[4 + group]))
    for copy in copies:
        copy.start()
    eye = identity(width, 1.0)
    copies[0].wait()
    copies[1].wait()
    row_start = lax.axis_index("row") * rows
    col_start = lax.axis_index("col") * cols
    tokens = chain_ref[...] * 2 + valid_ref[...]
    tokens = jnp.concatenate([tokens, jnp.zeros((1, -count % LANES), jnp.int32)], axis=1)
    masks, sames = token_vectors(tokens, row_start, col_start, rows, cols)
    copies[3].wait()
    bias_col = column(bias_ref)
    copies[2].wait()
    in_t = load_in_weights(w_ref[...], share)
    outs = []
    for group in range(groups):
        copies[4 + group].wait()
        at = slice(group * lanes, (group + 1) * lanes)
        mask = masks[group : group + 1]
        same = sames[group : group + 1]
        field = first_field(pair_ref, eye, bias_col, same, group, lanes)
        mask_same_ref[:, at] = jnp.concatenate([mask, same], axis=0)
        send_inputs(field, mask, in_t, group, share, sent_ref, gate_ref)
        at = pl.ds(group * lanes, lanes)
        sem = sems.at[4 + groups + group]
        outs.append(pltpu.make_async_copy(gate_ref.at[:, at], gate_hbm.at[:, at], sem))
        sem = sems.at[4 + 2 * groups + group]
        outs.append(pltpu.make_async_copy(sent_ref.at[:, group], sent_hbm.at[:, group], sem))
        outs[-2].start()
        outs[-1].start()
    outs.append(pltpu.make_async_copy(mask_same_ref, mask_same_hbm, sems.at[4 + 3 * groups]))
    outs[-1].start()
    for copy in outs:
        copy.wait()


def updated(wide, field, gate, out_t, group, line):
    width, lanes = field.shape
    pieces = lanes // LANES
    parts = []
    for piece in range(pieces):
        parts.append(wide[pl.ds(group * pieces + piece, width, stride=line), :])
    summed = jnp.concatenate(parts, axis=1)
    normed = layer_norm(summed, 0).astype(BF16)
    output = matmul(out_t, normed, ((1,), (0,)))
    return field + (gate * output + output)


def middle_kernel(share, rows, cols, line, mask_same_ref, got_ref, pair_ref, bias_ref, gate_in,
                  wo_ref, w_ref, sent_ref, gate_ref, field_ref, wide):
    lanes = SUB * cols
    width = pair_ref.shape[1]
    in_t = load_in_weights(w_ref[1], share)
    out_t = transposed(wo_ref[0], 0.5)
    eye = identity(width, 1.0)
    bias_col = column(bias_ref)
    wide[...] = got_ref[...].astype(F32)
    for group in range(rows // SUB):
        at = slice(group * lanes, (group + 1) * lanes)
        field = first_field(pair_ref, eye, bias_col, mask_same_ref[1:2, at], group, lanes)
        field = updated(wide, field, gate_in[:, at], out_t, group, line)
        field_ref[:, at] = field
        send_inputs(field, mask_same_ref[0:1, at], in_t, group, share, sent_ref, gate_ref)


def end_kernel(rows, cols, line, got_ref, field_in, gate_in, wo_ref, out_ref, wide):
    lanes = SUB * cols
    out_t = transposed(wo_ref[1], 0.5)
    wide[...] = got_ref[...].astype(F32)
    for group in range(rows // SUB):
        at = slice(group * lanes, (group + 1) * lanes)
        field = updated(wide, field_in[:, at], gate_in[:, at], out_t, group, line)
        out_ref[at, :] = field.T.astype(BF16)


def moved(source, moves, count):
    shape = None
    lane = None
    targets = [[] for _ in range(count)]
    for row, begin, length, target in moves:
        shift = (target - begin) % LANES
        while length > 0:
            size = min(length, LANES - begin % LANES, LANES - target % LANES)
            targets[target // LANES].append((target % LANES, row, begin // LANES, shift))
            begin, target, length = begin + size, target + size, length - size
    rolled = {}
    registers = []
    for pieces in targets:
        value = None
        for start, row, register, shift in sorted(pieces, key=lambda piece: piece[0]):
            key = (row, register, shift)
            if key not in rolled:
                tile = source(row, register)
                rolled[key] = pltpu.roll(tile, shift, 1) if shift else tile
            if value is None:
                value = rolled[key]
            else:
                if lane is None:
                    shape = value.shape
                    lane = lax.broadcasted_iota(jnp.int32, shape, 1)
                value = jnp.where(lane < start, value, rolled[key])
        registers.append(value)
    return registers


def wide_steps(tiles):
    place_step = tiles + 1 - tiles % 2
    return place_step, SUB * place_step + 1


def stacked(low, high):
    return jnp.concatenate([low, high], axis=0).astype(BF16)


def triangle_kernel(direction, share, rows, cols, row_devices, col_devices, line, got_ref, sent_ref,
                    wide, left_ref, right_ref, even_ref, result_ref, packed):
    groups = rows // SUB
    pieces = SUB * cols // LANES
    total = row_devices * rows
    blocks = -(-total // LANES)
    pairs = -(-groups // 2)
    rest = total - (blocks - 1) * LANES
    tail = lax.broadcasted_iota(jnp.int32, (2 * SUB, LANES), 1) < rest
    place_step, row_step = wide_steps(col_devices * groups * pieces)

    def spot(tile):
        device, number = divmod(tile, groups * pieces)
        col, row = divmod(device, row_devices)
        return row * row_step + col * groups * pieces + number

    for unit in range(got_ref.shape[0] // (2 * SUB)):
        both = got_ref[unit * 2 * SUB : (unit + 1) * 2 * SUB, :].astype(F32)
        for half in range(2):
            at = pl.ds(spot(2 * unit + half), SUB, stride=place_step)
            wide[at, :] = both[half * SUB : (half + 1) * SUB]

    def loaded(place, group, col, piece):
        if group >= groups:
            return jnp.zeros((SUB, LANES), F32)
        start = place * place_step + (col * groups + group) * pieces + piece
        return wide[pl.ds(start, row_devices, stride=row_step), :]

    for channel in range(share):
        spare = channel % 2
        for is_right, place in ((False, channel), (True, share + channel)):
            for pair in range(pairs):
                tiles = {}
                for col in range(col_devices):
                    for piece in range(pieces):
                        tiles[col, piece] = stacked(
                            loaded(place, 2 * pair, col, piece), loaded(place, 2 * pair + 1, col, piece)
                        )
                for step in range(SUB):
                    moves = [(col, step * cols, cols, col * cols) for col in range(col_devices)]
                    registers = moved(lambda col, piece: tiles[col, piece], moves, blocks)
                    registers[-1] = jnp.where(tail, registers[-1], jnp.zeros_like(registers[-1]))
                    for block in range(blocks):
                        if is_right and direction == 0:
                            both = registers[block].astype(F32)
                            for half in range(2):
                                group = 2 * pair + half
                                if group < groups:
                                    at = pl.ds(group * SUB + step, row_devices, stride=rows)
                                    even_ref[spare, block, at, :] = both[half * SUB : (half + 1) * SUB]
                        else:
                            target = right_ref if is_right else left_ref
                            start = (pair * SUB + step) * 2 * SUB
                            target[spare, start : start + 2 * SUB, block * LANES : (block + 1) * LANES] = (
                                registers[block]
                            )
        if direction == 0:
            right = [even_ref[spare, block].astype(BF16) for block in range(blocks)]
            right = jnp.concatenate(right, axis=1)
            summed = matmul(left_ref[spare], right, ((1,), (1,)))
            for block in range(blocks):
                size = min(LANES, total - block * LANES)
                part = summed[:, block * LANES : block * LANES + size].astype(BF16)
                result_ref[spare, block, :, 0:size] = part
        else:
            summed = matmul(left_ref[spare], right_ref[spare], ((0,), (0,)))
            for block in range(blocks):
                result_ref[spare, block] = summed[:, block * LANES : (block + 1) * LANES]

        def result_at(pair, step, block):
            if direction == 0:
                start = (pair * SUB + step) * 2 * SUB
                return result_ref[spare, block, start : start + 2 * SUB, :]
            halves = []
            for group in (2 * pair, 2 * pair + 1):
                if group < groups:
                    at = pl.ds(group * SUB + step, row_devices, stride=rows)
                    halves.append(result_ref[spare, block, at, :])
                else:
                    halves.append(jnp.zeros((SUB, LANES), F32))
            return stacked(*halves)

        for pair in range(pairs):
            tiles = {}
            for step in range(SUB):
                for block in range(blocks):
                    tiles[step, block] = result_at(pair, step, block)
            for col in range(col_devices):
                moves = [(step, col * cols, cols, step * cols) for step in range(SUB)]
                registers = moved(lambda step, block: tiles[step, block], moves, pieces)
                for piece in range(pieces):
                    both = registers[piece].astype(F32)
                    for half in range(2):
                        group = 2 * pair + half
                        if group < groups:
                            start = (col * row_devices * share + channel) * line + group * pieces + piece
                            packed[pl.ds(start, row_devices, stride=share * line), :] = (
                                both[half * SUB : (half + 1) * SUB]
                            )
    sent_ref[...] = packed[...].astype(BF16)


def by_channels(pair, token_mask, chain_ids, chain_bias, in_weights, out_weights, row_devices, col_devices):
    rows, cols, width = pair.shape
    devices = row_devices * col_devices
    share = width // devices
    lanes = SUB * cols
    pieces = lanes // LANES
    groups = rows // SUB
    chunk = groups * pieces * SUB
    spots = rows * cols
    line = -(-groups * pieces * share // SUB) * SUB // share
    total = row_devices * rows
    blocks = -(-total // LANES)
    tall = -(-groups // 2) * 2 * SUB * row_devices
    params = pltpu.CompilerParams(vmem_limit_bytes=40 * 1024 * 1024)
    whole = pl.BlockSpec(memory_space=pltpu.VMEM)
    far = pl.BlockSpec(memory_space=pltpu.HBM)

    sent_shape = jax.ShapeDtypeStruct((devices, groups, pieces * SUB, LANES), BF16)
    sum_shape = jax.ShapeDtypeStruct((devices * share * line, LANES), BF16)
    state_shape = jax.ShapeDtypeStruct((width, spots), F32)
    flags_shape = jax.ShapeDtypeStruct((2, spots), F32)

    def exchange(array, rows):
        split = array.reshape(devices, rows, LANES)
        return lax.all_to_all(split, ("col", "row"), 0, 0, tiled=True).reshape(devices * rows, LANES)

    def triangle(direction, sent):
        result_rows, result_type = (tall, BF16) if direction == 0 else (blocks * LANES, F32)
        wide_rows = row_devices * wide_steps(col_devices * groups * pieces)[1]
        summed = pl.pallas_call(
            functools.partial(
                triangle_kernel, direction, share, rows, cols, row_devices, col_devices, line
            ),
            out_shape=sum_shape,
            in_specs=[whole],
            out_specs=whole,
            scratch_shapes=[
                pltpu.VMEM((-(-wide_rows // SUB) * SUB, LANES), F32),
                pltpu.VMEM((2, tall, blocks * LANES), BF16),
                pltpu.VMEM((2, tall, blocks * LANES), BF16),
                pltpu.VMEM((2, blocks, total, LANES), F32),
                pltpu.VMEM((2, blocks, result_rows, LANES), result_type),
                pltpu.VMEM(sum_shape.shape, F32),
            ],
            compiler_params=params,
            name="triangle",
        )(exchange(sent, chunk))
        return exchange(summed, share * line)

    flat_pair = pair.reshape(spots, width)
    flat_bias = chain_bias.reshape(1, width)
    sent, gate, flags = pl.pallas_call(
        functools.partial(start_kernel, share, rows, cols),
        out_shape=[sent_shape, state_shape, flags_shape],
        in_specs=[far] * 5,
        out_specs=[far] * 3,
        scratch_shapes=[
            pltpu.VMEM(sent_shape.shape, BF16),
            pltpu.VMEM(state_shape.shape, F32),
            pltpu.VMEM(flags_shape.shape, F32),
            pltpu.VMEM((spots, width), BF16),
            pltpu.VMEM(in_weights.shape[1:], BF16),
            pltpu.VMEM((1, width), F32),
            pltpu.VMEM((1,) + token_mask.shape, jnp.int32),
            pltpu.VMEM((1,) + chain_ids.shape, jnp.int32),
            pltpu.SemaphoreType.DMA((5 + 3 * groups,)),
        ],
        compiler_params=pltpu.CompilerParams(vmem_limit_bytes=60 * 1024 * 1024),
        name="start",
    )(token_mask, chain_ids, flat_pair, chain_bias, in_weights)
    got = triangle(0, sent)
    sent, gate, field = pl.pallas_call(
        functools.partial(middle_kernel, share, rows, cols, line),
        out_shape=[sent_shape, state_shape, state_shape],
        in_specs=[whole] * 7,
        out_specs=[whole] * 3,
        scratch_shapes=[pltpu.VMEM(sum_shape.shape, F32)],
        compiler_params=params,
        name="middle",
    )(flags, got, flat_pair, flat_bias, gate, out_weights, in_weights)
    got = triangle(1, sent)
    out = pl.pallas_call(
        functools.partial(end_kernel, rows, cols, line),
        out_shape=jax.ShapeDtypeStruct((spots, width), BF16),
        in_specs=[whole] * 4,
        out_specs=whole,
        scratch_shapes=[pltpu.VMEM(sum_shape.shape, F32)],
        compiler_params=params,
        name="end",
    )(got, field, gate, out_weights)
    return out.reshape(pair.shape)


def gated_inputs(field, weights, pair_mask):
    width = weights.shape[0]
    normed = layer_norm(field).astype(BF16)
    projected = jnp.einsum("ijc,cd->ijd", normed, weights, preferred_element_type=F32)
    first = (
        jax.nn.sigmoid(projected[..., :width])
        * projected[..., width : 2 * width]
        * pair_mask[:, :, None]
    ).astype(BF16)
    second = (
        jax.nn.sigmoid(projected[..., 2 * width : 3 * width])
        * projected[..., 3 * width : 4 * width]
        * pair_mask[:, :, None]
    ).astype(BF16)
    gate_value = jax.nn.sigmoid(projected[..., 4 * width :])
    return (first, second, gate_value)


def update(field, summed, gate_value, weights):
    normed_sum = layer_norm(summed).astype(BF16)
    output = jnp.einsum("ijc,cd->ijd", normed_sum, weights, preferred_element_type=F32)
    return field + gate_value * output


def by_blocks(pair, token_mask, chain_ids, chain_bias, in_weights, out_weights):
    row_count = pair.shape[0]
    col_count = pair.shape[1]
    row_start = lax.axis_index("row") * row_count
    col_start = lax.axis_index("col") * col_count
    valid_rows = lax.dynamic_slice_in_dim(token_mask, row_start, row_count).astype(F32)
    valid_cols = lax.dynamic_slice_in_dim(token_mask, col_start, col_count).astype(F32)
    chain_rows = lax.dynamic_slice_in_dim(chain_ids, row_start, row_count)
    chain_cols = lax.dynamic_slice_in_dim(chain_ids, col_start, col_count)
    pair_mask = valid_rows[:, None] * valid_cols[None, :]
    same_chain = (chain_rows[:, None] == chain_cols[None, :]).astype(F32)
    field = pair.astype(F32) + same_chain[:, :, None] * chain_bias
    first, second, gate_value = gated_inputs(field, in_weights[0], pair_mask)
    second_rows = lax.all_gather(second, "row", axis=0, tiled=True)
    part = jnp.einsum("jkc,ikc->jic", second_rows, first, preferred_element_type=F32).astype(BF16)
    summed = lax.psum_scatter(part, "col", scatter_dimension=0, tiled=True).astype(F32)
    summed = jnp.transpose(summed, (1, 0, 2))
    field = update(field, summed, gate_value, out_weights[0])
    first, second, gate_value = gated_inputs(field, in_weights[1], pair_mask)
    first_cols = lax.all_gather(first, "col", axis=1, tiled=True)
    part = jnp.einsum("kic,kjc->ijc", first_cols, second, preferred_element_type=F32).astype(BF16)
    summed = lax.psum_scatter(part, "row", scatter_dimension=0, tiled=True).astype(F32)
    field = update(field, summed, gate_value, out_weights[1])
    return field.astype(BF16)


def solution(mesh):
    row_devices, col_devices = mesh.shape["row"], mesh.shape["col"]

    def per_device(pair, *rest):
        rows, cols, width = pair.shape
        devices = row_devices * col_devices
        fits = (
            width % devices == 0
            and 2 * (width // devices) == SUB
            and row_devices == SUB
            and rows % SUB == 0
            and (SUB * cols) % LANES == 0
            and max(rows, cols) <= LANES
        )
        if fits:
            return by_channels(pair, *rest, row_devices, col_devices)
        return by_blocks(pair, *rest)

    return jax.shard_map(
        per_device,
        mesh=mesh,
        in_specs=(P("row", "col", None), P(), P(), P(), P(), P()),
        out_specs=P("row", "col", None),
        check_vma=False,
    )
```

```python
import functools

import jax
import jax.numpy as jnp
from jax import lax
from jax.experimental import pallas as pl
from jax.experimental.pallas import tpu as pltpu
from jax.sharding import PartitionSpec as P

LANES = 128
SUB = 8
F32 = jnp.float32
BF16 = jnp.bfloat16


def layer_norm(values, axis=-1):
    center = values - jnp.mean(values, axis=axis, keepdims=True)
    spread = jnp.mean(center * center, axis=axis, keepdims=True)
    return center * lax.rsqrt(spread + 1e-05)


def matmul(left, right, dims):
    return lax.dot_general(left, right, (dims, ((), ())), preferred_element_type=F32)


def identity(size, scale):
    row = lax.broadcasted_iota(jnp.int32, (size, size), 0)
    col = lax.broadcasted_iota(jnp.int32, (size, size), 1)
    return jnp.where(row == col, scale, 0.0).astype(BF16)


def column(row_ref):
    width = row_ref.shape[1]
    return jnp.broadcast_to(row_ref[...], (width, width)).T[:, 0:1]


def transposed(weights, scale):
    eye = identity(weights.shape[1], scale)
    return matmul(eye, weights, ((1,), (1,))).astype(BF16)


def interleaved(first, second, share):
    width = first.shape[1]
    both = jnp.concatenate([first, second], axis=1)
    row = lax.broadcasted_iota(jnp.int32, (2 * width, 1), 0)
    col = lax.broadcasted_iota(jnp.int32, (2 * width, 2 * width), 1)
    owner, place = row // (2 * share), row % (2 * share)
    source = owner * share + place % share + jnp.where(place >= share, width, 0)
    pick = jnp.where(col == source, 0.5, 0.0).astype(BF16)
    return matmul(pick, both, ((1,), (1,))).astype(BF16)


def load_in_weights(weights, share):
    width = weights.shape[0]
    blocks = [weights[:, k * width : (k + 1) * width] for k in range(5)]
    return (
        interleaved(blocks[0], blocks[2], share),
        interleaved(blocks[1], blocks[3], share),
        transposed(blocks[4], 0.5),
    )


def token_vectors(tokens, row_start, col_start, rows, cols):
    groups = rows // SUB
    wide = tokens.shape[1]
    many = jnp.broadcast_to(tokens.astype(F32), (SUB, wide))
    lane = lax.broadcasted_iota(jnp.int32, (1, SUB * cols), 1)
    at_row = jnp.zeros_like(lane)
    for step in range(1, SUB):
        at_row = at_row + jnp.where(lane >= step * cols, 1, 0)
    at_col = lane - at_row * cols
    key = lax.broadcasted_iota(jnp.int32, (LANES, SUB * cols), 0)
    pick_row = jnp.where(key == at_row, 1.0, 0.0).astype(BF16)
    pick_col = jnp.where(key == at_col, 1.0, 0.0).astype(BF16)

    def window(start):
        return pltpu.roll(many, wide - start, 1)[:, :LANES]

    by_col = matmul(window(col_start).astype(BF16), pick_col, ((1,), (0,)))[0:1]
    windows = [window(row_start + group * SUB)[0:1] for group in range(groups)]
    windows.append(jnp.zeros((-groups % SUB, LANES), F32))
    by_row = matmul(jnp.concatenate(windows, axis=0).astype(BF16), pick_row, ((1,), (0,)))
    by_row = by_row.astype(jnp.int32)
    by_col = by_col.astype(jnp.int32)
    masks = (by_row & by_col & 1).astype(F32)
    sames = jnp.where((by_row >> 1) == (by_col >> 1), 1.0, 0.0)
    return masks, sames


def staged(count, stages):
    held = {}
    for step in range(count + len(stages) - 1):
        for number, stage in enumerate(stages):
            item = step - number
            if 0 <= item < count:
                held[item] = stage(item, held.get(item))


def projected(field, in_t):
    normed = layer_norm(field, 0).astype(BF16)
    return [matmul(weights, normed, ((1,), (0,))) for weights in in_t]


def gated(products, mask, group, share, sent_ref, gate_ref):
    gates, values, gate = products
    width, lanes = gate.shape
    sent = (jnp.tanh(gates) * values + values) * mask
    for owner in range(width // share):
        block = sent[owner * 2 * share : (owner + 1) * 2 * share]
        lines = [block[:, at : at + LANES] for at in range(0, lanes, LANES)]
        sent_ref[owner, group] = jnp.concatenate(lines, axis=0).astype(BF16)
    gate_ref[:, group * lanes : (group + 1) * lanes] = jnp.tanh(gate)


def start_kernel(share, rows, cols, valid_hbm, chain_hbm, pair_hbm, bias_hbm, w_hbm,
                 sent_hbm, gate_hbm, field_hbm, mask_hbm, sent_ref, gate_ref, field_ref, mask_ref,
                 pair_ref, w_ref, bias_ref, valid_ref, chain_ref, sems):
    lanes = SUB * cols
    groups = rows // SUB
    width = pair_ref.shape[1]
    count = valid_hbm.shape[0]
    started = []

    def copy(near, far):
        started.append(pltpu.make_async_copy(near, far, sems.at[len(started)]))
        started[-1].start()

    copy(valid_hbm, valid_ref.at[0])
    copy(chain_hbm, chain_ref.at[0])
    copy(w_hbm.at[0], w_ref)
    copy(bias_hbm, bias_ref.at[0])
    copy(pair_hbm, pair_ref)
    arriving = len(started)
    eye = identity(width, 1.0)
    row_start = lax.axis_index("row") * rows
    col_start = lax.axis_index("col") * cols
    for number in range(arriving):
        started[number].wait()
    tokens = chain_ref[...] * 2 + valid_ref[...]
    tokens = jnp.concatenate([tokens, jnp.zeros((1, -count % LANES), jnp.int32)], axis=1)
    masks, sames = token_vectors(tokens, row_start, col_start, rows, cols)
    in_t = load_in_weights(w_ref[...], share)
    bias_col = column(bias_ref)
    early = groups // 2 * lanes

    def make_field(group, _):
        at = slice(group * lanes, (group + 1) * lanes)
        field = matmul(eye, pair_ref[at, :], ((1,), (1,))) + bias_col * sames[group : group + 1]
        field_ref[:, at] = field
        mask_ref[:, at] = masks[group : group + 1]
        return field

    def project(group, field):
        if group == groups - 1:
            copy(field_ref, field_hbm)
            copy(mask_ref, mask_hbm)
        return projected(field, in_t)

    def finish(group, products):
        gated(products, masks[group : group + 1], group, share, sent_ref, gate_ref)
        copy(sent_ref.at[:, group], sent_hbm.at[:, group])
        if (group + 1) * lanes == early:
            copy(gate_ref.at[:, 0:early], gate_hbm.at[:, 0:early])

    staged(groups, (make_field, project, finish))
    late = pl.ds(early, groups * lanes - early)
    copy(gate_ref.at[:, late], gate_hbm.at[:, late])
    for number in range(arriving, len(started)):
        started[number].wait()


def output_of(wide, out_t, group, lanes, line):
    width = out_t.shape[1]
    pieces = lanes // LANES
    parts = []
    for piece in range(pieces):
        parts.append(wide[pl.ds(group * pieces + piece, width, stride=line), :])
    normed = layer_norm(jnp.concatenate(parts, axis=1), 0).astype(BF16)
    return matmul(out_t, normed, ((1,), (0,)))


def middle_kernel(share, rows, cols, line, mask_ref, got_ref, field_in, gate_in, wo_ref, w_ref,
                  sent_ref, gate_ref, field_ref, wide):
    lanes = SUB * cols
    in_t = load_in_weights(w_ref[1], share)
    out_t = transposed(wo_ref[0], 0.5)
    wide[...] = got_ref[...].astype(F32)

    def span(group):
        return slice(group * lanes, (group + 1) * lanes)

    def outgoing(group, _):
        return output_of(wide, out_t, group, lanes, line)

    def project(group, output):
        at = span(group)
        field = field_in[:, at] + (gate_in[:, at] * output + output)
        field_ref[:, at] = field
        return projected(field, in_t)

    def finish(group, products):
        gated(products, mask_ref[:, span(group)], group, share, sent_ref, gate_ref)

    staged(rows // SUB, (outgoing, project, finish))


def end_kernel(rows, cols, line, got_ref, field_in, gate_in, wo_ref, out_hbm, wide, out_ref, sems):
    lanes = SUB * cols
    out_t = transposed(wo_ref[1], 0.5)
    wide[...] = got_ref[...].astype(F32)
    copies = []

    def outgoing(group, _):
        return output_of(wide, out_t, group, lanes, line)

    def finish(group, output):
        at = slice(group * lanes, (group + 1) * lanes)
        field = field_in[:, at] + (gate_in[:, at] * output + output)
        out_ref[at, :] = field.T.astype(BF16)
        at = pl.ds(group * lanes, lanes)
        copies.append(pltpu.make_async_copy(out_ref.at[at], out_hbm.at[at], sems.at[group]))
        copies[-1].start()

    staged(rows // SUB, (outgoing, finish))
    for copy in copies:
        copy.wait()


def moved(source, moves, count):
    shape = None
    lane = None
    targets = [[] for _ in range(count)]
    for row, begin, length, target in moves:
        shift = (target - begin) % LANES
        while length > 0:
            size = min(length, LANES - begin % LANES, LANES - target % LANES)
            targets[target // LANES].append((target % LANES, row, begin // LANES, shift))
            begin, target, length = begin + size, target + size, length - size
    rolled = {}
    registers = []
    for pieces in targets:
        value = None
        for start, row, register, shift in sorted(pieces, key=lambda piece: piece[0]):
            key = (row, register, shift)
            if key not in rolled:
                tile = source(row, register)
                rolled[key] = pltpu.roll(tile, shift, 1) if shift else tile
            if value is None:
                value = rolled[key]
            else:
                if lane is None:
                    shape = value.shape
                    lane = lax.broadcasted_iota(jnp.int32, shape, 1)
                value = jnp.where(lane < start, value, rolled[key])
        registers.append(value)
    return registers


def wide_steps(tiles):
    place_step = tiles + 1 - tiles % 2
    return place_step, SUB * place_step + 1


def stacked(low, high):
    return jnp.concatenate([low, high], axis=0).astype(BF16)


def triangle_kernel(direction, share, rows, cols, row_devices, col_devices, line, got_ref, sent_ref,
                    wide, left_ref, right_ref, even_ref, result_ref, packed):
    groups = rows // SUB
    pieces = SUB * cols // LANES
    total = row_devices * rows
    blocks = -(-total // LANES)
    pairs = -(-groups // 2)
    rest = total - (blocks - 1) * LANES
    tail = lax.broadcasted_iota(jnp.int32, (2 * SUB, LANES), 1) < rest
    place_step, row_step = wide_steps(col_devices * groups * pieces)

    def spot(tile):
        device, number = divmod(tile, groups * pieces)
        col, row = divmod(device, row_devices)
        return row * row_step + col * groups * pieces + number

    def widen(pair):
        for unit in range(got_ref.shape[0] // (2 * SUB)):
            owners = [tile % (groups * pieces) // pieces // 2 for tile in (2 * unit, 2 * unit + 1)]
            if min(owners) != pair:
                continue
            both = got_ref[unit * 2 * SUB : (unit + 1) * 2 * SUB, :].astype(F32)
            for half in range(2):
                at = pl.ds(spot(2 * unit + half), SUB, stride=place_step)
                wide[at, :] = both[half * SUB : (half + 1) * SUB]

    def loaded(place, group, col, piece):
        if group >= groups:
            return jnp.zeros((SUB, LANES), F32)
        start = place * place_step + (col * groups + group) * pieces + piece
        return wide[pl.ds(start, row_devices, stride=row_step), :]

    def unpack(channel, only=range(pairs)):
        spare = channel % 2
        for pair in only:
            for is_right, place in ((False, channel), (True, share + channel)):
                tiles = {}
                for col in range(col_devices):
                    for piece in range(pieces):
                        tiles[col, piece] = stacked(
                            loaded(place, 2 * pair, col, piece), loaded(place, 2 * pair + 1, col, piece)
                        )
                for step in range(SUB):
                    moves = [(col, step * cols, cols, col * cols) for col in range(col_devices)]
                    registers = moved(lambda col, piece: tiles[col, piece], moves, blocks)
                    registers[-1] = jnp.where(tail, registers[-1], jnp.zeros_like(registers[-1]))
                    for block in range(blocks):
                        if is_right and direction == 0:
                            both = registers[block].astype(F32)
                            for half in range(2):
                                group = 2 * pair + half
                                if group < groups:
                                    at = pl.ds(group * SUB + step, row_devices, stride=rows)
                                    even_ref[spare, block, at, :] = both[half * SUB : (half + 1) * SUB]
                        else:
                            target = right_ref if is_right else left_ref
                            start = (pair * SUB + step) * 2 * SUB
                            target[spare, start : start + 2 * SUB, block * LANES : (block + 1) * LANES] = (
                                registers[block]
                            )

    def product(channel):
        spare = channel % 2
        if direction == 0:
            right = [even_ref[spare, block].astype(BF16) for block in range(blocks)]
            right = jnp.concatenate(right, axis=1)
            summed = matmul(left_ref[spare], right, ((1,), (1,)))
            for block in range(blocks):
                size = min(LANES, total - block * LANES)
                part = summed[:, block * LANES : block * LANES + size].astype(BF16)
                result_ref[spare, block, :, 0:size] = part
        else:
            summed = matmul(left_ref[spare], right_ref[spare], ((0,), (0,)))
            for block in range(blocks):
                result_ref[spare, block] = summed[:, block * LANES : (block + 1) * LANES]

    def pack(channel):
        spare = channel % 2

        def result_at(pair, step, block):
            if direction == 0:
                start = (pair * SUB + step) * 2 * SUB
                return result_ref[spare, block, start : start + 2 * SUB, :]
            halves = []
            for group in (2 * pair, 2 * pair + 1):
                if group < groups:
                    at = pl.ds(group * SUB + step, row_devices, stride=rows)
                    halves.append(result_ref[spare, block, at, :])
                else:
                    halves.append(jnp.zeros((SUB, LANES), F32))
            return stacked(*halves)

        for pair in range(pairs):
            tiles = {}
            for step in range(SUB):
                for block in range(blocks):
                    tiles[step, block] = result_at(pair, step, block)
            for col in range(col_devices):
                moves = [(step, col * cols, cols, step * cols) for step in range(SUB)]
                registers = moved(lambda step, block: tiles[step, block], moves, pieces)
                for piece in range(pieces):
                    both = registers[piece].astype(F32)
                    for half in range(2):
                        group = 2 * pair + half
                        if group < groups:
                            start = (col * row_devices * share + channel) * line + group * pieces + piece
                            packed[pl.ds(start, row_devices, stride=share * line), :] = (
                                both[half * SUB : (half + 1) * SUB]
                            )

    widen(0)
    for pair in range(pairs):
        if pair + 1 < pairs:
            widen(pair + 1)
        unpack(0, [pair])
    for channel in range(share):
        product(channel)
        if channel > 0:
            pack(channel - 1)
        if channel + 1 < share:
            unpack(channel + 1)
    pack(share - 1)
    sent_ref[...] = packed[...].astype(BF16)


def by_channels(pair, token_mask, chain_ids, chain_bias, in_weights, out_weights, row_devices, col_devices):
    rows, cols, width = pair.shape
    devices = row_devices * col_devices
    share = width // devices
    lanes = SUB * cols
    pieces = lanes // LANES
    groups = rows // SUB
    chunk = groups * pieces * SUB
    spots = rows * cols
    line = -(-groups * pieces * share // SUB) * SUB // share
    total = row_devices * rows
    blocks = -(-total // LANES)
    tall = -(-groups // 2) * 2 * SUB * row_devices
    params = pltpu.CompilerParams(vmem_limit_bytes=40 * 1024 * 1024)
    whole = pl.BlockSpec(memory_space=pltpu.VMEM)
    far = pl.BlockSpec(memory_space=pltpu.HBM)

    sent_shape = jax.ShapeDtypeStruct((devices, groups, pieces * SUB, LANES), BF16)
    sum_shape = jax.ShapeDtypeStruct((devices * share * line, LANES), BF16)
    state_shape = jax.ShapeDtypeStruct((width, spots), F32)
    mask_shape = jax.ShapeDtypeStruct((1, spots), F32)

    def exchange(array, rows):
        split = array.reshape(devices, rows, LANES)
        return lax.all_to_all(split, ("col", "row"), 0, 0, tiled=True).reshape(devices * rows, LANES)

    def triangle(direction, sent):
        result_rows, result_type = (tall, BF16) if direction == 0 else (blocks * LANES, F32)
        wide_rows = row_devices * wide_steps(col_devices * groups * pieces)[1]
        summed = pl.pallas_call(
            functools.partial(
                triangle_kernel, direction, share, rows, cols, row_devices, col_devices, line
            ),
            out_shape=sum_shape,
            in_specs=[whole],
            out_specs=whole,
            scratch_shapes=[
                pltpu.VMEM((-(-wide_rows // SUB) * SUB, LANES), F32),
                pltpu.VMEM((2, tall, blocks * LANES), BF16),
                pltpu.VMEM((2, tall, blocks * LANES), BF16),
                pltpu.VMEM((2, blocks, total, LANES), F32),
                pltpu.VMEM((2, blocks, result_rows, LANES), result_type),
                pltpu.VMEM(sum_shape.shape, F32),
            ],
            compiler_params=params,
            name="triangle",
        )(exchange(sent, chunk))
        return exchange(summed, share * line)

    flat_pair = pair.reshape(spots, width)
    sent, gate, field, mask = pl.pallas_call(
        functools.partial(start_kernel, share, rows, cols),
        out_shape=[sent_shape, state_shape, state_shape, mask_shape],
        in_specs=[far] * 5,
        out_specs=[far] * 4,
        scratch_shapes=[
            pltpu.VMEM(sent_shape.shape, BF16),
            pltpu.VMEM(state_shape.shape, F32),
            pltpu.VMEM(state_shape.shape, F32),
            pltpu.VMEM(mask_shape.shape, F32),
            pltpu.VMEM((spots, width), BF16),
            pltpu.VMEM(in_weights.shape[1:], BF16),
            pltpu.VMEM((1, width), F32),
            pltpu.VMEM((1,) + token_mask.shape, jnp.int32),
            pltpu.VMEM((1,) + chain_ids.shape, jnp.int32),
            pltpu.SemaphoreType.DMA((9 + groups,)),
        ],
        compiler_params=pltpu.CompilerParams(vmem_limit_bytes=60 * 1024 * 1024),
        name="start",
    )(token_mask, chain_ids, flat_pair, chain_bias, in_weights)
    got = triangle(0, sent)
    sent, gate, field = pl.pallas_call(
        functools.partial(middle_kernel, share, rows, cols, line),
        out_shape=[sent_shape, state_shape, state_shape],
        in_specs=[whole] * 6,
        out_specs=[whole] * 3,
        scratch_shapes=[pltpu.VMEM(sum_shape.shape, F32)],
        compiler_params=params,
        name="middle",
    )(mask, got, field, gate, out_weights, in_weights)
    got = triangle(1, sent)
    out = pl.pallas_call(
        functools.partial(end_kernel, rows, cols, line),
        out_shape=jax.ShapeDtypeStruct((spots, width), BF16),
        in_specs=[whole] * 4,
        out_specs=far,
        scratch_shapes=[
            pltpu.VMEM(sum_shape.shape, F32),
            pltpu.VMEM((spots, width), BF16),
            pltpu.SemaphoreType.DMA((groups,)),
        ],
        compiler_params=params,
        name="end",
    )(got, field, gate, out_weights)
    return out.reshape(pair.shape)


def gated_inputs(field, weights, pair_mask):
    width = weights.shape[0]
    normed = layer_norm(field).astype(BF16)
    projected = jnp.einsum("ijc,cd->ijd", normed, weights, preferred_element_type=F32)
    first = (
        jax.nn.sigmoid(projected[..., :width])
        * projected[..., width : 2 * width]
        * pair_mask[:, :, None]
    ).astype(BF16)
    second = (
        jax.nn.sigmoid(projected[..., 2 * width : 3 * width])
        * projected[..., 3 * width : 4 * width]
        * pair_mask[:, :, None]
    ).astype(BF16)
    gate_value = jax.nn.sigmoid(projected[..., 4 * width :])
    return (first, second, gate_value)


def update(field, summed, gate_value, weights):
    normed_sum = layer_norm(summed).astype(BF16)
    output = jnp.einsum("ijc,cd->ijd", normed_sum, weights, preferred_element_type=F32)
    return field + gate_value * output


def by_blocks(pair, token_mask, chain_ids, chain_bias, in_weights, out_weights):
    row_count = pair.shape[0]
    col_count = pair.shape[1]
    row_start = lax.axis_index("row") * row_count
    col_start = lax.axis_index("col") * col_count
    valid_rows = lax.dynamic_slice_in_dim(token_mask, row_start, row_count).astype(F32)
    valid_cols = lax.dynamic_slice_in_dim(token_mask, col_start, col_count).astype(F32)
    chain_rows = lax.dynamic_slice_in_dim(chain_ids, row_start, row_count)
    chain_cols = lax.dynamic_slice_in_dim(chain_ids, col_start, col_count)
    pair_mask = valid_rows[:, None] * valid_cols[None, :]
    same_chain = (chain_rows[:, None] == chain_cols[None, :]).astype(F32)
    field = pair.astype(F32) + same_chain[:, :, None] * chain_bias
    first, second, gate_value = gated_inputs(field, in_weights[0], pair_mask)
    second_rows = lax.all_gather(second, "row", axis=0, tiled=True)
    part = jnp.einsum("jkc,ikc->jic", second_rows, first, preferred_element_type=F32).astype(BF16)
    summed = lax.psum_scatter(part, "col", scatter_dimension=0, tiled=True).astype(F32)
    summed = jnp.transpose(summed, (1, 0, 2))
    field = update(field, summed, gate_value, out_weights[0])
    first, second, gate_value = gated_inputs(field, in_weights[1], pair_mask)
    first_cols = lax.all_gather(first, "col", axis=1, tiled=True)
    part = jnp.einsum("kic,kjc->ijc", first_cols, second, preferred_element_type=F32).astype(BF16)
    summed = lax.psum_scatter(part, "row", scatter_dimension=0, tiled=True).astype(F32)
    field = update(field, summed, gate_value, out_weights[1])
    return field.astype(BF16)


def solution(mesh):
    row_devices, col_devices = mesh.shape["row"], mesh.shape["col"]

    def per_device(pair, *rest):
        rows, cols, width = pair.shape
        devices = row_devices * col_devices
        fits = (
            width % devices == 0
            and 2 * (width // devices) == SUB
            and row_devices == SUB
            and rows % SUB == 0
            and (SUB * cols) % LANES == 0
            and max(rows, cols) <= LANES
        )
        if fits:
            return by_channels(pair, *rest, row_devices, col_devices)
        return by_blocks(pair, *rest)

    return jax.shard_map(
        per_device,
        mesh=mesh,
        in_specs=(P("row", "col", None), P(), P(), P(), P(), P()),
        out_specs=P("row", "col", None),
        check_vma=False,
    )
```

```python
import functools

import jax
import jax.numpy as jnp
from jax import lax
from jax.experimental import pallas as pl
from jax.experimental.pallas import tpu as pltpu
from jax.sharding import PartitionSpec as P

LANES = 128
SUB = 8
F32 = jnp.float32
BF16 = jnp.bfloat16


def layer_norm(values, axis=-1):
    center = values - jnp.mean(values, axis=axis, keepdims=True)
    spread = jnp.mean(center * center, axis=axis, keepdims=True)
    return center * lax.rsqrt(spread + 1e-05)


def matmul(left, right, dims):
    return lax.dot_general(left, right, (dims, ((), ())), preferred_element_type=F32)


def identity(size, scale):
    row = lax.broadcasted_iota(jnp.int32, (size, size), 0)
    col = lax.broadcasted_iota(jnp.int32, (size, size), 1)
    return jnp.where(row == col, scale, 0.0).astype(BF16)


def column(row_ref):
    width = row_ref.shape[1]
    return jnp.broadcast_to(row_ref[...], (width, width)).T[:, 0:1]


def transposed(weights, scale):
    eye = identity(weights.shape[1], scale)
    return matmul(eye, weights, ((1,), (1,))).astype(BF16)


def interleaved(first, second, share):
    width = first.shape[1]
    both = jnp.concatenate([first, second], axis=1)
    row = lax.broadcasted_iota(jnp.int32, (2 * width, 1), 0)
    col = lax.broadcasted_iota(jnp.int32, (2 * width, 2 * width), 1)
    owner, place = row // (2 * share), row % (2 * share)
    source = owner * share + place % share + jnp.where(place >= share, width, 0)
    pick = jnp.where(col == source, 0.5, 0.0).astype(BF16)
    return matmul(pick, both, ((1,), (1,))).astype(BF16)


def load_in_weights(weights, share):
    width = weights.shape[0]
    blocks = [weights[:, k * width : (k + 1) * width] for k in range(5)]
    return (
        interleaved(blocks[0], blocks[2], share),
        interleaved(blocks[1], blocks[3], share),
        transposed(blocks[4], 0.5),
    )


def token_vectors(tokens, row_start, col_start, rows, cols):
    groups = rows // SUB
    wide = tokens.shape[1]
    many = jnp.broadcast_to(tokens.astype(F32), (SUB, wide))
    lane = lax.broadcasted_iota(jnp.int32, (1, SUB * cols), 1)
    at_row = jnp.zeros_like(lane)
    for step in range(1, SUB):
        at_row = at_row + jnp.where(lane >= step * cols, 1, 0)
    at_col = lane - at_row * cols
    key = lax.broadcasted_iota(jnp.int32, (LANES, SUB * cols), 0)
    pick_row = jnp.where(key == at_row, 1.0, 0.0).astype(BF16)
    pick_col = jnp.where(key == at_col, 1.0, 0.0).astype(BF16)

    def window(start):
        return pltpu.roll(many, wide - start, 1)[:, :LANES]

    by_col = matmul(window(col_start).astype(BF16), pick_col, ((1,), (0,)))[0:1]
    windows = [window(row_start + group * SUB)[0:1] for group in range(groups)]
    windows.append(jnp.zeros((-groups % SUB, LANES), F32))
    by_row = matmul(jnp.concatenate(windows, axis=0).astype(BF16), pick_row, ((1,), (0,)))
    by_row = by_row.astype(jnp.int32)
    by_col = by_col.astype(jnp.int32)
    masks = (by_row & by_col & 1).astype(F32)
    sames = jnp.where((by_row >> 1) == (by_col >> 1), 1.0, 0.0)
    return masks, sames


def staged(count, stages):
    held = {}
    for step in range(count + len(stages) - 1):
        for number, stage in enumerate(stages):
            item = step - number
            if 0 <= item < count:
                held[item] = stage(item, held.get(item))


def projected(field, in_t):
    normed = layer_norm(field, 0).astype(BF16)
    return [matmul(weights, normed, ((1,), (0,))) for weights in in_t]


def gated(products, mask, group, share, sent_ref, gate_ref):
    gates, values, gate = products
    width, lanes = gate.shape
    sent = (jnp.tanh(gates) * values + values) * mask
    for owner in range(width // share):
        block = sent[owner * 2 * share : (owner + 1) * 2 * share]
        lines = [block[:, at : at + LANES] for at in range(0, lanes, LANES)]
        sent_ref[owner, group] = jnp.concatenate(lines, axis=0).astype(BF16)
    gate_ref[:, group * lanes : (group + 1) * lanes] = jnp.tanh(gate)


def start_kernel(share, rows, cols, valid_hbm, chain_hbm, pair_hbm, bias_hbm, w_hbm,
                 sent_hbm, gate_hbm, field_hbm, mask_hbm, sent_ref, gate_ref, field_ref, mask_ref,
                 pair_ref, w_ref, bias_ref, valid_ref, chain_ref, sems):
    lanes = SUB * cols
    groups = rows // SUB
    width = pair_ref.shape[1]
    count = valid_hbm.shape[0]
    started = []

    def copy(near, far):
        started.append(pltpu.make_async_copy(near, far, sems.at[len(started)]))
        started[-1].start()

    copy(valid_hbm, valid_ref.at[0])
    copy(chain_hbm, chain_ref.at[0])
    copy(w_hbm.at[0], w_ref)
    copy(bias_hbm, bias_ref.at[0])
    copy(pair_hbm, pair_ref)
    arriving = len(started)
    eye = identity(width, 1.0)
    row_start = lax.axis_index("row") * rows
    col_start = lax.axis_index("col") * cols
    for number in range(arriving):
        started[number].wait()

    def lift(group):
        rows_of = pair_ref[group * lanes : (group + 1) * lanes, :]
        return matmul(eye, rows_of, ((1,), (1,)))

    lifted = {0: lift(0)}
    tokens = chain_ref[...] * 2 + valid_ref[...]
    tokens = jnp.concatenate([tokens, jnp.zeros((1, -count % LANES), jnp.int32)], axis=1)
    masks, sames = token_vectors(tokens, row_start, col_start, rows, cols)
    in_t = load_in_weights(w_ref[...], share)
    bias_col = column(bias_ref)
    early = groups // 2 * lanes

    def make_field(group, _):
        at = slice(group * lanes, (group + 1) * lanes)
        if group + 1 < groups:
            lifted[group + 1] = lift(group + 1)
        field = lifted.pop(group) + bias_col * sames[group : group + 1]
        field_ref[:, at] = field
        mask_ref[:, at] = masks[group : group + 1]
        return field

    def project(group, field):
        if group == groups - 1:
            copy(field_ref, field_hbm)
            copy(mask_ref, mask_hbm)
        return projected(field, in_t)

    def finish(group, products):
        gated(products, masks[group : group + 1], group, share, sent_ref, gate_ref)
        copy(sent_ref.at[:, group], sent_hbm.at[:, group])
        if (group + 1) * lanes == early:
            copy(gate_ref.at[:, 0:early], gate_hbm.at[:, 0:early])

    staged(groups, (make_field, project, finish))
    late = pl.ds(early, groups * lanes - early)
    copy(gate_ref.at[:, late], gate_hbm.at[:, late])
    for number in range(arriving, len(started)):
        started[number].wait()


def output_of(wide, out_t, group, lanes, line):
    width = out_t.shape[1]
    pieces = lanes // LANES
    parts = []
    for piece in range(pieces):
        parts.append(wide[pl.ds(group * pieces + piece, width, stride=line), :])
    normed = layer_norm(jnp.concatenate(parts, axis=1), 0).astype(BF16)
    return matmul(out_t, normed, ((1,), (0,)))


def middle_kernel(share, rows, cols, line, mask_ref, got_ref, field_in, gate_in, wo_ref, w_ref,
                  sent_ref, gate_ref, field_ref, wide):
    lanes = SUB * cols
    in_t = load_in_weights(w_ref[1], share)
    out_t = transposed(wo_ref[0], 0.5)
    wide[...] = got_ref[...].astype(F32)

    def span(group):
        return slice(group * lanes, (group + 1) * lanes)

    def outgoing(group, _):
        return output_of(wide, out_t, group, lanes, line)

    def project(group, output):
        at = span(group)
        field = field_in[:, at] + (gate_in[:, at] * output + output)
        field_ref[:, at] = field
        return projected(field, in_t)

    def finish(group, products):
        gated(products, mask_ref[:, span(group)], group, share, sent_ref, gate_ref)

    staged(rows // SUB, (outgoing, project, finish))


def end_kernel(rows, cols, line, got_ref, field_in, gate_in, wo_ref, out_hbm, wide, out_ref, sems):
    lanes = SUB * cols
    out_t = transposed(wo_ref[1], 0.5)
    wide[...] = got_ref[...].astype(F32)
    copies = []

    def outgoing(group, _):
        return output_of(wide, out_t, group, lanes, line)

    def finish(group, output):
        at = slice(group * lanes, (group + 1) * lanes)
        field = field_in[:, at] + (gate_in[:, at] * output + output)
        out_ref[at, :] = field.astype(BF16).T
        at = pl.ds(group * lanes, lanes)
        copies.append(pltpu.make_async_copy(out_ref.at[at], out_hbm.at[at], sems.at[group]))
        copies[-1].start()

    staged(rows // SUB, (outgoing, finish))
    for copy in copies:
        copy.wait()


def moved(source, moves, count):
    shape = None
    lane = None
    targets = [[] for _ in range(count)]
    for row, begin, length, target in moves:
        shift = (target - begin) % LANES
        while length > 0:
            size = min(length, LANES - begin % LANES, LANES - target % LANES)
            targets[target // LANES].append((target % LANES, row, begin // LANES, shift))
            begin, target, length = begin + size, target + size, length - size
    rolled = {}
    registers = []
    for pieces in targets:
        value = None
        for start, row, register, shift in sorted(pieces, key=lambda piece: piece[0]):
            key = (row, register, shift)
            if key not in rolled:
                tile = source(row, register)
                rolled[key] = pltpu.roll(tile, shift, 1) if shift else tile
            if value is None:
                value = rolled[key]
            else:
                if lane is None:
                    shape = value.shape
                    lane = lax.broadcasted_iota(jnp.int32, shape, 1)
                value = jnp.where(lane < start, value, rolled[key])
        registers.append(value)
    return registers


def wide_steps(tiles):
    place_step = tiles + 1 - tiles % 2
    return place_step, SUB * place_step + 1


def stacked(low, high):
    return jnp.concatenate([low, high], axis=0).astype(BF16)


def triangle_kernel(direction, share, rows, cols, row_devices, col_devices, line, got_ref, sent_ref,
                    wide, left_ref, right_ref, even_ref, result_ref, packed):
    groups = rows // SUB
    pieces = SUB * cols // LANES
    total = row_devices * rows
    blocks = -(-total // LANES)
    pairs = -(-groups // 2)
    rest = total - (blocks - 1) * LANES
    tail = lax.broadcasted_iota(jnp.int32, (2 * SUB, LANES), 1) < rest
    place_step, row_step = wide_steps(col_devices * groups * pieces)

    def spot(tile):
        device, number = divmod(tile, groups * pieces)
        col, row = divmod(device, row_devices)
        return row * row_step + col * groups * pieces + number

    def widen(pair):
        for unit in range(got_ref.shape[0] // (2 * SUB)):
            owners = [tile % (groups * pieces) // pieces // 2 for tile in (2 * unit, 2 * unit + 1)]
            if min(owners) != pair:
                continue
            both = got_ref[unit * 2 * SUB : (unit + 1) * 2 * SUB, :].astype(F32)
            for half in range(2):
                at = pl.ds(spot(2 * unit + half), SUB, stride=place_step)
                wide[at, :] = both[half * SUB : (half + 1) * SUB]

    def loaded(place, group, col, piece):
        start = place * place_step + (col * groups + group) * pieces + piece
        return wide[pl.ds(start, row_devices, stride=row_step), :]

    def spread(tiles, step):
        moves = [(col, step * cols, cols, col * cols) for col in range(col_devices)]
        registers = moved(lambda col, piece: tiles[col, piece], moves, blocks)
        registers[-1] = jnp.where(tail, registers[-1], jnp.zeros_like(registers[-1]))
        return registers

    def put(target, spare, start, block, value):
        target[spare, start : start + 2 * SUB, block * LANES : (block + 1) * LANES] = value

    def put_even(spare, group, step, block, value):
        even_ref[spare, block, pl.ds(group * SUB + step, row_devices, stride=rows), :] = value

    def unpack(channel, only=range(pairs)):
        spare = channel % 2
        for pair in only:
            if 2 * pair + 1 < groups:
                unpack_pair(channel, spare, pair)
            else:
                unpack_last(channel, spare, 2 * pair)

    def unpack_pair(channel, spare, pair):
        for is_right, place in ((False, channel), (True, share + channel)):
            tiles = {}
            for col in range(col_devices):
                for piece in range(pieces):
                    tiles[col, piece] = stacked(
                        loaded(place, 2 * pair, col, piece), loaded(place, 2 * pair + 1, col, piece)
                    )
            for step in range(SUB):
                for block, register in enumerate(spread(tiles, step)):
                    if is_right and direction == 0:
                        both = register.astype(F32)
                        for half in range(2):
                            put_even(spare, 2 * pair + half, step, block, both[half * SUB : (half + 1) * SUB])
                    else:
                        target = right_ref if is_right else left_ref
                        put(target, spare, (pair * SUB + step) * 2 * SUB, block, register)

    def unpack_last(channel, spare, group):
        tiles = {}
        for col in range(col_devices):
            for piece in range(pieces):
                tiles[col, piece] = stacked(
                    loaded(channel, group, col, piece), loaded(share + channel, group, col, piece)
                )
        before = None
        for step in range(SUB):
            now = [register.astype(F32) for register in spread(tiles, step)]
            for block in range(blocks):
                if direction == 0:
                    put_even(spare, group, step, block, now[block][SUB:])
                if step % 2:
                    start = (group * SUB + step - 1) * SUB
                    put(left_ref, spare, start, block, stacked(before[block][:SUB], now[block][:SUB]))
                    if direction == 1:
                        put(right_ref, spare, start, block, stacked(before[block][SUB:], now[block][SUB:]))
            before = now

    def product(channel):
        spare = channel % 2
        if direction == 0:
            right = [even_ref[spare, block].astype(BF16) for block in range(blocks)]
            right = jnp.concatenate(right, axis=1)
            summed = matmul(left_ref[spare], right, ((1,), (1,)))
            for block in range(blocks):
                size = min(LANES, total - block * LANES)
                part = summed[:, block * LANES : block * LANES + size].astype(BF16)
                result_ref[spare, block, :, 0:size] = part
        else:
            summed = matmul(left_ref[spare], right_ref[spare], ((0,), (0,)))
            for block in range(blocks):
                result_ref[spare, block] = summed[:, block * LANES : (block + 1) * LANES]

    def pack(channel):
        spare = channel % 2

        def result_at(pair, step, block):
            halves = []
            for group in (2 * pair, 2 * pair + 1):
                if group >= groups:
                    halves.append(jnp.zeros((SUB, LANES), F32))
                elif direction == 1:
                    at = pl.ds(group * SUB + step, row_devices, stride=rows)
                    halves.append(result_ref[spare, block, at, :])
                elif 2 * pair + 1 < groups:
                    start = (pair * SUB + step) * 2 * SUB
                    return result_ref[spare, block, start : start + 2 * SUB, :]
                else:
                    start = (group * SUB + step // 2 * 2) * SUB
                    both = result_ref[spare, block, start : start + 2 * SUB, :].astype(F32)
                    halves.append(both[step % 2 * SUB : (step % 2 + 1) * SUB])
            return stacked(*halves)

        for pair in range(pairs):
            tiles = {}
            for step in range(SUB):
                for block in range(blocks):
                    tiles[step, block] = result_at(pair, step, block)
            for col in range(col_devices):
                moves = [(step, col * cols, cols, step * cols) for step in range(SUB)]
                registers = moved(lambda step, block: tiles[step, block], moves, pieces)
                for piece in range(pieces):
                    both = registers[piece].astype(F32)
                    for half in range(2):
                        group = 2 * pair + half
                        if group < groups:
                            start = (col * row_devices * share + channel) * line + group * pieces + piece
                            packed[pl.ds(start, row_devices, stride=share * line), :] = (
                                both[half * SUB : (half + 1) * SUB]
                            )

    widen(0)
    for pair in range(pairs):
        if pair + 1 < pairs:
            widen(pair + 1)
        unpack(0, [pair])
    for channel in range(share):
        product(channel)
        if channel > 0:
            pack(channel - 1)
        if channel + 1 < share:
            unpack(channel + 1)
    pack(share - 1)
    sent_ref[...] = packed[...].astype(BF16)


def by_channels(pair, token_mask, chain_ids, chain_bias, in_weights, out_weights, row_devices, col_devices):
    rows, cols, width = pair.shape
    devices = row_devices * col_devices
    share = width // devices
    lanes = SUB * cols
    pieces = lanes // LANES
    groups = rows // SUB
    chunk = groups * pieces * SUB
    spots = rows * cols
    line = -(-groups * pieces * share // SUB) * SUB // share
    total = row_devices * rows
    blocks = -(-total // LANES)
    tall = groups * SUB * row_devices
    params = pltpu.CompilerParams(vmem_limit_bytes=40 * 1024 * 1024)
    whole = pl.BlockSpec(memory_space=pltpu.VMEM)
    far = pl.BlockSpec(memory_space=pltpu.HBM)

    sent_shape = jax.ShapeDtypeStruct((devices, groups, pieces * SUB, LANES), BF16)
    sum_shape = jax.ShapeDtypeStruct((devices * share * line, LANES), BF16)
    state_shape = jax.ShapeDtypeStruct((width, spots), F32)
    mask_shape = jax.ShapeDtypeStruct((1, spots), F32)

    def exchange(array, rows):
        split = array.reshape(devices, rows, LANES)
        return lax.all_to_all(split, ("col", "row"), 0, 0, tiled=True).reshape(devices * rows, LANES)

    def triangle(direction, sent):
        result_rows, result_type = (tall, BF16) if direction == 0 else (blocks * LANES, F32)
        wide_rows = row_devices * wide_steps(col_devices * groups * pieces)[1]
        summed = pl.pallas_call(
            functools.partial(
                triangle_kernel, direction, share, rows, cols, row_devices, col_devices, line
            ),
            out_shape=sum_shape,
            in_specs=[whole],
            out_specs=whole,
            scratch_shapes=[
                pltpu.VMEM((-(-wide_rows // SUB) * SUB, LANES), F32),
                pltpu.VMEM((2, tall, blocks * LANES), BF16),
                pltpu.VMEM((2, tall, blocks * LANES), BF16),
                pltpu.VMEM((2, blocks, total, LANES), F32),
                pltpu.VMEM((2, blocks, result_rows, LANES), result_type),
                pltpu.VMEM(sum_shape.shape, F32),
            ],
            compiler_params=params,
            name="triangle",
        )(exchange(sent, chunk))
        return exchange(summed, share * line)

    flat_pair = pair.reshape(spots, width)
    sent, gate, field, mask = pl.pallas_call(
        functools.partial(start_kernel, share, rows, cols),
        out_shape=[sent_shape, state_shape, state_shape, mask_shape],
        in_specs=[far] * 5,
        out_specs=[far] * 4,
        scratch_shapes=[
            pltpu.VMEM(sent_shape.shape, BF16),
            pltpu.VMEM(state_shape.shape, F32),
            pltpu.VMEM(state_shape.shape, F32),
            pltpu.VMEM(mask_shape.shape, F32),
            pltpu.VMEM((spots, width), BF16),
            pltpu.VMEM(in_weights.shape[1:], BF16),
            pltpu.VMEM((1, width), F32),
            pltpu.VMEM((1,) + token_mask.shape, jnp.int32),
            pltpu.VMEM((1,) + chain_ids.shape, jnp.int32),
            pltpu.SemaphoreType.DMA((9 + groups,)),
        ],
        compiler_params=pltpu.CompilerParams(vmem_limit_bytes=60 * 1024 * 1024),
        name="start",
    )(token_mask, chain_ids, flat_pair, chain_bias, in_weights)
    got = triangle(0, sent)
    sent, gate, field = pl.pallas_call(
        functools.partial(middle_kernel, share, rows, cols, line),
        out_shape=[sent_shape, state_shape, state_shape],
        in_specs=[whole] * 6,
        out_specs=[whole] * 3,
        scratch_shapes=[pltpu.VMEM(sum_shape.shape, F32)],
        compiler_params=params,
        name="middle",
    )(mask, got, field, gate, out_weights, in_weights)
    got = triangle(1, sent)
    out = pl.pallas_call(
        functools.partial(end_kernel, rows, cols, line),
        out_shape=jax.ShapeDtypeStruct((spots, width), BF16),
        in_specs=[whole] * 4,
        out_specs=far,
        scratch_shapes=[
            pltpu.VMEM(sum_shape.shape, F32),
            pltpu.VMEM((spots, width), BF16),
            pltpu.SemaphoreType.DMA((groups,)),
        ],
        compiler_params=params,
        name="end",
    )(got, field, gate, out_weights)
    return out.reshape(pair.shape)


def gated_inputs(field, weights, pair_mask):
    width = weights.shape[0]
    normed = layer_norm(field).astype(BF16)
    projected = jnp.einsum("ijc,cd->ijd", normed, weights, preferred_element_type=F32)
    first = (
        jax.nn.sigmoid(projected[..., :width])
        * projected[..., width : 2 * width]
        * pair_mask[:, :, None]
    ).astype(BF16)
    second = (
        jax.nn.sigmoid(projected[..., 2 * width : 3 * width])
        * projected[..., 3 * width : 4 * width]
        * pair_mask[:, :, None]
    ).astype(BF16)
    gate_value = jax.nn.sigmoid(projected[..., 4 * width :])
    return (first, second, gate_value)


def update(field, summed, gate_value, weights):
    normed_sum = layer_norm(summed).astype(BF16)
    output = jnp.einsum("ijc,cd->ijd", normed_sum, weights, preferred_element_type=F32)
    return field + gate_value * output


def by_blocks(pair, token_mask, chain_ids, chain_bias, in_weights, out_weights):
    row_count = pair.shape[0]
    col_count = pair.shape[1]
    row_start = lax.axis_index("row") * row_count
    col_start = lax.axis_index("col") * col_count
    valid_rows = lax.dynamic_slice_in_dim(token_mask, row_start, row_count).astype(F32)
    valid_cols = lax.dynamic_slice_in_dim(token_mask, col_start, col_count).astype(F32)
    chain_rows = lax.dynamic_slice_in_dim(chain_ids, row_start, row_count)
    chain_cols = lax.dynamic_slice_in_dim(chain_ids, col_start, col_count)
    pair_mask = valid_rows[:, None] * valid_cols[None, :]
    same_chain = (chain_rows[:, None] == chain_cols[None, :]).astype(F32)
    field = pair.astype(F32) + same_chain[:, :, None] * chain_bias
    first, second, gate_value = gated_inputs(field, in_weights[0], pair_mask)
    second_rows = lax.all_gather(second, "row", axis=0, tiled=True)
    part = jnp.einsum("jkc,ikc->jic", second_rows, first, preferred_element_type=F32).astype(BF16)
    summed = lax.psum_scatter(part, "col", scatter_dimension=0, tiled=True).astype(F32)
    summed = jnp.transpose(summed, (1, 0, 2))
    field = update(field, summed, gate_value, out_weights[0])
    first, second, gate_value = gated_inputs(field, in_weights[1], pair_mask)
    first_cols = lax.all_gather(first, "col", axis=1, tiled=True)
    part = jnp.einsum("kic,kjc->ijc", first_cols, second, preferred_element_type=F32).astype(BF16)
    summed = lax.psum_scatter(part, "row", scatter_dimension=0, tiled=True).astype(F32)
    field = update(field, summed, gate_value, out_weights[1])
    return field.astype(BF16)


def solution(mesh):
    row_devices, col_devices = mesh.shape["row"], mesh.shape["col"]

    def per_device(pair, *rest):
        rows, cols, width = pair.shape
        devices = row_devices * col_devices
        fits = (
            width % devices == 0
            and 2 * (width // devices) == SUB
            and row_devices == SUB
            and rows % SUB == 0
            and (SUB * cols) % LANES == 0
            and max(rows, cols) <= LANES
        )
        if fits:
            return by_channels(pair, *rest, row_devices, col_devices)
        return by_blocks(pair, *rest)

    return jax.shard_map(
        per_device,
        mesh=mesh,
        in_specs=(P("row", "col", None), P(), P(), P(), P(), P()),
        out_specs=P("row", "col", None),
        check_vma=False,
    )
```

```python
import functools

import jax
import jax.numpy as jnp
from jax import lax
from jax.experimental import pallas as pl
from jax.experimental.pallas import tpu as pltpu
from jax.sharding import PartitionSpec as P

LANES = 128
SUB = 8
F32 = jnp.float32
BF16 = jnp.bfloat16


def layer_norm(values, axis=-1):
    center = values - jnp.mean(values, axis=axis, keepdims=True)
    spread = jnp.mean(center * center, axis=axis, keepdims=True)
    return center * lax.rsqrt(spread + 1e-05)


def matmul(left, right, dims):
    return lax.dot_general(left, right, (dims, ((), ())), preferred_element_type=F32)


def identity(size, scale):
    row = lax.broadcasted_iota(jnp.int32, (size, size), 0)
    col = lax.broadcasted_iota(jnp.int32, (size, size), 1)
    return jnp.where(row == col, scale, 0.0).astype(BF16)


def column(row_ref):
    width = row_ref.shape[1]
    return jnp.broadcast_to(row_ref[...], (width, width)).T[:, 0:1]


def transposed(weights, scale):
    eye = identity(weights.shape[1], scale)
    return matmul(eye, weights, ((1,), (1,))).astype(BF16)


def interleaved(first, second, share):
    width = first.shape[1]
    both = jnp.concatenate([first, second], axis=1)
    row = lax.broadcasted_iota(jnp.int32, (2 * width, 1), 0)
    col = lax.broadcasted_iota(jnp.int32, (2 * width, 2 * width), 1)
    owner, place = row // (2 * share), row % (2 * share)
    source = owner * share + place % share + jnp.where(place >= share, width, 0)
    pick = jnp.where(col == source, 0.5, 0.0).astype(BF16)
    return matmul(pick, both, ((1,), (1,))).astype(BF16)


def load_in_weights(weights, share):
    width = weights.shape[0]
    blocks = [weights[:, k * width : (k + 1) * width] for k in range(5)]
    return (
        interleaved(blocks[0], blocks[2], share),
        interleaved(blocks[1], blocks[3], share),
        transposed(blocks[4], 0.5),
    )


def token_vectors(tokens, row_start, col_start, rows, cols):
    groups = rows // SUB
    wide = tokens.shape[1]
    many = jnp.broadcast_to(tokens.astype(F32), (SUB, wide))
    lane = lax.broadcasted_iota(jnp.int32, (1, SUB * cols), 1)
    at_row = jnp.zeros_like(lane)
    for step in range(1, SUB):
        at_row = at_row + jnp.where(lane >= step * cols, 1, 0)
    at_col = lane - at_row * cols
    key = lax.broadcasted_iota(jnp.int32, (LANES, SUB * cols), 0)
    pick_row = jnp.where(key == at_row, 1.0, 0.0).astype(BF16)
    pick_col = jnp.where(key == at_col, 1.0, 0.0).astype(BF16)

    def window(start):
        return pltpu.roll(many, wide - start, 1)[:, :LANES]

    by_col = matmul(window(col_start).astype(BF16), pick_col, ((1,), (0,)))[0:1]
    windows = [window(row_start + group * SUB)[0:1] for group in range(groups)]
    windows.append(jnp.zeros((-groups % SUB, LANES), F32))
    by_row = matmul(jnp.concatenate(windows, axis=0).astype(BF16), pick_row, ((1,), (0,)))
    by_row = by_row.astype(jnp.int32)
    by_col = by_col.astype(jnp.int32)
    masks = (by_row & by_col & 1).astype(F32)
    sames = jnp.where((by_row >> 1) == (by_col >> 1), 1.0, 0.0)
    return masks, sames


def staged(count, stages):
    held = {}
    for step in range(count + len(stages) - 1):
        for number, stage in enumerate(stages):
            item = step - number
            if 0 <= item < count:
                held[item] = stage(item, held.get(item))


def projected(field, in_t):
    normed = layer_norm(field, 0).astype(BF16)
    return [matmul(weights, normed, ((1,), (0,))) for weights in in_t]


def gated(products, mask, group, share, sent_ref, gate_ref):
    gates, values, gate = products
    width, lanes = gate.shape
    sent = (jnp.tanh(gates) * values + values) * mask
    for owner in range(width // share):
        block = sent[owner * 2 * share : (owner + 1) * 2 * share]
        lines = [block[:, at : at + LANES] for at in range(0, lanes, LANES)]
        sent_ref[owner, group] = jnp.concatenate(lines, axis=0).astype(BF16)
    gate_ref[:, group * lanes : (group + 1) * lanes] = jnp.tanh(gate)


def start_kernel(share, rows, cols, valid_hbm, chain_hbm, pair_hbm, bias_hbm, w_hbm,
                 sent_hbm, gate_hbm, field_hbm, mask_hbm, sent_ref, gate_ref, field_ref, mask_ref,
                 pair_ref, w_ref, bias_ref, valid_ref, chain_ref, sems):
    lanes = SUB * cols
    groups = rows // SUB
    width = pair_ref.shape[1]
    count = valid_hbm.shape[0]
    started = []

    def copy(near, far):
        started.append(pltpu.make_async_copy(near, far, sems.at[len(started)]))
        started[-1].start()

    copy(w_hbm.at[0], w_ref)
    copy(valid_hbm, valid_ref.at[0])
    copy(chain_hbm, chain_ref.at[0])
    copy(bias_hbm, bias_ref.at[0])
    copy(pair_hbm, pair_ref)
    arriving = len(started)
    eye = identity(width, 1.0)
    row_start = lax.axis_index("row") * rows
    col_start = lax.axis_index("col") * cols
    started[0].wait()
    in_t = load_in_weights(w_ref[...], share)
    for number in range(1, arriving):
        started[number].wait()

    def lift(group):
        rows_of = pair_ref[group * lanes : (group + 1) * lanes, :]
        return matmul(eye, rows_of, ((1,), (1,)))

    lifted = {0: lift(0)}
    tokens = chain_ref[...] * 2 + valid_ref[...]
    tokens = jnp.concatenate([tokens, jnp.zeros((1, -count % LANES), jnp.int32)], axis=1)
    masks, sames = token_vectors(tokens, row_start, col_start, rows, cols)
    bias_col = column(bias_ref)

    def make_field(group, _):
        at = slice(group * lanes, (group + 1) * lanes)
        if group + 1 < groups:
            lifted[group + 1] = lift(group + 1)
        field = lifted.pop(group) + bias_col * sames[group : group + 1]
        field_ref[:, at] = field
        mask_ref[:, at] = masks[group : group + 1]
        return field

    def project(group, field):
        if group == groups - 1:
            copy(field_ref, field_hbm)
            copy(mask_ref, mask_hbm)
        return projected(field, in_t)

    def finish(group, products):
        gated(products, masks[group : group + 1], group, share, sent_ref, gate_ref)
        copy(sent_ref.at[:, group], sent_hbm.at[:, group])
        at = pl.ds(group * lanes, lanes)
        copy(gate_ref.at[:, at], gate_hbm.at[:, at])

    staged(groups, (make_field, project, finish))
    for number in range(arriving, len(started)):
        started[number].wait()


def output_of(wide, out_t, group, lanes, line):
    width = out_t.shape[1]
    pieces = lanes // LANES
    parts = []
    for piece in range(pieces):
        parts.append(wide[pl.ds(group * pieces + piece, width, stride=line), :])
    normed = layer_norm(jnp.concatenate(parts, axis=1), 0).astype(BF16)
    return matmul(out_t, normed, ((1,), (0,)))


def middle_kernel(share, rows, cols, line, mask_ref, got_ref, field_in, gate_in, wo_ref, w_ref,
                  sent_ref, gate_ref, field_ref, wide):
    lanes = SUB * cols
    in_t = load_in_weights(w_ref[1], share)
    out_t = transposed(wo_ref[0], 0.5)
    wide[...] = got_ref[...].astype(F32)

    def span(group):
        return slice(group * lanes, (group + 1) * lanes)

    def outgoing(group, _):
        return output_of(wide, out_t, group, lanes, line)

    def project(group, output):
        at = span(group)
        field = field_in[:, at] + (gate_in[:, at] * output + output)
        field_ref[:, at] = field
        return projected(field, in_t)

    def finish(group, products):
        gated(products, mask_ref[:, span(group)], group, share, sent_ref, gate_ref)

    staged(rows // SUB, (outgoing, project, finish))


def end_kernel(rows, cols, line, got_ref, field_in, gate_in, wo_ref, out_hbm, wide, out_ref, sems):
    lanes = SUB * cols
    out_t = transposed(wo_ref[1], 0.5)
    wide[...] = got_ref[...].astype(F32)
    copies = []

    def outgoing(group, _):
        return output_of(wide, out_t, group, lanes, line)

    def finish(group, output):
        at = slice(group * lanes, (group + 1) * lanes)
        field = field_in[:, at] + (gate_in[:, at] * output + output)
        out_ref[at, :] = field.astype(BF16).T
        at = pl.ds(group * lanes, lanes)
        copies.append(pltpu.make_async_copy(out_ref.at[at], out_hbm.at[at], sems.at[group]))
        copies[-1].start()

    staged(rows // SUB, (outgoing, finish))
    for copy in copies:
        copy.wait()


def moved(source, moves, count):
    shape = None
    lane = None
    targets = [[] for _ in range(count)]
    for row, begin, length, target in moves:
        shift = (target - begin) % LANES
        while length > 0:
            size = min(length, LANES - begin % LANES, LANES - target % LANES)
            targets[target // LANES].append((target % LANES, row, begin // LANES, shift))
            begin, target, length = begin + size, target + size, length - size
    rolled = {}
    registers = []
    for pieces in targets:
        value = None
        for start, row, register, shift in sorted(pieces, key=lambda piece: piece[0]):
            key = (row, register, shift)
            if key not in rolled:
                tile = source(row, register)
                rolled[key] = pltpu.roll(tile, shift, 1) if shift else tile
            if value is None:
                value = rolled[key]
            else:
                if lane is None:
                    shape = value.shape
                    lane = lax.broadcasted_iota(jnp.int32, shape, 1)
                value = jnp.where(lane < start, value, rolled[key])
        registers.append(value)
    return registers


def wide_steps(tiles):
    place_step = tiles + 1 - tiles % 2
    return place_step, SUB * place_step + 1


def row_order(groups, row_devices, rows, width):
    line = lax.broadcasted_iota(jnp.int32, (groups * SUB * row_devices, 1), 0)
    row, rest = line % row_devices, line // row_devices
    paired = groups // 2 * 2
    pair, inside = rest // (2 * SUB), rest % (2 * SUB)
    of_pair = (2 * pair + inside % 2) * SUB + inside // 2
    place = jnp.where(rest < paired * SUB, of_pair, rest)
    lane = lax.broadcasted_iota(jnp.int32, (groups * SUB * row_devices, width), 1)
    return jnp.where(lane == row * rows + place, 1.0, 0.0).astype(BF16)


def stacked(low, high):
    return jnp.concatenate([low, high], axis=0).astype(BF16)


def triangle_kernel(direction, share, rows, cols, row_devices, col_devices, line, got_ref, sent_ref,
                    wide, left_ref, right_ref, even_ref, result_ref, packed):
    groups = rows // SUB
    pieces = SUB * cols // LANES
    total = row_devices * rows
    blocks = -(-total // LANES)
    pairs = -(-groups // 2)
    rest = total - (blocks - 1) * LANES
    tail = lax.broadcasted_iota(jnp.int32, (2 * SUB, LANES), 1) < rest
    place_step, row_step = wide_steps(col_devices * groups * pieces)
    pick = row_order(groups, row_devices, rows, blocks * LANES) if direction == 1 else None

    def spot(tile):
        device, number = divmod(tile, groups * pieces)
        col, row = divmod(device, row_devices)
        return row * row_step + col * groups * pieces + number

    def widen(pair):
        for unit in range(got_ref.shape[0] // (2 * SUB)):
            owners = [tile % (groups * pieces) // pieces // 2 for tile in (2 * unit, 2 * unit + 1)]
            if min(owners) != pair:
                continue
            both = got_ref[unit * 2 * SUB : (unit + 1) * 2 * SUB, :].astype(F32)
            for half in range(2):
                at = pl.ds(spot(2 * unit + half), SUB, stride=place_step)
                wide[at, :] = both[half * SUB : (half + 1) * SUB]

    def loaded(place, group, col, piece):
        start = place * place_step + (col * groups + group) * pieces + piece
        return wide[pl.ds(start, row_devices, stride=row_step), :]

    def spread(tiles, step):
        moves = [(col, step * cols, cols, col * cols) for col in range(col_devices)]
        registers = moved(lambda col, piece: tiles[col, piece], moves, blocks)
        registers[-1] = jnp.where(tail, registers[-1], jnp.zeros_like(registers[-1]))
        return registers

    def put(target, spare, start, block, value):
        target[spare, start : start + 2 * SUB, block * LANES : (block + 1) * LANES] = value

    def put_even(spare, group, step, block, value):
        even_ref[spare, block, pl.ds(group * SUB + step, row_devices, stride=rows), :] = value

    def unpack(channel, only=range(pairs)):
        spare = channel % 2
        for pair in only:
            if 2 * pair + 1 < groups:
                unpack_pair(channel, spare, pair)
            else:
                unpack_last(channel, spare, 2 * pair)

    def unpack_pair(channel, spare, pair):
        for is_right, place in ((False, channel), (True, share + channel)):
            tiles = {}
            for col in range(col_devices):
                for piece in range(pieces):
                    tiles[col, piece] = stacked(
                        loaded(place, 2 * pair, col, piece), loaded(place, 2 * pair + 1, col, piece)
                    )
            for step in range(SUB):
                for block, register in enumerate(spread(tiles, step)):
                    if is_right and direction == 0:
                        both = register.astype(F32)
                        for half in range(2):
                            put_even(spare, 2 * pair + half, step, block, both[half * SUB : (half + 1) * SUB])
                    else:
                        target = right_ref if is_right else left_ref
                        put(target, spare, (pair * SUB + step) * 2 * SUB, block, register)

    def unpack_last(channel, spare, group):
        tiles = {}
        for col in range(col_devices):
            for piece in range(pieces):
                tiles[col, piece] = stacked(
                    loaded(channel, group, col, piece), loaded(share + channel, group, col, piece)
                )
        before = None
        for step in range(SUB):
            now = [register.astype(F32) for register in spread(tiles, step)]
            for block in range(blocks):
                if direction == 0:
                    put_even(spare, group, step, block, now[block][SUB:])
                if step % 2:
                    start = (group * SUB + step - 1) * SUB
                    put(left_ref, spare, start, block, stacked(before[block][:SUB], now[block][:SUB]))
                    if direction == 1:
                        put(right_ref, spare, start, block, stacked(before[block][SUB:], now[block][SUB:]))
            before = now

    def product(channel):
        spare = channel % 2
        if direction == 0:
            right = [even_ref[spare, block].astype(BF16) for block in range(blocks)]
            right = jnp.concatenate(right, axis=1)
            summed = matmul(left_ref[spare], right, ((1,), (1,)))
        else:
            turned = matmul(pick, left_ref[spare], ((1,), (1,))).astype(BF16)
            summed = matmul(turned, right_ref[spare], ((1,), (0,)))
        for block in range(blocks):
            size = min(LANES, total - block * LANES)
            part = summed[:, block * LANES : block * LANES + size].astype(BF16)
            result_ref[spare, block, :, 0:size] = part

    def pack(channel):
        spare = channel % 2

        def result_at(pair, step, block):
            halves = []
            for group in (2 * pair, 2 * pair + 1):
                if group >= groups:
                    halves.append(jnp.zeros((SUB, LANES), F32))
                elif 2 * pair + 1 < groups:
                    start = (pair * SUB + step) * 2 * SUB
                    return result_ref[spare, block, start : start + 2 * SUB, :]
                else:
                    start = (group * SUB + step // 2 * 2) * SUB
                    both = result_ref[spare, block, start : start + 2 * SUB, :].astype(F32)
                    halves.append(both[step % 2 * SUB : (step % 2 + 1) * SUB])
            return stacked(*halves)

        for pair in range(pairs):
            tiles = {}
            for step in range(SUB):
                for block in range(blocks):
                    tiles[step, block] = result_at(pair, step, block)
            for col in range(col_devices):
                moves = [(step, col * cols, cols, step * cols) for step in range(SUB)]
                registers = moved(lambda step, block: tiles[step, block], moves, pieces)
                for piece in range(pieces):
                    both = registers[piece].astype(F32)
                    for half in range(2):
                        group = 2 * pair + half
                        if group < groups:
                            start = (col * row_devices * share + channel) * line + group * pieces + piece
                            packed[pl.ds(start, row_devices, stride=share * line), :] = (
                                both[half * SUB : (half + 1) * SUB]
                            )

    widen(0)
    for pair in range(pairs):
        if pair + 1 < pairs:
            widen(pair + 1)
        unpack(0, [pair])
    for channel in range(share):
        product(channel)
        if channel > 0:
            pack(channel - 1)
        if channel + 1 < share:
            unpack(channel + 1)
    pack(share - 1)
    sent_ref[...] = packed[...].astype(BF16)


def by_channels(pair, token_mask, chain_ids, chain_bias, in_weights, out_weights, row_devices, col_devices):
    rows, cols, width = pair.shape
    devices = row_devices * col_devices
    share = width // devices
    lanes = SUB * cols
    pieces = lanes // LANES
    groups = rows // SUB
    chunk = groups * pieces * SUB
    spots = rows * cols
    line = groups * pieces
    total = row_devices * rows
    blocks = -(-total // LANES)
    tall = groups * SUB * row_devices
    params = pltpu.CompilerParams(vmem_limit_bytes=40 * 1024 * 1024)
    whole = pl.BlockSpec(memory_space=pltpu.VMEM)
    far = pl.BlockSpec(memory_space=pltpu.HBM)

    sent_shape = jax.ShapeDtypeStruct((devices, groups, pieces * SUB, LANES), BF16)
    sum_shape = jax.ShapeDtypeStruct((devices * share * line, LANES), BF16)
    state_shape = jax.ShapeDtypeStruct((width, spots), F32)
    mask_shape = jax.ShapeDtypeStruct((1, spots), F32)

    def exchange(array, rows):
        shape = (devices, rows) if rows % SUB == 0 else (devices, rows * 2 // SUB, SUB // 2)
        split = array.reshape(*shape, LANES)
        return lax.all_to_all(split, ("col", "row"), 0, 0, tiled=True).reshape(devices * rows, LANES)

    def triangle(direction, sent):
        wide_rows = row_devices * wide_steps(col_devices * groups * pieces)[1]
        summed = pl.pallas_call(
            functools.partial(
                triangle_kernel, direction, share, rows, cols, row_devices, col_devices, line
            ),
            out_shape=sum_shape,
            in_specs=[whole],
            out_specs=whole,
            scratch_shapes=[
                pltpu.VMEM((-(-wide_rows // SUB) * SUB, LANES), F32),
                pltpu.VMEM((2, tall, blocks * LANES), BF16),
                pltpu.VMEM((2, tall, blocks * LANES), BF16),
                pltpu.VMEM((2, blocks, total, LANES), F32),
                pltpu.VMEM((2, blocks, tall, LANES), BF16),
                pltpu.VMEM(sum_shape.shape, F32),
            ],
            compiler_params=params,
            name="triangle",
        )(exchange(sent, chunk))
        return exchange(summed, share * line)

    flat_pair = pair.reshape(spots, width)
    sent, gate, field, mask = pl.pallas_call(
        functools.partial(start_kernel, share, rows, cols),
        out_shape=[sent_shape, state_shape, state_shape, mask_shape],
        in_specs=[far] * 5,
        out_specs=[far] * 4,
        scratch_shapes=[
            pltpu.VMEM(sent_shape.shape, BF16),
            pltpu.VMEM(state_shape.shape, F32),
            pltpu.VMEM(state_shape.shape, F32),
            pltpu.VMEM(mask_shape.shape, F32),
            pltpu.VMEM((spots, width), BF16),
            pltpu.VMEM(in_weights.shape[1:], BF16),
            pltpu.VMEM((1, width), F32),
            pltpu.VMEM((1,) + token_mask.shape, jnp.int32),
            pltpu.VMEM((1,) + chain_ids.shape, jnp.int32),
            pltpu.SemaphoreType.DMA((7 + 2 * groups,)),
        ],
        compiler_params=pltpu.CompilerParams(vmem_limit_bytes=60 * 1024 * 1024),
        name="start",
    )(token_mask, chain_ids, flat_pair, chain_bias, in_weights)
    got = triangle(0, sent)
    sent, gate, field = pl.pallas_call(
        functools.partial(middle_kernel, share, rows, cols, line),
        out_shape=[sent_shape, state_shape, state_shape],
        in_specs=[whole] * 6,
        out_specs=[whole] * 3,
        scratch_shapes=[pltpu.VMEM(sum_shape.shape, F32)],
        compiler_params=params,
        name="middle",
    )(mask, got, field, gate, out_weights, in_weights)
    got = triangle(1, sent)
    out = pl.pallas_call(
        functools.partial(end_kernel, rows, cols, line),
        out_shape=jax.ShapeDtypeStruct((spots, width), BF16),
        in_specs=[whole] * 4,
        out_specs=far,
        scratch_shapes=[
            pltpu.VMEM(sum_shape.shape, F32),
            pltpu.VMEM((spots, width), BF16),
            pltpu.SemaphoreType.DMA((groups,)),
        ],
        compiler_params=params,
        name="end",
    )(got, field, gate, out_weights)
    return out.reshape(pair.shape)


def gated_inputs(field, weights, pair_mask):
    width = weights.shape[0]
    normed = layer_norm(field).astype(BF16)
    projected = jnp.einsum("ijc,cd->ijd", normed, weights, preferred_element_type=F32)
    first = (
        jax.nn.sigmoid(projected[..., :width])
        * projected[..., width : 2 * width]
        * pair_mask[:, :, None]
    ).astype(BF16)
    second = (
        jax.nn.sigmoid(projected[..., 2 * width : 3 * width])
        * projected[..., 3 * width : 4 * width]
        * pair_mask[:, :, None]
    ).astype(BF16)
    gate_value = jax.nn.sigmoid(projected[..., 4 * width :])
    return (first, second, gate_value)


def update(field, summed, gate_value, weights):
    normed_sum = layer_norm(summed).astype(BF16)
    output = jnp.einsum("ijc,cd->ijd", normed_sum, weights, preferred_element_type=F32)
    return field + gate_value * output


def by_blocks(pair, token_mask, chain_ids, chain_bias, in_weights, out_weights):
    row_count = pair.shape[0]
    col_count = pair.shape[1]
    row_start = lax.axis_index("row") * row_count
    col_start = lax.axis_index("col") * col_count
    valid_rows = lax.dynamic_slice_in_dim(token_mask, row_start, row_count).astype(F32)
    valid_cols = lax.dynamic_slice_in_dim(token_mask, col_start, col_count).astype(F32)
    chain_rows = lax.dynamic_slice_in_dim(chain_ids, row_start, row_count)
    chain_cols = lax.dynamic_slice_in_dim(chain_ids, col_start, col_count)
    pair_mask = valid_rows[:, None] * valid_cols[None, :]
    same_chain = (chain_rows[:, None] == chain_cols[None, :]).astype(F32)
    field = pair.astype(F32) + same_chain[:, :, None] * chain_bias
    first, second, gate_value = gated_inputs(field, in_weights[0], pair_mask)
    second_rows = lax.all_gather(second, "row", axis=0, tiled=True)
    part = jnp.einsum("jkc,ikc->jic", second_rows, first, preferred_element_type=F32).astype(BF16)
    summed = lax.psum_scatter(part, "col", scatter_dimension=0, tiled=True).astype(F32)
    summed = jnp.transpose(summed, (1, 0, 2))
    field = update(field, summed, gate_value, out_weights[0])
    first, second, gate_value = gated_inputs(field, in_weights[1], pair_mask)
    first_cols = lax.all_gather(first, "col", axis=1, tiled=True)
    part = jnp.einsum("kic,kjc->ijc", first_cols, second, preferred_element_type=F32).astype(BF16)
    summed = lax.psum_scatter(part, "row", scatter_dimension=0, tiled=True).astype(F32)
    field = update(field, summed, gate_value, out_weights[1])
    return field.astype(BF16)


def solution(mesh):
    row_devices, col_devices = mesh.shape["row"], mesh.shape["col"]

    def per_device(pair, *rest):
        rows, cols, width = pair.shape
        devices = row_devices * col_devices
        fits = (
            width % devices == 0
            and 2 * (width // devices) == SUB
            and row_devices == SUB
            and rows % SUB == 0
            and (SUB * cols) % LANES == 0
            and max(rows, cols) <= LANES
        )
        if fits:
            return by_channels(pair, *rest, row_devices, col_devices)
        return by_blocks(pair, *rest)

    return jax.shard_map(
        per_device,
        mesh=mesh,
        in_specs=(P("row", "col", None), P(), P(), P(), P(), P()),
        out_specs=P("row", "col", None),
        check_vma=False,
    )
```

```python
import functools

import jax
import jax.numpy as jnp
from jax import lax
from jax.experimental import pallas as pl
from jax.experimental.pallas import tpu as pltpu
from jax.sharding import PartitionSpec as P

LANES = 128
SUB = 8
F32 = jnp.float32
BF16 = jnp.bfloat16


def layer_norm(values, axis=-1):
    center = values - jnp.mean(values, axis=axis, keepdims=True)
    spread = jnp.mean(center * center, axis=axis, keepdims=True)
    return center * lax.rsqrt(spread + 1e-05)


def matmul(left, right, dims):
    return lax.dot_general(left, right, (dims, ((), ())), preferred_element_type=F32)


def identity(size, scale):
    row = lax.broadcasted_iota(jnp.int32, (size, size), 0)
    col = lax.broadcasted_iota(jnp.int32, (size, size), 1)
    return jnp.where(row == col, scale, 0.0).astype(BF16)


def column(row_ref):
    width = row_ref.shape[1]
    return jnp.broadcast_to(row_ref[...], (width, width)).T[:, 0:1]


def transposed(weights, scale):
    eye = identity(weights.shape[1], scale)
    return matmul(eye, weights, ((1,), (1,))).astype(BF16)


def interleaved(first, second, share):
    width = first.shape[1]
    both = jnp.concatenate([first, second], axis=1)
    row = lax.broadcasted_iota(jnp.int32, (2 * width, 1), 0)
    col = lax.broadcasted_iota(jnp.int32, (2 * width, 2 * width), 1)
    owner, place = row // (2 * share), row % (2 * share)
    source = owner * share + place % share + jnp.where(place >= share, width, 0)
    pick = jnp.where(col == source, 0.5, 0.0).astype(BF16)
    return matmul(pick, both, ((1,), (1,))).astype(BF16)


def load_in_weights(weights, share):
    width = weights.shape[0]
    blocks = [weights[:, k * width : (k + 1) * width] for k in range(5)]
    return (
        interleaved(blocks[0], blocks[2], share),
        interleaved(blocks[1], blocks[3], share),
        transposed(blocks[4], 0.5),
    )


def token_vectors(tokens, row_start, col_start, rows, cols):
    groups = rows // SUB
    wide = tokens.shape[1]
    many = jnp.broadcast_to(tokens.astype(F32), (SUB, wide))
    lane = lax.broadcasted_iota(jnp.int32, (1, SUB * cols), 1)
    at_row = jnp.zeros_like(lane)
    for step in range(1, SUB):
        at_row = at_row + jnp.where(lane >= step * cols, 1, 0)
    at_col = lane - at_row * cols
    key = lax.broadcasted_iota(jnp.int32, (LANES, SUB * cols), 0)
    pick_row = jnp.where(key == at_row, 1.0, 0.0).astype(BF16)
    pick_col = jnp.where(key == at_col, 1.0, 0.0).astype(BF16)

    def window(start):
        return pltpu.roll(many, wide - start, 1)[:, :LANES]

    by_col = matmul(window(col_start).astype(BF16), pick_col, ((1,), (0,)))[0:1]
    windows = [window(row_start + group * SUB)[0:1] for group in range(groups)]
    windows.append(jnp.zeros((-groups % SUB, LANES), F32))
    by_row = matmul(jnp.concatenate(windows, axis=0).astype(BF16), pick_row, ((1,), (0,)))
    by_row = by_row.astype(jnp.int32)
    by_col = by_col.astype(jnp.int32)
    masks = (by_row & by_col & 1).astype(F32)
    sames = jnp.where((by_row >> 1) == (by_col >> 1), 1.0, 0.0)
    return masks, sames


def staged(count, stages):
    held = {}
    for step in range(count + len(stages) - 1):
        for number, stage in enumerate(stages):
            item = step - number
            if 0 <= item < count:
                held[item] = stage(item, held.get(item))


def projected(field, in_t):
    normed = layer_norm(field, 0).astype(BF16)
    return [matmul(weights, normed, ((1,), (0,))) for weights in in_t]


def gated(products, mask, group, share, sent_ref, gate_ref):
    gates, values, gate = products
    width, lanes = gate.shape
    sent = (jnp.tanh(gates) * values + values) * mask
    for owner in range(width // share):
        block = sent[owner * 2 * share : (owner + 1) * 2 * share]
        lines = [block[:, at : at + LANES] for at in range(0, lanes, LANES)]
        sent_ref[owner, group] = jnp.concatenate(lines, axis=0).astype(BF16)
    gate_ref[:, group * lanes : (group + 1) * lanes] = jnp.tanh(gate)


def start_kernel(share, rows, cols, valid_hbm, chain_hbm, pair_hbm, bias_hbm, w_hbm,
                 sent_hbm, gate_hbm, field_hbm, mask_hbm, sent_ref, gate_ref, field_ref, mask_ref,
                 pair_ref, w_ref, bias_ref, valid_ref, chain_ref, sems):
    lanes = SUB * cols
    groups = rows // SUB
    width = pair_ref.shape[1]
    count = valid_hbm.shape[0]
    started = []

    def copy(near, far):
        started.append(pltpu.make_async_copy(near, far, sems.at[len(started)]))
        started[-1].start()

    copy(w_hbm.at[0], w_ref)
    copy(valid_hbm, valid_ref.at[0])
    copy(chain_hbm, chain_ref.at[0])
    copy(bias_hbm, bias_ref.at[0])
    for at in (pl.ds(0, 2 * lanes), pl.ds(2 * lanes, (groups - 2) * lanes)):
        copy(pair_hbm.at[at], pair_ref.at[at])
    arriving = len(started)
    eye = identity(width, 1.0)
    row_start = lax.axis_index("row") * rows
    col_start = lax.axis_index("col") * cols
    started[0].wait()
    in_t = load_in_weights(w_ref[...], share)
    for number in range(1, arriving - 1):
        started[number].wait()

    def lift(group):
        if group == 2:
            started[arriving - 1].wait()
        rows_of = pair_ref[group * lanes : (group + 1) * lanes, :]
        return matmul(eye, rows_of, ((1,), (1,)))

    lifted = {0: lift(0)}
    tokens = chain_ref[...] * 2 + valid_ref[...]
    tokens = jnp.concatenate([tokens, jnp.zeros((1, -count % LANES), jnp.int32)], axis=1)
    masks, sames = token_vectors(tokens, row_start, col_start, rows, cols)
    bias_col = column(bias_ref)

    def make_field(group, _):
        at = slice(group * lanes, (group + 1) * lanes)
        if group + 1 < groups:
            lifted[group + 1] = lift(group + 1)
        field = lifted.pop(group) + bias_col * sames[group : group + 1]
        field_ref[:, at] = field
        mask_ref[:, at] = masks[group : group + 1]
        return field

    def project(group, field):
        if group == groups - 1:
            copy(field_ref, field_hbm)
            copy(mask_ref, mask_hbm)
        return projected(field, in_t)

    def finish(group, products):
        gated(products, masks[group : group + 1], group, share, sent_ref, gate_ref)
        copy(sent_ref.at[:, group], sent_hbm.at[:, group])
        at = pl.ds(group * lanes, lanes)
        copy(gate_ref.at[:, at], gate_hbm.at[:, at])

    staged(groups, (make_field, project, finish))
    for number in range(arriving, len(started)):
        started[number].wait()


def output_of(wide, out_t, group, lanes, line):
    width = out_t.shape[1]
    pieces = lanes // LANES
    parts = []
    for piece in range(pieces):
        parts.append(wide[pl.ds(group * pieces + piece, width, stride=line), :])
    normed = layer_norm(jnp.concatenate(parts, axis=1), 0).astype(BF16)
    return matmul(out_t, normed, ((1,), (0,)))


def middle_kernel(share, rows, cols, line, mask_ref, got_ref, field_in, gate_in, wo_ref, w_ref,
                  sent_ref, gate_ref, field_ref, wide):
    lanes = SUB * cols
    half = got_ref.shape[0] // 2
    wide[:half, :] = got_ref[:half, :].astype(F32)
    out_t = transposed(wo_ref[0], 0.5)
    wide[half:, :] = got_ref[half:, :].astype(F32)
    in_t = load_in_weights(w_ref[1], share)

    def span(group):
        return slice(group * lanes, (group + 1) * lanes)

    def outgoing(group, _):
        return output_of(wide, out_t, group, lanes, line)

    def project(group, output):
        at = span(group)
        field = field_in[:, at] + (gate_in[:, at] * output + output)
        field_ref[:, at] = field
        return projected(field, in_t)

    def finish(group, products):
        gated(products, mask_ref[:, span(group)], group, share, sent_ref, gate_ref)

    staged(rows // SUB, (outgoing, project, finish))


def end_kernel(rows, cols, line, got_ref, field_in, gate_in, wo_ref, out_hbm, wide, out_ref, sems):
    lanes = SUB * cols
    out_t = transposed(wo_ref[1], 0.5)
    wide[...] = got_ref[...].astype(F32)
    copies = []

    def outgoing(group, _):
        return output_of(wide, out_t, group, lanes, line)

    def finish(group, output):
        at = slice(group * lanes, (group + 1) * lanes)
        field = field_in[:, at] + (gate_in[:, at] * output + output)
        out_ref[at, :] = field.astype(BF16).T
        at = pl.ds(group * lanes, lanes)
        copies.append(pltpu.make_async_copy(out_ref.at[at], out_hbm.at[at], sems.at[group]))
        copies[-1].start()

    staged(rows // SUB, (outgoing, finish))
    for copy in copies:
        copy.wait()


def moved(source, moves, count):
    shape = None
    lane = None
    targets = [[] for _ in range(count)]
    for row, begin, length, target in moves:
        shift = (target - begin) % LANES
        while length > 0:
            size = min(length, LANES - begin % LANES, LANES - target % LANES)
            targets[target // LANES].append((target % LANES, row, begin // LANES, shift))
            begin, target, length = begin + size, target + size, length - size
    rolled = {}
    registers = []
    for pieces in targets:
        value = None
        for start, row, register, shift in sorted(pieces, key=lambda piece: piece[0]):
            key = (row, register, shift)
            if key not in rolled:
                tile = source(row, register)
                rolled[key] = pltpu.roll(tile, shift, 1) if shift else tile
            if value is None:
                value = rolled[key]
            else:
                if lane is None:
                    shape = value.shape
                    lane = lax.broadcasted_iota(jnp.int32, shape, 1)
                value = jnp.where(lane < start, value, rolled[key])
        registers.append(value)
    return registers


def wide_steps(tiles):
    place_step = tiles + 1 - tiles % 2
    return place_step, SUB * place_step + 1


def row_order(groups, row_devices, rows, width):
    line = lax.broadcasted_iota(jnp.int32, (groups * SUB * row_devices, 1), 0)
    row, rest = line % row_devices, line // row_devices
    paired = groups // 2 * 2
    pair, inside = rest // (2 * SUB), rest % (2 * SUB)
    of_pair = (2 * pair + inside % 2) * SUB + inside // 2
    place = jnp.where(rest < paired * SUB, of_pair, rest)
    lane = lax.broadcasted_iota(jnp.int32, (groups * SUB * row_devices, width), 1)
    return jnp.where(lane == row * rows + place, 1.0, 0.0).astype(BF16)


def stacked(low, high):
    return jnp.concatenate([low, high], axis=0).astype(BF16)


def triangle_kernel(direction, share, rows, cols, row_devices, col_devices, line, got_ref, sent_ref,
                    wide, left_ref, right_ref, even_ref, result_ref, packed):
    groups = rows // SUB
    pieces = SUB * cols // LANES
    total = row_devices * rows
    blocks = -(-total // LANES)
    pairs = -(-groups // 2)
    rest = total - (blocks - 1) * LANES
    tail = lax.broadcasted_iota(jnp.int32, (2 * SUB, LANES), 1) < rest
    place_step, row_step = wide_steps(col_devices * groups * pieces)
    pick = row_order(groups, row_devices, rows, blocks * LANES) if direction == 1 else None

    def spot(tile):
        device, number = divmod(tile, groups * pieces)
        col, row = divmod(device, row_devices)
        return row * row_step + col * groups * pieces + number

    def widen(pair):
        for unit in range(got_ref.shape[0] // (2 * SUB)):
            owners = [tile % (groups * pieces) // pieces // 2 for tile in (2 * unit, 2 * unit + 1)]
            if min(owners) != pair:
                continue
            both = got_ref[unit * 2 * SUB : (unit + 1) * 2 * SUB, :].astype(F32)
            for half in range(2):
                at = pl.ds(spot(2 * unit + half), SUB, stride=place_step)
                wide[at, :] = both[half * SUB : (half + 1) * SUB]

    def loaded(place, group, col, piece):
        start = place * place_step + (col * groups + group) * pieces + piece
        return wide[pl.ds(start, row_devices, stride=row_step), :]

    def spread(tiles, step, cleared):
        moves = [(col, step * cols, cols, col * cols) for col in range(col_devices)]
        registers = moved(lambda col, piece: tiles[col, piece], moves, blocks)
        if cleared:
            registers[-1] = jnp.where(tail, registers[-1], jnp.zeros_like(registers[-1]))
        return registers

    def put(target, spare, start, block, value):
        target[spare, start : start + 2 * SUB, block * LANES : (block + 1) * LANES] = value

    def put_even(spare, group, step, block, value):
        even_ref[spare, block, pl.ds(group * SUB + step, row_devices, stride=rows), :] = value

    def unpack(channel, only=range(pairs)):
        spare = channel % 2
        for pair in only:
            if 2 * pair + 1 < groups:
                unpack_pair(channel, spare, pair)
            else:
                unpack_last(channel, spare, 2 * pair)

    def unpack_pair(channel, spare, pair):
        for is_right, place in ((False, channel), (True, share + channel)):
            tiles = {}
            for col in range(col_devices):
                for piece in range(pieces):
                    tiles[col, piece] = stacked(
                        loaded(place, 2 * pair, col, piece), loaded(place, 2 * pair + 1, col, piece)
                    )
            for step in range(SUB):
                for block, register in enumerate(spread(tiles, step, direction == 0 and not is_right)):
                    if is_right and direction == 0:
                        both = register.astype(F32)
                        for half in range(2):
                            put_even(spare, 2 * pair + half, step, block, both[half * SUB : (half + 1) * SUB])
                    else:
                        target = right_ref if is_right else left_ref
                        put(target, spare, (pair * SUB + step) * 2 * SUB, block, register)

    def unpack_last(channel, spare, group):
        tiles = {}
        for col in range(col_devices):
            for piece in range(pieces):
                tiles[col, piece] = stacked(
                    loaded(channel, group, col, piece), loaded(share + channel, group, col, piece)
                )
        before = None
        for step in range(SUB):
            now = [register.astype(F32) for register in spread(tiles, step, direction == 0)]
            for block in range(blocks):
                if direction == 0:
                    put_even(spare, group, step, block, now[block][SUB:])
                if step % 2:
                    start = (group * SUB + step - 1) * SUB
                    put(left_ref, spare, start, block, stacked(before[block][:SUB], now[block][:SUB]))
                    if direction == 1:
                        put(right_ref, spare, start, block, stacked(before[block][SUB:], now[block][SUB:]))
            before = now

    def product(channel):
        spare = channel % 2
        if direction == 0:
            right = [even_ref[spare, block].astype(BF16) for block in range(blocks)]
            right = jnp.concatenate(right, axis=1)
            summed = matmul(left_ref[spare], right, ((1,), (1,)))
        else:
            turned = matmul(pick, left_ref[spare], ((1,), (1,))).astype(BF16)
            summed = matmul(turned, right_ref[spare], ((1,), (0,)))
        for block in range(blocks):
            size = min(LANES, total - block * LANES)
            part = summed[:, block * LANES : block * LANES + size].astype(BF16)
            result_ref[channel, block, :, 0:size] = part

    def send(tiles, targets):
        for col in range(col_devices):
            moves = [(step, col * cols, cols, step * cols) for step in range(SUB)]
            registers = moved(lambda step, block: tiles[step, block], moves, pieces)
            for piece in range(pieces):
                both = registers[piece].astype(F32)
                for half, (channel, group) in enumerate(targets):
                    start = (col * row_devices * share + channel) * line + group * pieces + piece
                    packed[pl.ds(start, row_devices, stride=share * line), :] = (
                        both[half * SUB : (half + 1) * SUB]
                    )

    def pack(channel):
        for pair in range(groups // 2):
            tiles = {}
            for step in range(SUB):
                for block in range(blocks):
                    start = (pair * SUB + step) * 2 * SUB
                    tiles[step, block] = result_ref[channel, block, start : start + 2 * SUB, :]
            send(tiles, [(channel, 2 * pair), (channel, 2 * pair + 1)])
        if groups % 2 and channel % 2:
            group = groups - 1
            tiles = {}
            for block in range(blocks):
                for step in range(0, SUB, 2):
                    start = (group * SUB + step) * SUB
                    low, high = [
                        result_ref[one, block, start : start + 2 * SUB, :].astype(F32)
                        for one in (channel - 1, channel)
                    ]
                    tiles[step, block] = stacked(low[:SUB], high[:SUB])
                    tiles[step + 1, block] = stacked(low[SUB:], high[SUB:])
            send(tiles, [(channel - 1, group), (channel, group)])

    widen(0)
    for pair in range(pairs):
        if pair + 1 < pairs:
            widen(pair + 1)
        unpack(0, [pair])
    for channel in range(share):
        product(channel)
        if channel > 0:
            pack(channel - 1)
        if channel + 1 < share:
            unpack(channel + 1)
    pack(share - 1)
    sent_ref[...] = packed[...].astype(BF16)


def by_channels(pair, token_mask, chain_ids, chain_bias, in_weights, out_weights, row_devices, col_devices):
    rows, cols, width = pair.shape
    devices = row_devices * col_devices
    share = width // devices
    lanes = SUB * cols
    pieces = lanes // LANES
    groups = rows // SUB
    chunk = groups * pieces * SUB
    spots = rows * cols
    line = groups * pieces
    total = row_devices * rows
    blocks = -(-total // LANES)
    tall = groups * SUB * row_devices
    params = pltpu.CompilerParams(vmem_limit_bytes=40 * 1024 * 1024)
    whole = pl.BlockSpec(memory_space=pltpu.VMEM)
    far = pl.BlockSpec(memory_space=pltpu.HBM)

    sent_shape = jax.ShapeDtypeStruct((devices, groups, pieces * SUB, LANES), BF16)
    sum_shape = jax.ShapeDtypeStruct((devices * share * line, LANES), BF16)
    state_shape = jax.ShapeDtypeStruct((width, spots), F32)
    mask_shape = jax.ShapeDtypeStruct((1, spots), F32)

    def exchange(array, rows):
        shape = (devices, rows) if rows % SUB == 0 else (devices, rows * 2 // SUB, SUB // 2)
        split = array.reshape(*shape, LANES)
        return lax.all_to_all(split, ("col", "row"), 0, 0, tiled=True).reshape(devices * rows, LANES)

    def triangle(direction, sent):
        wide_rows = row_devices * wide_steps(col_devices * groups * pieces)[1]
        summed = pl.pallas_call(
            functools.partial(
                triangle_kernel, direction, share, rows, cols, row_devices, col_devices, line
            ),
            out_shape=sum_shape,
            in_specs=[whole],
            out_specs=whole,
            scratch_shapes=[
                pltpu.VMEM((-(-wide_rows // SUB) * SUB, LANES), F32),
                pltpu.VMEM((2, tall, blocks * LANES), BF16),
                pltpu.VMEM((2, tall, blocks * LANES), BF16),
                pltpu.VMEM((2, blocks, total, LANES), F32),
                pltpu.VMEM((share, blocks, tall, LANES), BF16),
                pltpu.VMEM(sum_shape.shape, F32),
            ],
            compiler_params=params,
            name="triangle",
        )(exchange(sent, chunk))
        return exchange(summed, share * line)

    flat_pair = pair.reshape(spots, width)
    sent, gate, field, mask = pl.pallas_call(
        functools.partial(start_kernel, share, rows, cols),
        out_shape=[sent_shape, state_shape, state_shape, mask_shape],
        in_specs=[far] * 5,
        out_specs=[far] * 4,
        scratch_shapes=[
            pltpu.VMEM(sent_shape.shape, BF16),
            pltpu.VMEM(state_shape.shape, F32),
            pltpu.VMEM(state_shape.shape, F32),
            pltpu.VMEM(mask_shape.shape, F32),
            pltpu.VMEM((spots, width), BF16),
            pltpu.VMEM(in_weights.shape[1:], BF16),
            pltpu.VMEM((1, width), F32),
            pltpu.VMEM((1,) + token_mask.shape, jnp.int32),
            pltpu.VMEM((1,) + chain_ids.shape, jnp.int32),
            pltpu.SemaphoreType.DMA((8 + 2 * groups,)),
        ],
        compiler_params=pltpu.CompilerParams(vmem_limit_bytes=60 * 1024 * 1024),
        name="start",
    )(token_mask, chain_ids, flat_pair, chain_bias, in_weights)
    got = triangle(0, sent)
    sent, gate, field = pl.pallas_call(
        functools.partial(middle_kernel, share, rows, cols, line),
        out_shape=[sent_shape, state_shape, state_shape],
        in_specs=[whole] * 6,
        out_specs=[whole] * 3,
        scratch_shapes=[pltpu.VMEM(sum_shape.shape, F32)],
        compiler_params=params,
        name="middle",
    )(mask, got, field, gate, out_weights, in_weights)
    got = triangle(1, sent)
    out = pl.pallas_call(
        functools.partial(end_kernel, rows, cols, line),
        out_shape=jax.ShapeDtypeStruct((spots, width), BF16),
        in_specs=[whole] * 4,
        out_specs=far,
        scratch_shapes=[
            pltpu.VMEM(sum_shape.shape, F32),
            pltpu.VMEM((spots, width), BF16),
            pltpu.SemaphoreType.DMA((groups,)),
        ],
        compiler_params=params,
        name="end",
    )(got, field, gate, out_weights)
    return out.reshape(pair.shape)


def gated_inputs(field, weights, pair_mask):
    width = weights.shape[0]
    normed = layer_norm(field).astype(BF16)
    projected = jnp.einsum("ijc,cd->ijd", normed, weights, preferred_element_type=F32)
    first = (
        jax.nn.sigmoid(projected[..., :width])
        * projected[..., width : 2 * width]
        * pair_mask[:, :, None]
    ).astype(BF16)
    second = (
        jax.nn.sigmoid(projected[..., 2 * width : 3 * width])
        * projected[..., 3 * width : 4 * width]
        * pair_mask[:, :, None]
    ).astype(BF16)
    gate_value = jax.nn.sigmoid(projected[..., 4 * width :])
    return (first, second, gate_value)


def update(field, summed, gate_value, weights):
    normed_sum = layer_norm(summed).astype(BF16)
    output = jnp.einsum("ijc,cd->ijd", normed_sum, weights, preferred_element_type=F32)
    return field + gate_value * output


def by_blocks(pair, token_mask, chain_ids, chain_bias, in_weights, out_weights):
    row_count = pair.shape[0]
    col_count = pair.shape[1]
    row_start = lax.axis_index("row") * row_count
    col_start = lax.axis_index("col") * col_count
    valid_rows = lax.dynamic_slice_in_dim(token_mask, row_start, row_count).astype(F32)
    valid_cols = lax.dynamic_slice_in_dim(token_mask, col_start, col_count).astype(F32)
    chain_rows = lax.dynamic_slice_in_dim(chain_ids, row_start, row_count)
    chain_cols = lax.dynamic_slice_in_dim(chain_ids, col_start, col_count)
    pair_mask = valid_rows[:, None] * valid_cols[None, :]
    same_chain = (chain_rows[:, None] == chain_cols[None, :]).astype(F32)
    field = pair.astype(F32) + same_chain[:, :, None] * chain_bias
    first, second, gate_value = gated_inputs(field, in_weights[0], pair_mask)
    second_rows = lax.all_gather(second, "row", axis=0, tiled=True)
    part = jnp.einsum("jkc,ikc->jic", second_rows, first, preferred_element_type=F32).astype(BF16)
    summed = lax.psum_scatter(part, "col", scatter_dimension=0, tiled=True).astype(F32)
    summed = jnp.transpose(summed, (1, 0, 2))
    field = update(field, summed, gate_value, out_weights[0])
    first, second, gate_value = gated_inputs(field, in_weights[1], pair_mask)
    first_cols = lax.all_gather(first, "col", axis=1, tiled=True)
    part = jnp.einsum("kic,kjc->ijc", first_cols, second, preferred_element_type=F32).astype(BF16)
    summed = lax.psum_scatter(part, "row", scatter_dimension=0, tiled=True).astype(F32)
    field = update(field, summed, gate_value, out_weights[1])
    return field.astype(BF16)


def solution(mesh):
    row_devices, col_devices = mesh.shape["row"], mesh.shape["col"]

    def per_device(pair, *rest):
        rows, cols, width = pair.shape
        devices = row_devices * col_devices
        fits = (
            width % devices == 0
            and 2 * (width // devices) == SUB
            and row_devices == SUB
            and rows % SUB == 0
            and rows >= 3 * SUB
            and (SUB * cols) % LANES == 0
            and max(rows, cols) <= LANES
        )
        if fits:
            return by_channels(pair, *rest, row_devices, col_devices)
        return by_blocks(pair, *rest)

    return jax.shard_map(
        per_device,
        mesh=mesh,
        in_specs=(P("row", "col", None), P(), P(), P(), P(), P()),
        out_specs=P("row", "col", None),
        check_vma=False,
    )
```

```python
import functools

import jax
import jax.numpy as jnp
from jax import lax
from jax.experimental import pallas as pl
from jax.experimental.pallas import tpu as pltpu
from jax.sharding import PartitionSpec as P

LANES = 128
SUB = 8
F32 = jnp.float32
BF16 = jnp.bfloat16


def layer_norm(values, axis=-1):
    center = values - jnp.mean(values, axis=axis, keepdims=True)
    spread = jnp.mean(center * center, axis=axis, keepdims=True)
    return center * lax.rsqrt(spread + 1e-05)


def matmul(left, right, dims):
    return lax.dot_general(left, right, (dims, ((), ())), preferred_element_type=F32)


def identity(size, scale):
    row = lax.broadcasted_iota(jnp.int32, (size, size), 0)
    col = lax.broadcasted_iota(jnp.int32, (size, size), 1)
    return jnp.where(row == col, scale, 0.0).astype(BF16)


def column(row_ref):
    width = row_ref.shape[1]
    return jnp.broadcast_to(row_ref[...], (width, width)).T[:, 0:1]


def transposed(weights, scale):
    eye = identity(weights.shape[1], scale)
    return matmul(eye, weights, ((1,), (1,))).astype(BF16)


def interleaved(first, second, share):
    width = first.shape[1]
    both = jnp.concatenate([first, second], axis=1)
    row = lax.broadcasted_iota(jnp.int32, (2 * width, 1), 0)
    col = lax.broadcasted_iota(jnp.int32, (2 * width, 2 * width), 1)
    owner, place = row // (2 * share), row % (2 * share)
    source = owner * share + place % share + jnp.where(place >= share, width, 0)
    pick = jnp.where(col == source, 0.5, 0.0).astype(BF16)
    return matmul(pick, both, ((1,), (1,))).astype(BF16)


def load_in_weights(weights, share):
    width = weights.shape[0]
    blocks = [weights[:, k * width : (k + 1) * width] for k in range(5)]
    return (
        interleaved(blocks[0], blocks[2], share),
        interleaved(blocks[1], blocks[3], share),
        transposed(blocks[4], 0.5),
    )


def token_vectors(tokens, row_start, col_start, rows, cols):
    groups = rows // SUB
    wide = tokens.shape[1]
    many = jnp.broadcast_to(tokens.astype(F32), (SUB, wide))
    lane = lax.broadcasted_iota(jnp.int32, (1, SUB * cols), 1)
    at_row = jnp.zeros_like(lane)
    for step in range(1, SUB):
        at_row = at_row + jnp.where(lane >= step * cols, 1, 0)
    at_col = lane - at_row * cols
    key = lax.broadcasted_iota(jnp.int32, (LANES, SUB * cols), 0)
    pick_row = jnp.where(key == at_row, 1.0, 0.0).astype(BF16)
    pick_col = jnp.where(key == at_col, 1.0, 0.0).astype(BF16)

    def window(start):
        return pltpu.roll(many, wide - start, 1)[:, :LANES]

    by_col = matmul(window(col_start).astype(BF16), pick_col, ((1,), (0,)))[0:1]
    windows = [window(row_start + group * SUB)[0:1] for group in range(groups)]
    windows.append(jnp.zeros((-groups % SUB, LANES), F32))
    by_row = matmul(jnp.concatenate(windows, axis=0).astype(BF16), pick_row, ((1,), (0,)))
    by_row = by_row.astype(jnp.int32)
    by_col = by_col.astype(jnp.int32)
    masks = (by_row & by_col & 1).astype(F32)
    sames = jnp.where((by_row >> 1) == (by_col >> 1), 1.0, 0.0)
    return masks, sames


def staged(count, stages):
    held = {}
    for step in range(count + len(stages) - 1):
        for number, stage in enumerate(stages):
            item = step - number
            if 0 <= item < count:
                held[item] = stage(item, held.get(item))


def projected(field, in_t):
    normed = layer_norm(field, 0).astype(BF16)
    return [matmul(weights, normed, ((1,), (0,))) for weights in in_t]


def gated(products, mask, group, share, sent_ref, gate_ref):
    gates, values, gate = products
    width, lanes = gate.shape
    sent = (jnp.tanh(gates) * values + values) * mask
    for owner in range(width // share):
        block = sent[owner * 2 * share : (owner + 1) * 2 * share]
        lines = [block[:, at : at + LANES] for at in range(0, lanes, LANES)]
        sent_ref[owner, group] = jnp.concatenate(lines, axis=0).astype(BF16)
    gate_ref[:, group * lanes : (group + 1) * lanes] = jnp.tanh(gate)


def start_kernel(share, rows, cols, valid_hbm, chain_hbm, pair_hbm, bias_hbm, w_hbm,
                 sent_hbm, gate_hbm, field_hbm, mask_hbm, sent_ref, gate_ref, field_ref, mask_ref,
                 pair_ref, w_ref, bias_ref, valid_ref, chain_ref, sems):
    lanes = SUB * cols
    groups = rows // SUB
    width = pair_ref.shape[1]
    count = valid_hbm.shape[0]
    started = []

    def copy(near, far):
        started.append(pltpu.make_async_copy(near, far, sems.at[len(started)]))
        started[-1].start()

    copy(w_hbm.at[0], w_ref)
    copy(valid_hbm, valid_ref.at[0])
    copy(chain_hbm, chain_ref.at[0])
    copy(bias_hbm, bias_ref.at[0])
    for at in (pl.ds(0, 2 * lanes), pl.ds(2 * lanes, (groups - 2) * lanes)):
        copy(pair_hbm.at[at], pair_ref.at[at])
    arriving = len(started)
    eye = identity(width, 1.0)
    row_start = lax.axis_index("row") * rows
    col_start = lax.axis_index("col") * cols
    started[0].wait()
    in_t = load_in_weights(w_ref[...], share)
    for number in range(1, arriving - 1):
        started[number].wait()

    def lift(group):
        if group == 2:
            started[arriving - 1].wait()
        rows_of = pair_ref[group * lanes : (group + 1) * lanes, :]
        return matmul(eye, rows_of, ((1,), (1,)))

    lifted = {0: lift(0)}
    tokens = chain_ref[...] * 2 + valid_ref[...]
    tokens = jnp.concatenate([tokens, jnp.zeros((1, -count % LANES), jnp.int32)], axis=1)
    masks, sames = token_vectors(tokens, row_start, col_start, rows, cols)
    bias_col = column(bias_ref)

    def make_field(group, _):
        at = slice(group * lanes, (group + 1) * lanes)
        if group + 1 < groups:
            lifted[group + 1] = lift(group + 1)
        field = lifted.pop(group) + bias_col * sames[group : group + 1]
        field_ref[:, at] = field
        mask_ref[:, at] = masks[group : group + 1]
        return field

    def project(group, field):
        if group == groups - 1:
            copy(field_ref, field_hbm)
            copy(mask_ref, mask_hbm)
        return projected(field, in_t)

    def finish(group, products):
        gated(products, masks[group : group + 1], group, share, sent_ref, gate_ref)
        copy(sent_ref.at[:, group], sent_hbm.at[:, group])
        at = pl.ds(group * lanes, lanes)
        copy(gate_ref.at[:, at], gate_hbm.at[:, at])

    staged(groups, (make_field, project, finish))
    for number in range(arriving, len(started)):
        started[number].wait()


def output_of(wide, out_t, group, lanes, line):
    width = out_t.shape[1]
    pieces = lanes // LANES
    parts = []
    for piece in range(pieces):
        parts.append(wide[pl.ds(group * pieces + piece, width, stride=line), :])
    normed = layer_norm(jnp.concatenate(parts, axis=1), 0).astype(BF16)
    return matmul(out_t, normed, ((1,), (0,)))


def middle_kernel(share, rows, cols, line, mask_ref, got_ref, field_in, gate_in, wo_ref, w_ref,
                  sent_ref, gate_ref, field_ref, wide):
    lanes = SUB * cols
    count = got_ref.shape[0]
    half = count // 2
    wide[:half, :] = got_ref[:half, :].astype(F32)
    out_t = transposed(wo_ref[0], 0.5)
    wide[half:count, :] = got_ref[half:, :].astype(F32)
    in_t = load_in_weights(w_ref[1], share)

    def span(group):
        return slice(group * lanes, (group + 1) * lanes)

    def outgoing(group, _):
        return output_of(wide, out_t, group, lanes, line)

    def project(group, output):
        at = span(group)
        field = field_in[:, at] + (gate_in[:, at] * output + output)
        field_ref[:, at] = field
        return projected(field, in_t)

    def finish(group, products):
        gated(products, mask_ref[:, span(group)], group, share, sent_ref, gate_ref)

    staged(rows // SUB, (outgoing, project, finish))


def end_kernel(rows, cols, line, got_ref, field_in, gate_in, wo_ref, out_hbm, wide, out_ref, sems):
    lanes = SUB * cols
    out_t = transposed(wo_ref[1], 0.5)
    wide[: got_ref.shape[0], :] = got_ref[...].astype(F32)
    copies = []

    def outgoing(group, _):
        return output_of(wide, out_t, group, lanes, line)

    def finish(group, output):
        at = slice(group * lanes, (group + 1) * lanes)
        field = field_in[:, at] + (gate_in[:, at] * output + output)
        out_ref[at, :] = field.astype(BF16).T
        at = pl.ds(group * lanes, lanes)
        copies.append(pltpu.make_async_copy(out_ref.at[at], out_hbm.at[at], sems.at[group]))
        copies[-1].start()

    staged(rows // SUB, (outgoing, finish))
    for copy in copies:
        copy.wait()


def moved(source, moves, count):
    shape = None
    lane = None
    targets = [[] for _ in range(count)]
    for row, begin, length, target in moves:
        shift = (target - begin) % LANES
        while length > 0:
            size = min(length, LANES - begin % LANES, LANES - target % LANES)
            targets[target // LANES].append((target % LANES, row, begin // LANES, shift))
            begin, target, length = begin + size, target + size, length - size
    rolled = {}
    registers = []
    for pieces in targets:
        value = None
        for start, row, register, shift in sorted(pieces, key=lambda piece: piece[0]):
            key = (row, register, shift)
            if key not in rolled:
                tile = source(row, register)
                rolled[key] = pltpu.roll(tile, shift, 1) if shift else tile
            if value is None:
                value = rolled[key]
            else:
                if lane is None:
                    shape = value.shape
                    lane = lax.broadcasted_iota(jnp.int32, shape, 1)
                value = jnp.where(lane < start, value, rolled[key])
        registers.append(value)
    return registers


def wide_steps(tiles):
    place_step = tiles + 1 - tiles % 2
    return place_step, SUB * place_step + 1


def row_order(groups, row_devices, rows, width):
    line = lax.broadcasted_iota(jnp.int32, (groups * SUB * row_devices, 1), 0)
    row, rest = line % row_devices, line // row_devices
    paired = groups // 2 * 2
    pair, inside = rest // (2 * SUB), rest % (2 * SUB)
    of_pair = (2 * pair + inside % 2) * SUB + inside // 2
    place = jnp.where(rest < paired * SUB, of_pair, rest)
    lane = lax.broadcasted_iota(jnp.int32, (groups * SUB * row_devices, width), 1)
    return jnp.where(lane == row * rows + place, 1.0, 0.0).astype(BF16)


def stacked(low, high):
    return jnp.concatenate([low, high], axis=0).astype(BF16)


def triangle_kernel(direction, share, rows, cols, row_devices, col_devices, line, got_ref, sent_ref,
                    wide, left_ref, right_ref, even_ref, result_ref, packed):
    groups = rows // SUB
    pieces = SUB * cols // LANES
    total = row_devices * rows
    blocks = -(-total // LANES)
    pairs = -(-groups // 2)
    rest = total - (blocks - 1) * LANES
    tail = lax.broadcasted_iota(jnp.int32, (2 * SUB, LANES), 1) < rest
    place_step, row_step = wide_steps(col_devices * groups * pieces)
    pick = row_order(groups, row_devices, rows, blocks * LANES) if direction == 1 else None

    def spot(tile):
        device, number = divmod(tile, groups * pieces)
        col, row = divmod(device, row_devices)
        return row * row_step + col * groups * pieces + number

    def widen(pair):
        for unit in range(got_ref.shape[0] // (2 * SUB)):
            owners = [tile % (groups * pieces) // pieces // 2 for tile in (2 * unit, 2 * unit + 1)]
            if min(owners) != pair:
                continue
            both = got_ref[unit * 2 * SUB : (unit + 1) * 2 * SUB, :].astype(F32)
            for half in range(2):
                at = pl.ds(spot(2 * unit + half), SUB, stride=place_step)
                wide[at, :] = both[half * SUB : (half + 1) * SUB]

    def loaded(place, group, col, piece):
        start = place * place_step + (col * groups + group) * pieces + piece
        return wide[pl.ds(start, row_devices, stride=row_step), :]

    def spread(tiles, step, cleared):
        moves = [(col, step * cols, cols, col * cols) for col in range(col_devices)]
        registers = moved(lambda col, piece: tiles[col, piece], moves, blocks)
        if cleared:
            registers[-1] = jnp.where(tail, registers[-1], jnp.zeros_like(registers[-1]))
        return registers

    def put(target, spare, start, block, value):
        target[spare, start : start + 2 * SUB, block * LANES : (block + 1) * LANES] = value

    def put_even(spare, group, step, block, value):
        even_ref[spare, block, pl.ds(group * SUB + step, row_devices, stride=rows), :] = value

    def unpack(channel, only=range(pairs)):
        spare = channel % 2
        for pair in only:
            if 2 * pair + 1 < groups:
                unpack_pair(channel, spare, pair)
            else:
                unpack_last(channel, spare, 2 * pair)

    def unpack_pair(channel, spare, pair):
        for is_right, place in ((False, channel), (True, share + channel)):
            tiles = {}
            for col in range(col_devices):
                for piece in range(pieces):
                    tiles[col, piece] = stacked(
                        loaded(place, 2 * pair, col, piece), loaded(place, 2 * pair + 1, col, piece)
                    )
            for step in range(SUB):
                for block, register in enumerate(spread(tiles, step, direction == 0 and not is_right)):
                    if is_right and direction == 0:
                        both = register.astype(F32)
                        for half in range(2):
                            put_even(spare, 2 * pair + half, step, block, both[half * SUB : (half + 1) * SUB])
                    else:
                        target = right_ref if is_right else left_ref
                        put(target, spare, (pair * SUB + step) * 2 * SUB, block, register)

    def unpack_last(channel, spare, group):
        tiles = {}
        for col in range(col_devices):
            for piece in range(pieces):
                tiles[col, piece] = stacked(
                    loaded(channel, group, col, piece), loaded(share + channel, group, col, piece)
                )
        before = None
        for step in range(SUB):
            now = [register.astype(F32) for register in spread(tiles, step, direction == 0)]
            for block in range(blocks):
                if direction == 0:
                    put_even(spare, group, step, block, now[block][SUB:])
                if step % 2:
                    start = (group * SUB + step - 1) * SUB
                    put(left_ref, spare, start, block, stacked(before[block][:SUB], now[block][:SUB]))
                    if direction == 1:
                        put(right_ref, spare, start, block, stacked(before[block][SUB:], now[block][SUB:]))
            before = now

    def product(channel):
        spare = channel % 2
        if direction == 0:
            right = [even_ref[spare, block, 0:total].astype(BF16) for block in range(blocks)]
            right = jnp.concatenate(right, axis=1)
            summed = matmul(left_ref[spare], right, ((1,), (1,)))
        else:
            turned = matmul(pick, left_ref[spare], ((1,), (1,))).astype(BF16)
            summed = matmul(turned, right_ref[spare], ((1,), (0,)))
        for block in range(blocks):
            size = min(LANES, total - block * LANES)
            part = summed[:, block * LANES : block * LANES + size].astype(BF16)
            result_ref[channel, block, :, 0:size] = part

    def send(tiles, targets):
        for col in range(col_devices):
            moves = [(step, col * cols, cols, step * cols) for step in range(SUB)]
            registers = moved(lambda step, block: tiles[step, block], moves, pieces)
            for piece in range(pieces):
                both = registers[piece].astype(F32)
                for half, (channel, group) in enumerate(targets):
                    start = (col * row_devices * share + channel) * line + group * pieces + piece
                    packed[pl.ds(start, row_devices, stride=share * line), :] = (
                        both[half * SUB : (half + 1) * SUB]
                    )
        missing.difference_update(targets)

    missing = set((channel, group) for channel in range(share) for group in range(groups))
    waiting = list(range(sent_ref.shape[0] // (2 * SUB)))

    def finish():
        for unit in list(waiting):
            lines = range(unit * 2 * SUB, (unit + 1) * 2 * SUB)
            if any((at // line % share, at % line // pieces) in missing for at in lines):
                continue
            waiting.remove(unit)
            at = slice(unit * 2 * SUB, (unit + 1) * 2 * SUB)
            sent_ref[at, :] = packed[at, :].astype(BF16)

    def pack(channel):
        for pair in range(groups // 2):
            tiles = {}
            for step in range(SUB):
                for block in range(blocks):
                    start = (pair * SUB + step) * 2 * SUB
                    tiles[step, block] = result_ref[channel, block, start : start + 2 * SUB, :]
            send(tiles, [(channel, 2 * pair), (channel, 2 * pair + 1)])
        if groups % 2 and channel % 2:
            group = groups - 1
            tiles = {}
            for block in range(blocks):
                for step in range(0, SUB, 2):
                    start = (group * SUB + step) * SUB
                    low, high = [
                        result_ref[one, block, start : start + 2 * SUB, :].astype(F32)
                        for one in (channel - 1, channel)
                    ]
                    tiles[step, block] = stacked(low[:SUB], high[:SUB])
                    tiles[step + 1, block] = stacked(low[SUB:], high[SUB:])
            send(tiles, [(channel - 1, group), (channel, group)])

    widen(0)
    for pair in range(pairs):
        if pair + 1 < pairs:
            widen(pair + 1)
        unpack(0, [pair])
    for channel in range(share):
        product(channel)
        if channel > 0:
            pack(channel - 1)
        if channel + 1 < share:
            unpack(channel + 1)
        else:
            finish()
    pack(share - 1)
    finish()


def by_channels(pair, token_mask, chain_ids, chain_bias, in_weights, out_weights, row_devices, col_devices):
    rows, cols, width = pair.shape
    devices = row_devices * col_devices
    share = width // devices
    lanes = SUB * cols
    pieces = lanes // LANES
    groups = rows // SUB
    chunk = groups * pieces * SUB
    spots = rows * cols
    line = groups * pieces
    total = row_devices * rows
    blocks = -(-total // LANES)
    tall = groups * SUB * row_devices
    params = pltpu.CompilerParams(vmem_limit_bytes=40 * 1024 * 1024)
    whole = pl.BlockSpec(memory_space=pltpu.VMEM)
    far = pl.BlockSpec(memory_space=pltpu.HBM)

    sent_shape = jax.ShapeDtypeStruct((devices, groups, pieces * SUB, LANES), BF16)
    sum_shape = jax.ShapeDtypeStruct((devices * share * line, LANES), BF16)
    state_shape = jax.ShapeDtypeStruct((width, spots), F32)
    mask_shape = jax.ShapeDtypeStruct((1, spots), F32)
    padded_sum = pltpu.VMEM((-(-(devices + 1) * share * line // SUB) * SUB, LANES), F32)

    def exchange(array, rows):
        shape = (devices, rows) if rows % SUB == 0 else (devices, rows * 2 // SUB, SUB // 2)
        split = array.reshape(*shape, LANES)
        return lax.all_to_all(split, ("col", "row"), 0, 0, tiled=True).reshape(devices * rows, LANES)

    def triangle(direction, sent):
        wide_rows = (row_devices + 1) * wide_steps(col_devices * groups * pieces)[1]
        summed = pl.pallas_call(
            functools.partial(
                triangle_kernel, direction, share, rows, cols, row_devices, col_devices, line
            ),
            out_shape=sum_shape,
            in_specs=[whole],
            out_specs=whole,
            scratch_shapes=[
                pltpu.VMEM((-(-wide_rows // SUB) * SUB, LANES), F32),
                pltpu.VMEM((2, tall, blocks * LANES), BF16),
                pltpu.VMEM((2, tall, blocks * LANES), BF16),
                pltpu.VMEM((2, blocks, total + rows, LANES), F32),
                pltpu.VMEM((share, blocks, tall, LANES), BF16),
                padded_sum,
            ],
            compiler_params=params,
            name="triangle",
        )(exchange(sent, chunk))
        return exchange(summed, share * line)

    flat_pair = pair.reshape(spots, width)
    sent, gate, field, mask = pl.pallas_call(
        functools.partial(start_kernel, share, rows, cols),
        out_shape=[sent_shape, state_shape, state_shape, mask_shape],
        in_specs=[far] * 5,
        out_specs=[far] * 4,
        scratch_shapes=[
            pltpu.VMEM(sent_shape.shape, BF16),
            pltpu.VMEM(state_shape.shape, F32),
            pltpu.VMEM(state_shape.shape, F32),
            pltpu.VMEM(mask_shape.shape, F32),
            pltpu.VMEM((spots, width), BF16),
            pltpu.VMEM(in_weights.shape[1:], BF16),
            pltpu.VMEM((1, width), F32),
            pltpu.VMEM((1,) + token_mask.shape, jnp.int32),
            pltpu.VMEM((1,) + chain_ids.shape, jnp.int32),
            pltpu.SemaphoreType.DMA((8 + 2 * groups,)),
        ],
        compiler_params=pltpu.CompilerParams(vmem_limit_bytes=60 * 1024 * 1024),
        name="start",
    )(token_mask, chain_ids, flat_pair, chain_bias, in_weights)
    got = triangle(0, sent)
    sent, gate, field = pl.pallas_call(
        functools.partial(middle_kernel, share, rows, cols, line),
        out_shape=[sent_shape, state_shape, state_shape],
        in_specs=[whole] * 6,
        out_specs=[whole] * 3,
        scratch_shapes=[padded_sum],
        compiler_params=params,
        name="middle",
    )(mask, got, field, gate, out_weights, in_weights)
    got = triangle(1, sent)
    out = pl.pallas_call(
        functools.partial(end_kernel, rows, cols, line),
        out_shape=jax.ShapeDtypeStruct((spots, width), BF16),
        in_specs=[whole] * 4,
        out_specs=far,
        scratch_shapes=[
            padded_sum,
            pltpu.VMEM((spots, width), BF16),
            pltpu.SemaphoreType.DMA((groups,)),
        ],
        compiler_params=params,
        name="end",
    )(got, field, gate, out_weights)
    return out.reshape(pair.shape)


def gated_inputs(field, weights, pair_mask):
    width = weights.shape[0]
    normed = layer_norm(field).astype(BF16)
    projected = jnp.einsum("ijc,cd->ijd", normed, weights, preferred_element_type=F32)
    first = (
        jax.nn.sigmoid(projected[..., :width])
        * projected[..., width : 2 * width]
        * pair_mask[:, :, None]
    ).astype(BF16)
    second = (
        jax.nn.sigmoid(projected[..., 2 * width : 3 * width])
        * projected[..., 3 * width : 4 * width]
        * pair_mask[:, :, None]
    ).astype(BF16)
    gate_value = jax.nn.sigmoid(projected[..., 4 * width :])
    return (first, second, gate_value)


def update(field, summed, gate_value, weights):
    normed_sum = layer_norm(summed).astype(BF16)
    output = jnp.einsum("ijc,cd->ijd", normed_sum, weights, preferred_element_type=F32)
    return field + gate_value * output


def by_blocks(pair, token_mask, chain_ids, chain_bias, in_weights, out_weights):
    row_count = pair.shape[0]
    col_count = pair.shape[1]
    row_start = lax.axis_index("row") * row_count
    col_start = lax.axis_index("col") * col_count
    valid_rows = lax.dynamic_slice_in_dim(token_mask, row_start, row_count).astype(F32)
    valid_cols = lax.dynamic_slice_in_dim(token_mask, col_start, col_count).astype(F32)
    chain_rows = lax.dynamic_slice_in_dim(chain_ids, row_start, row_count)
    chain_cols = lax.dynamic_slice_in_dim(chain_ids, col_start, col_count)
    pair_mask = valid_rows[:, None] * valid_cols[None, :]
    same_chain = (chain_rows[:, None] == chain_cols[None, :]).astype(F32)
    field = pair.astype(F32) + same_chain[:, :, None] * chain_bias
    first, second, gate_value = gated_inputs(field, in_weights[0], pair_mask)
    second_rows = lax.all_gather(second, "row", axis=0, tiled=True)
    part = jnp.einsum("jkc,ikc->jic", second_rows, first, preferred_element_type=F32).astype(BF16)
    summed = lax.psum_scatter(part, "col", scatter_dimension=0, tiled=True).astype(F32)
    summed = jnp.transpose(summed, (1, 0, 2))
    field = update(field, summed, gate_value, out_weights[0])
    first, second, gate_value = gated_inputs(field, in_weights[1], pair_mask)
    first_cols = lax.all_gather(first, "col", axis=1, tiled=True)
    part = jnp.einsum("kic,kjc->ijc", first_cols, second, preferred_element_type=F32).astype(BF16)
    summed = lax.psum_scatter(part, "row", scatter_dimension=0, tiled=True).astype(F32)
    field = update(field, summed, gate_value, out_weights[1])
    return field.astype(BF16)


def solution(mesh):
    row_devices, col_devices = mesh.shape["row"], mesh.shape["col"]

    def per_device(pair, *rest):
        rows, cols, width = pair.shape
        devices = row_devices * col_devices
        fits = (
            width % devices == 0
            and 2 * (width // devices) == SUB
            and row_devices == SUB
            and rows % SUB == 0
            and rows >= 3 * SUB
            and (SUB * cols) % LANES == 0
            and max(rows, cols) <= LANES
        )
        if fits:
            return by_channels(pair, *rest, row_devices, col_devices)
        return by_blocks(pair, *rest)

    return jax.shard_map(
        per_device,
        mesh=mesh,
        in_specs=(P("row", "col", None), P(), P(), P(), P(), P()),
        out_specs=P("row", "col", None),
        check_vma=False,
    )
```

```python
import functools

import jax
import jax.numpy as jnp
from jax import lax
from jax.experimental import pallas as pl
from jax.experimental.pallas import tpu as pltpu
from jax.sharding import PartitionSpec as P

LANES = 128
SUB = 8
F32 = jnp.float32
BF16 = jnp.bfloat16


def layer_norm(values, axis=-1):
    center = values - jnp.mean(values, axis=axis, keepdims=True)
    spread = jnp.mean(center * center, axis=axis, keepdims=True)
    return center * lax.rsqrt(spread + 1e-05)


def matmul(left, right, dims):
    return lax.dot_general(left, right, (dims, ((), ())), preferred_element_type=F32)


def identity(size, scale):
    row = lax.broadcasted_iota(jnp.int32, (size, size), 0)
    col = lax.broadcasted_iota(jnp.int32, (size, size), 1)
    return jnp.where(row == col, scale, 0.0).astype(BF16)


def column(row_ref):
    width = row_ref.shape[1]
    return jnp.broadcast_to(row_ref[...], (width, width)).T[:, 0:1]


def transposed(weights, scale):
    eye = identity(weights.shape[1], scale)
    return matmul(eye, weights, ((1,), (1,))).astype(BF16)


def interleaved(first, second, share):
    width = first.shape[1]
    both = jnp.concatenate([first, second], axis=1)
    row = lax.broadcasted_iota(jnp.int32, (2 * width, 1), 0)
    col = lax.broadcasted_iota(jnp.int32, (2 * width, 2 * width), 1)
    owner, place = row // (2 * share), row % (2 * share)
    source = owner * share + place % share + jnp.where(place >= share, width, 0)
    pick = jnp.where(col == source, 0.5, 0.0).astype(BF16)
    return matmul(pick, both, ((1,), (1,))).astype(BF16)


def load_in_weights(weights, share):
    width = weights.shape[0]
    blocks = [weights[:, k * width : (k + 1) * width] for k in range(5)]
    return (
        interleaved(blocks[0], blocks[2], share),
        interleaved(blocks[1], blocks[3], share),
        transposed(blocks[4], 0.5),
    )


def token_vectors(tokens, row_start, col_start, rows, cols):
    groups = rows // SUB
    wide = tokens.shape[1]
    many = jnp.broadcast_to(tokens.astype(F32), (SUB, wide))
    lane = lax.broadcasted_iota(jnp.int32, (1, SUB * cols), 1)
    at_row = jnp.zeros_like(lane)
    for step in range(1, SUB):
        at_row = at_row + jnp.where(lane >= step * cols, 1, 0)
    at_col = lane - at_row * cols
    key = lax.broadcasted_iota(jnp.int32, (LANES, SUB * cols), 0)
    pick_row = jnp.where(key == at_row, 1.0, 0.0).astype(BF16)
    pick_col = jnp.where(key == at_col, 1.0, 0.0).astype(BF16)

    def window(start):
        return pltpu.roll(many, wide - start, 1)[:, :LANES]

    by_col = matmul(window(col_start).astype(BF16), pick_col, ((1,), (0,)))[0:1]
    windows = [window(row_start + group * SUB)[0:1] for group in range(groups)]
    windows.append(jnp.zeros((-groups % SUB, LANES), F32))
    by_row = matmul(jnp.concatenate(windows, axis=0).astype(BF16), pick_row, ((1,), (0,)))
    by_row = by_row.astype(jnp.int32)
    by_col = by_col.astype(jnp.int32)
    masks = (by_row & by_col & 1).astype(F32)
    sames = jnp.where((by_row >> 1) == (by_col >> 1), 1.0, 0.0)
    return masks, sames


def staged(count, stages):
    held = {}
    for step in range(count + len(stages) - 1):
        for number, stage in enumerate(stages):
            item = step - number
            if 0 <= item < count:
                held[item] = stage(item, held.get(item))


def projected(field, in_t):
    normed = layer_norm(field, 0).astype(BF16)
    return [matmul(weights, normed, ((1,), (0,))) for weights in in_t]


def gated(products, mask, group, share, sent_ref, gate_ref):
    gates, values, gate = products
    width, lanes = gate.shape
    sent = (jnp.tanh(gates) * values + values) * mask
    for owner in range(width // share):
        block = sent[owner * 2 * share : (owner + 1) * 2 * share]
        lines = [block[:, at : at + LANES] for at in range(0, lanes, LANES)]
        sent_ref[owner, group] = jnp.concatenate(lines, axis=0).astype(BF16)
    gate_ref[:, group * lanes : (group + 1) * lanes] = jnp.tanh(gate)


def start_kernel(share, rows, cols, valid_hbm, chain_hbm, pair_hbm, bias_hbm, w_hbm,
                 sent_ref, gate_ref, field_ref, mask_ref,
                 pair_ref, w_ref, bias_ref, valid_ref, chain_ref, sems):
    lanes = SUB * cols
    groups = rows // SUB
    width = pair_ref.shape[1]
    count = valid_hbm.shape[0]
    started = []

    def copy(near, far):
        started.append(pltpu.make_async_copy(near, far, sems.at[len(started)]))
        started[-1].start()

    copy(w_hbm.at[0], w_ref)
    copy(valid_hbm, valid_ref.at[0])
    copy(chain_hbm, chain_ref.at[0])
    copy(bias_hbm, bias_ref.at[0])
    for at in (pl.ds(0, 2 * lanes), pl.ds(2 * lanes, (groups - 2) * lanes)):
        copy(pair_hbm.at[at], pair_ref.at[at])
    arriving = len(started)
    eye = identity(width, 1.0)
    row_start = lax.axis_index("row") * rows
    col_start = lax.axis_index("col") * cols
    started[0].wait()
    in_t = load_in_weights(w_ref[...], share)
    for number in range(1, arriving - 1):
        started[number].wait()

    def lift(group):
        if group == 2:
            started[arriving - 1].wait()
        rows_of = pair_ref[group * lanes : (group + 1) * lanes, :]
        return matmul(eye, rows_of, ((1,), (1,)))

    lifted = {0: lift(0)}
    tokens = chain_ref[...] * 2 + valid_ref[...]
    tokens = jnp.concatenate([tokens, jnp.zeros((1, -count % LANES), jnp.int32)], axis=1)
    masks, sames = token_vectors(tokens, row_start, col_start, rows, cols)
    bias_col = column(bias_ref)

    def make_field(group, _):
        at = slice(group * lanes, (group + 1) * lanes)
        if group + 1 < groups:
            lifted[group + 1] = lift(group + 1)
        field = lifted.pop(group) + bias_col * sames[group : group + 1]
        field_ref[:, at] = field
        mask_ref[:, at] = masks[group : group + 1]
        return field

    def project(group, field):
        return projected(field, in_t)

    def finish(group, products):
        gated(products, masks[group : group + 1], group, share, sent_ref, gate_ref)

    staged(groups, (make_field, project, finish))


def output_of(wide, out_t, group, lanes, line):
    width = out_t.shape[1]
    pieces = lanes // LANES
    parts = []
    for piece in range(pieces):
        parts.append(wide[pl.ds(group * pieces + piece, width, stride=line), :])
    normed = layer_norm(jnp.concatenate(parts, axis=1), 0).astype(BF16)
    return matmul(out_t, normed, ((1,), (0,)))


def middle_kernel(share, rows, cols, line, mask_ref, got_ref, field_in, gate_in, wo_ref, w_ref,
                  sent_ref, gate_ref, field_ref, wide):
    lanes = SUB * cols
    count = got_ref.shape[0]
    half = count // 2
    wide[:half, :] = got_ref[:half, :].astype(F32)
    out_t = transposed(wo_ref[0], 0.5)
    wide[half:count, :] = got_ref[half:, :].astype(F32)
    in_t = load_in_weights(w_ref[1], share)

    def span(group):
        return slice(group * lanes, (group + 1) * lanes)

    def outgoing(group, _):
        return output_of(wide, out_t, group, lanes, line)

    def project(group, output):
        at = span(group)
        field = field_in[:, at] + (gate_in[:, at] * output + output)
        field_ref[:, at] = field
        return projected(field, in_t)

    def finish(group, products):
        gated(products, mask_ref[:, span(group)], group, share, sent_ref, gate_ref)

    staged(rows // SUB, (outgoing, project, finish))


def end_kernel(rows, cols, line, got_ref, field_in, gate_in, wo_ref, out_hbm, wide, out_ref, sems):
    lanes = SUB * cols
    out_t = transposed(wo_ref[1], 0.5)
    wide[: got_ref.shape[0], :] = got_ref[...].astype(F32)
    copies = []

    def outgoing(group, _):
        return output_of(wide, out_t, group, lanes, line)

    def finish(group, output):
        at = slice(group * lanes, (group + 1) * lanes)
        field = field_in[:, at] + (gate_in[:, at] * output + output)
        out_ref[at, :] = field.astype(BF16).T
        at = pl.ds(group * lanes, lanes)
        copies.append(pltpu.make_async_copy(out_ref.at[at], out_hbm.at[at], sems.at[group]))
        copies[-1].start()

    staged(rows // SUB, (outgoing, finish))
    for copy in copies:
        copy.wait()


def moved(source, moves, count):
    shape = None
    lane = None
    targets = [[] for _ in range(count)]
    for row, begin, length, target in moves:
        shift = (target - begin) % LANES
        while length > 0:
            size = min(length, LANES - begin % LANES, LANES - target % LANES)
            targets[target // LANES].append((target % LANES, row, begin // LANES, shift))
            begin, target, length = begin + size, target + size, length - size
    rolled = {}
    registers = []
    for pieces in targets:
        value = None
        for start, row, register, shift in sorted(pieces, key=lambda piece: piece[0]):
            key = (row, register, shift)
            if key not in rolled:
                tile = source(row, register)
                rolled[key] = pltpu.roll(tile, shift, 1) if shift else tile
            if value is None:
                value = rolled[key]
            else:
                if lane is None:
                    shape = value.shape
                    lane = lax.broadcasted_iota(jnp.int32, shape, 1)
                value = jnp.where(lane < start, value, rolled[key])
        registers.append(value)
    return registers


def wide_steps(tiles):
    place_step = tiles + 1 - tiles % 2
    return place_step, SUB * place_step + 1


def row_order(groups, row_devices, rows, width):
    line = lax.broadcasted_iota(jnp.int32, (groups * SUB * row_devices, 1), 0)
    row, rest = line % row_devices, line // row_devices
    paired = groups // 2 * 2
    pair, inside = rest // (2 * SUB), rest % (2 * SUB)
    of_pair = (2 * pair + inside % 2) * SUB + inside // 2
    place = jnp.where(rest < paired * SUB, of_pair, rest)
    lane = lax.broadcasted_iota(jnp.int32, (groups * SUB * row_devices, width), 1)
    return jnp.where(lane == row * rows + place, 1.0, 0.0).astype(BF16)


def stacked(low, high):
    return jnp.concatenate([low, high], axis=0).astype(BF16)


def triangle_kernel(direction, share, rows, cols, row_devices, col_devices, line, got_ref, sent_ref,
                    wide, left_ref, right_ref, even_ref, result_ref, packed):
    groups = rows // SUB
    pieces = SUB * cols // LANES
    total = row_devices * rows
    blocks = -(-total // LANES)
    pairs = -(-groups // 2)
    rest = total - (blocks - 1) * LANES
    tail = lax.broadcasted_iota(jnp.int32, (2 * SUB, LANES), 1) < rest
    place_step, row_step = wide_steps(col_devices * groups * pieces)
    pick = row_order(groups, row_devices, rows, blocks * LANES) if direction == 1 else None

    def spot(tile):
        device, number = divmod(tile, groups * pieces)
        col, row = divmod(device, row_devices)
        return row * row_step + col * groups * pieces + number

    def widen(pair):
        for unit in range(got_ref.shape[0] // (2 * SUB)):
            owners = [tile % (groups * pieces) // pieces // 2 for tile in (2 * unit, 2 * unit + 1)]
            if min(owners) != pair:
                continue
            both = got_ref[unit * 2 * SUB : (unit + 1) * 2 * SUB, :].astype(F32)
            for half in range(2):
                at = pl.ds(spot(2 * unit + half), SUB, stride=place_step)
                wide[at, :] = both[half * SUB : (half + 1) * SUB]

    def loaded(place, group, col, piece):
        start = place * place_step + (col * groups + group) * pieces + piece
        return wide[pl.ds(start, row_devices, stride=row_step), :]

    def spread(tiles, step, cleared):
        moves = [(col, step * cols, cols, col * cols) for col in range(col_devices)]
        registers = moved(lambda col, piece: tiles[col, piece], moves, blocks)
        if cleared:
            registers[-1] = jnp.where(tail, registers[-1], jnp.zeros_like(registers[-1]))
        return registers

    def put(target, spare, start, block, value):
        target[spare, start : start + 2 * SUB, block * LANES : (block + 1) * LANES] = value

    def put_even(spare, group, step, block, value):
        even_ref[spare, block, pl.ds(group * SUB + step, row_devices, stride=rows), :] = value

    def unpack(channel, only=range(pairs)):
        spare = channel % 2
        for pair in only:
            if 2 * pair + 1 < groups:
                unpack_pair(channel, spare, pair)
            else:
                unpack_last(channel, spare, 2 * pair)

    def unpack_pair(channel, spare, pair):
        for is_right, place in ((False, channel), (True, share + channel)):
            tiles = {}
            for col in range(col_devices):
                for piece in range(pieces):
                    tiles[col, piece] = stacked(
                        loaded(place, 2 * pair, col, piece), loaded(place, 2 * pair + 1, col, piece)
                    )
            for step in range(SUB):
                for block, register in enumerate(spread(tiles, step, direction == 0 and not is_right)):
                    if is_right and direction == 0:
                        both = register.astype(F32)
                        for half in range(2):
                            put_even(spare, 2 * pair + half, step, block, both[half * SUB : (half + 1) * SUB])
                    else:
                        target = right_ref if is_right else left_ref
                        put(target, spare, (pair * SUB + step) * 2 * SUB, block, register)

    def unpack_last(channel, spare, group):
        tiles = {}
        for col in range(col_devices):
            for piece in range(pieces):
                tiles[col, piece] = stacked(
                    loaded(channel, group, col, piece), loaded(share + channel, group, col, piece)
                )
        before = None
        for step in range(SUB):
            now = [register.astype(F32) for register in spread(tiles, step, direction == 0)]
            for block in range(blocks):
                if direction == 0:
                    put_even(spare, group, step, block, now[block][SUB:])
                if step % 2:
                    start = (group * SUB + step - 1) * SUB
                    put(left_ref, spare, start, block, stacked(before[block][:SUB], now[block][:SUB]))
                    if direction == 1:
                        put(right_ref, spare, start, block, stacked(before[block][SUB:], now[block][SUB:]))
            before = now

    def product(channel):
        spare = channel % 2
        if direction == 0:
            right = [even_ref[spare, block, 0:total].astype(BF16) for block in range(blocks)]
            right = jnp.concatenate(right, axis=1)
            summed = matmul(left_ref[spare], right, ((1,), (1,)))
        else:
            turned = matmul(pick, left_ref[spare], ((1,), (1,))).astype(BF16)
            summed = matmul(turned, right_ref[spare], ((1,), (0,)))
        for block in range(blocks):
            size = min(LANES, total - block * LANES)
            part = summed[:, block * LANES : block * LANES + size].astype(BF16)
            result_ref[channel, block, :, 0:size] = part

    def send(tiles, targets):
        for col in range(col_devices):
            moves = [(step, col * cols, cols, step * cols) for step in range(SUB)]
            registers = moved(lambda step, block: tiles[step, block], moves, pieces)
            for piece in range(pieces):
                both = registers[piece].astype(F32)
                for half, (channel, group) in enumerate(targets):
                    start = (col * row_devices * share + channel) * line + group * pieces + piece
                    packed[pl.ds(start, row_devices, stride=share * line), :] = (
                        both[half * SUB : (half + 1) * SUB]
                    )
        missing.difference_update(targets)

    missing = set((channel, group) for channel in range(share) for group in range(groups))
    waiting = list(range(sent_ref.shape[0] // (2 * SUB)))

    def finish():
        for unit in list(waiting):
            lines = range(unit * 2 * SUB, (unit + 1) * 2 * SUB)
            if any((at // line % share, at % line // pieces) in missing for at in lines):
                continue
            waiting.remove(unit)
            at = slice(unit * 2 * SUB, (unit + 1) * 2 * SUB)
            sent_ref[at, :] = packed[at, :].astype(BF16)

    def pack(channel):
        for pair in range(groups // 2):
            tiles = {}
            for step in range(SUB):
                for block in range(blocks):
                    start = (pair * SUB + step) * 2 * SUB
                    tiles[step, block] = result_ref[channel, block, start : start + 2 * SUB, :]
            send(tiles, [(channel, 2 * pair), (channel, 2 * pair + 1)])
        if groups % 2 and channel % 2:
            group = groups - 1
            tiles = {}
            for block in range(blocks):
                for step in range(0, SUB, 2):
                    start = (group * SUB + step) * SUB
                    low, high = [
                        result_ref[one, block, start : start + 2 * SUB, :].astype(F32)
                        for one in (channel - 1, channel)
                    ]
                    tiles[step, block] = stacked(low[:SUB], high[:SUB])
                    tiles[step + 1, block] = stacked(low[SUB:], high[SUB:])
            send(tiles, [(channel - 1, group), (channel, group)])

    widen(0)
    for pair in range(pairs):
        if pair + 1 < pairs:
            widen(pair + 1)
        unpack(0, [pair])
    for channel in range(share):
        product(channel)
        if channel > 0:
            pack(channel - 1)
        if channel + 1 < share:
            unpack(channel + 1)
        else:
            finish()
    pack(share - 1)
    finish()


def by_channels(pair, token_mask, chain_ids, chain_bias, in_weights, out_weights, row_devices, col_devices):
    rows, cols, width = pair.shape
    devices = row_devices * col_devices
    share = width // devices
    lanes = SUB * cols
    pieces = lanes // LANES
    groups = rows // SUB
    chunk = groups * pieces * SUB
    spots = rows * cols
    line = groups * pieces
    total = row_devices * rows
    blocks = -(-total // LANES)
    tall = groups * SUB * row_devices
    params = pltpu.CompilerParams(vmem_limit_bytes=40 * 1024 * 1024)
    whole = pl.BlockSpec(memory_space=pltpu.VMEM)
    far = pl.BlockSpec(memory_space=pltpu.HBM)

    sent_shape = jax.ShapeDtypeStruct((devices, groups, pieces * SUB, LANES), BF16)
    sum_shape = jax.ShapeDtypeStruct((devices * share * line, LANES), BF16)
    state_shape = jax.ShapeDtypeStruct((width, spots), F32)
    mask_shape = jax.ShapeDtypeStruct((1, spots), F32)
    padded_sum = pltpu.VMEM((-(-(devices + 1) * share * line // SUB) * SUB, LANES), F32)

    def exchange(array, rows):
        shape = (devices, rows) if rows % SUB == 0 else (devices, rows * 2 // SUB, SUB // 2)
        split = array.reshape(*shape, LANES)
        return lax.all_to_all(split, ("col", "row"), 0, 0, tiled=True).reshape(devices * rows, LANES)

    def triangle(direction, sent):
        wide_rows = (row_devices + 1) * wide_steps(col_devices * groups * pieces)[1]
        summed = pl.pallas_call(
            functools.partial(
                triangle_kernel, direction, share, rows, cols, row_devices, col_devices, line
            ),
            out_shape=sum_shape,
            in_specs=[whole],
            out_specs=whole,
            scratch_shapes=[
                pltpu.VMEM((-(-wide_rows // SUB) * SUB, LANES), F32),
                pltpu.VMEM((2, tall, blocks * LANES), BF16),
                pltpu.VMEM((2, tall, blocks * LANES), BF16),
                pltpu.VMEM((2, blocks, total + rows, LANES), F32),
                pltpu.VMEM((share, blocks, tall, LANES), BF16),
                padded_sum,
            ],
            compiler_params=params,
            name="triangle",
        )(exchange(sent, chunk))
        return exchange(summed, share * line)

    flat_pair = pair.reshape(spots, width)
    sent, gate, field, mask = pl.pallas_call(
        functools.partial(start_kernel, share, rows, cols),
        out_shape=[sent_shape, state_shape, state_shape, mask_shape],
        in_specs=[far] * 5,
        out_specs=[whole] * 4,
        scratch_shapes=[
            pltpu.VMEM((spots, width), BF16),
            pltpu.VMEM(in_weights.shape[1:], BF16),
            pltpu.VMEM((1, width), F32),
            pltpu.VMEM((1,) + token_mask.shape, jnp.int32),
            pltpu.VMEM((1,) + chain_ids.shape, jnp.int32),
            pltpu.SemaphoreType.DMA((6,)),
        ],
        compiler_params=params,
        name="start",
    )(*[
        pltpu.with_memory_space_constraint(array, pltpu.HBM)
        for array in (token_mask, chain_ids, flat_pair, chain_bias, in_weights)
    ])
    got = triangle(0, sent)
    sent, gate, field = pl.pallas_call(
        functools.partial(middle_kernel, share, rows, cols, line),
        out_shape=[sent_shape, state_shape, state_shape],
        in_specs=[whole] * 6,
        out_specs=[whole] * 3,
        scratch_shapes=[padded_sum],
        compiler_params=params,
        name="middle",
    )(mask, got, field, gate, out_weights, in_weights)
    got = triangle(1, sent)
    out = pl.pallas_call(
        functools.partial(end_kernel, rows, cols, line),
        out_shape=jax.ShapeDtypeStruct((spots, width), BF16),
        in_specs=[whole] * 4,
        out_specs=far,
        scratch_shapes=[
            padded_sum,
            pltpu.VMEM((spots, width), BF16),
            pltpu.SemaphoreType.DMA((groups,)),
        ],
        compiler_params=params,
        name="end",
    )(got, field, gate, out_weights)
    return out.reshape(pair.shape)


def gated_inputs(field, weights, pair_mask):
    width = weights.shape[0]
    normed = layer_norm(field).astype(BF16)
    projected = jnp.einsum("ijc,cd->ijd", normed, weights, preferred_element_type=F32)
    first = (
        jax.nn.sigmoid(projected[..., :width])
        * projected[..., width : 2 * width]
        * pair_mask[:, :, None]
    ).astype(BF16)
    second = (
        jax.nn.sigmoid(projected[..., 2 * width : 3 * width])
        * projected[..., 3 * width : 4 * width]
        * pair_mask[:, :, None]
    ).astype(BF16)
    gate_value = jax.nn.sigmoid(projected[..., 4 * width :])
    return (first, second, gate_value)


def update(field, summed, gate_value, weights):
    normed_sum = layer_norm(summed).astype(BF16)
    output = jnp.einsum("ijc,cd->ijd", normed_sum, weights, preferred_element_type=F32)
    return field + gate_value * output


def by_blocks(pair, token_mask, chain_ids, chain_bias, in_weights, out_weights):
    row_count = pair.shape[0]
    col_count = pair.shape[1]
    row_start = lax.axis_index("row") * row_count
    col_start = lax.axis_index("col") * col_count
    valid_rows = lax.dynamic_slice_in_dim(token_mask, row_start, row_count).astype(F32)
    valid_cols = lax.dynamic_slice_in_dim(token_mask, col_start, col_count).astype(F32)
    chain_rows = lax.dynamic_slice_in_dim(chain_ids, row_start, row_count)
    chain_cols = lax.dynamic_slice_in_dim(chain_ids, col_start, col_count)
    pair_mask = valid_rows[:, None] * valid_cols[None, :]
    same_chain = (chain_rows[:, None] == chain_cols[None, :]).astype(F32)
    field = pair.astype(F32) + same_chain[:, :, None] * chain_bias
    first, second, gate_value = gated_inputs(field, in_weights[0], pair_mask)
    second_rows = lax.all_gather(second, "row", axis=0, tiled=True)
    part = jnp.einsum("jkc,ikc->jic", second_rows, first, preferred_element_type=F32).astype(BF16)
    summed = lax.psum_scatter(part, "col", scatter_dimension=0, tiled=True).astype(F32)
    summed = jnp.transpose(summed, (1, 0, 2))
    field = update(field, summed, gate_value, out_weights[0])
    first, second, gate_value = gated_inputs(field, in_weights[1], pair_mask)
    first_cols = lax.all_gather(first, "col", axis=1, tiled=True)
    part = jnp.einsum("kic,kjc->ijc", first_cols, second, preferred_element_type=F32).astype(BF16)
    summed = lax.psum_scatter(part, "row", scatter_dimension=0, tiled=True).astype(F32)
    field = update(field, summed, gate_value, out_weights[1])
    return field.astype(BF16)


def solution(mesh):
    row_devices, col_devices = mesh.shape["row"], mesh.shape["col"]

    def per_device(pair, *rest):
        rows, cols, width = pair.shape
        devices = row_devices * col_devices
        fits = (
            width % devices == 0
            and 2 * (width // devices) == SUB
            and row_devices == SUB
            and rows % SUB == 0
            and rows >= 3 * SUB
            and (SUB * cols) % LANES == 0
            and max(rows, cols) <= LANES
        )
        if fits:
            return by_channels(pair, *rest, row_devices, col_devices)
        return by_blocks(pair, *rest)

    return jax.shard_map(
        per_device,
        mesh=mesh,
        in_specs=(P("row", "col", None), P(), P(), P(), P(), P()),
        out_specs=P("row", "col", None),
        check_vma=False,
    )
```

```python
import functools

import jax
import jax.numpy as jnp
from jax import lax
from jax.experimental import pallas as pl
from jax.experimental.pallas import tpu as pltpu
from jax.sharding import PartitionSpec as P

LANES = 128
SUB = 8
SPAN = 256
F32 = jnp.float32
BF16 = jnp.bfloat16


def layer_norm(values, axis=-1):
    center = values - jnp.mean(values, axis=axis, keepdims=True)
    spread = jnp.mean(center * center, axis=axis, keepdims=True)
    return center * lax.rsqrt(spread + 1e-05)


def matmul(left, right, dims):
    return lax.dot_general(left, right, (dims, ((), ())), preferred_element_type=F32)


def identity(size, scale):
    row = lax.broadcasted_iota(jnp.int32, (size, size), 0)
    col = lax.broadcasted_iota(jnp.int32, (size, size), 1)
    return jnp.where(row == col, scale, 0.0).astype(BF16)


def column(row_ref):
    width = row_ref.shape[1]
    return jnp.broadcast_to(row_ref[...], (width, width)).T[:, 0:1]


def transposed(weights, scale):
    eye = identity(weights.shape[1], scale)
    return matmul(eye, weights, ((1,), (1,))).astype(BF16)


def interleaved(first, second, share):
    width = first.shape[1]
    both = jnp.concatenate([first, second], axis=1)
    row = lax.broadcasted_iota(jnp.int32, (2 * width, 1), 0)
    col = lax.broadcasted_iota(jnp.int32, (2 * width, 2 * width), 1)
    owner, place = row // (2 * share), row % (2 * share)
    source = owner * share + place % share + jnp.where(place >= share, width, 0)
    pick = jnp.where(col == source, 0.5, 0.0).astype(BF16)
    return matmul(pick, both, ((1,), (1,))).astype(BF16)


def load_in_weights(weights, share):
    width = weights.shape[0]
    blocks = [weights[:, k * width : (k + 1) * width] for k in range(5)]
    return (
        interleaved(blocks[0], blocks[2], share),
        interleaved(blocks[1], blocks[3], share),
        transposed(blocks[4], 0.5),
    )


def token_vectors(tokens, row_start, col_start, rows, cols):
    groups = rows // SUB
    wide = tokens.shape[1]
    many = jnp.broadcast_to(tokens.astype(F32), (SUB, wide))
    lane = lax.broadcasted_iota(jnp.int32, (1, SUB * cols), 1)
    at_row = jnp.zeros_like(lane)
    for step in range(1, SUB):
        at_row = at_row + jnp.where(lane >= step * cols, 1, 0)
    at_col = lane - at_row * cols
    key = lax.broadcasted_iota(jnp.int32, (LANES, SUB * cols), 0)
    pick_row = jnp.where(key == at_row, 1.0, 0.0).astype(BF16)
    pick_col = jnp.where(key == at_col, 1.0, 0.0).astype(BF16)

    def window(start):
        return pltpu.roll(many, wide - start, 1)[:, :LANES]

    by_col = matmul(window(col_start).astype(BF16), pick_col, ((1,), (0,)))[0:1]
    windows = [window(row_start + group * SUB)[0:1] for group in range(groups)]
    windows.append(jnp.zeros((-groups % SUB, LANES), F32))
    by_row = matmul(jnp.concatenate(windows, axis=0).astype(BF16), pick_row, ((1,), (0,)))
    by_row = by_row.astype(jnp.int32)
    by_col = by_col.astype(jnp.int32)
    masks = (by_row & by_col & 1).astype(F32)
    sames = jnp.where((by_row >> 1) == (by_col >> 1), 1.0, 0.0)
    return masks, sames


def staged(count, stages):
    held = {}
    for step in range(count + len(stages) - 1):
        for number, stage in enumerate(stages):
            item = step - number
            if 0 <= item < count:
                held[item] = stage(item, held.get(item))


def spans(total):
    return [slice(at, min(at + SPAN, total)) for at in range(0, total, SPAN)]


def projected(field, in_t):
    normed = layer_norm(field, 0).astype(BF16)
    return [matmul(weights, normed, ((1,), (0,))) for weights in in_t]


def gated(products, mask, at, share, sent_ref, gate_ref):
    gates, values, gate = products
    width, lanes = gate.shape
    sent = (jnp.tanh(gates) * values + values) * mask
    lines = slice(at.start // LANES * SUB, at.stop // LANES * SUB)
    for owner in range(width // share):
        block = sent[owner * 2 * share : (owner + 1) * 2 * share]
        tiles = [block[:, lane : lane + LANES] for lane in range(0, lanes, LANES)]
        sent_ref[owner, lines, :] = jnp.concatenate(tiles, axis=0).astype(BF16)
    gate_ref[:, at] = jnp.tanh(gate)


def start_kernel(share, rows, cols, valid_hbm, chain_hbm, pair_hbm, bias_hbm, w_hbm,
                 sent_ref, gate_ref, field_ref, mask_ref,
                 same_ref, pair_ref, w_ref, bias_ref, valid_ref, chain_ref, sems):
    lanes = SUB * cols
    groups = rows // SUB
    spots, width = pair_ref.shape
    count = valid_hbm.shape[0]
    ranges = spans(spots)
    first = ranges[len(ranges) // 3].start
    started = []

    def copy(near, far):
        started.append(pltpu.make_async_copy(near, far, sems.at[len(started)]))
        started[-1].start()

    copy(w_hbm.at[0], w_ref)
    copy(valid_hbm, valid_ref.at[0])
    copy(chain_hbm, chain_ref.at[0])
    copy(bias_hbm, bias_ref.at[0])
    for at in (pl.ds(0, first), pl.ds(first, spots - first)):
        copy(pair_hbm.at[at], pair_ref.at[at])
    eye = identity(width, 1.0)
    row_start = lax.axis_index("row") * rows
    col_start = lax.axis_index("col") * cols
    started[0].wait()
    in_t = load_in_weights(w_ref[...], share)
    for number in range(1, len(started) - 1):
        started[number].wait()

    def lift(item):
        if ranges[item].start == first:
            started[-1].wait()
        return matmul(eye, pair_ref[ranges[item], :], ((1,), (1,)))

    lifted = {0: lift(0)}
    tokens = chain_ref[...] * 2 + valid_ref[...]
    tokens = jnp.concatenate([tokens, jnp.zeros((1, -count % LANES), jnp.int32)], axis=1)
    masks, sames = token_vectors(tokens, row_start, col_start, rows, cols)
    for group in range(groups):
        at = slice(group * lanes, (group + 1) * lanes)
        mask_ref[:, at] = masks[group : group + 1]
        same_ref[:, at] = sames[group : group + 1]
    bias_col = column(bias_ref)

    def make_field(item, _):
        if item + 1 < len(ranges):
            lifted[item + 1] = lift(item + 1)
        field = lifted.pop(item) + bias_col * same_ref[:, ranges[item]]
        field_ref[:, ranges[item]] = field
        return field

    def project(item, field):
        return projected(field, in_t)

    def finish(item, products):
        at = ranges[item]
        gated(products, mask_ref[:, at], at, share, sent_ref, gate_ref)

    staged(len(ranges), (make_field, project, finish))


def output_of(wide, out_t, at, line):
    width = out_t.shape[1]
    parts = []
    for piece in range(at.start // LANES, at.stop // LANES):
        parts.append(wide[pl.ds(piece, width, stride=line), :])
    normed = layer_norm(jnp.concatenate(parts, axis=1), 0).astype(BF16)
    return matmul(out_t, normed, ((1,), (0,)))


def middle_kernel(share, line, mask_ref, got_ref, field_in, gate_in, wo_ref, w_ref,
                  sent_ref, gate_ref, field_ref, wide):
    ranges = spans(field_in.shape[1])
    count = got_ref.shape[0]
    half = count // 2
    wide[:half, :] = got_ref[:half, :].astype(F32)
    out_t = transposed(wo_ref[0], 0.5)
    wide[half:count, :] = got_ref[half:, :].astype(F32)
    in_t = load_in_weights(w_ref[1], share)

    def outgoing(item, _):
        return output_of(wide, out_t, ranges[item], line)

    def project(item, output):
        at = ranges[item]
        field = field_in[:, at] + (gate_in[:, at] * output + output)
        field_ref[:, at] = field
        return projected(field, in_t)

    def finish(item, products):
        at = ranges[item]
        gated(products, mask_ref[:, at], at, share, sent_ref, gate_ref)

    staged(len(ranges), (outgoing, project, finish))


def end_kernel(line, got_ref, field_in, gate_in, wo_ref, out_hbm, wide, out_ref, sems):
    ranges = spans(field_in.shape[1])
    out_t = transposed(wo_ref[1], 0.5)
    wide[: got_ref.shape[0], :] = got_ref[...].astype(F32)
    copies = []
    done = [0]

    def outgoing(item, _):
        return output_of(wide, out_t, ranges[item], line)

    def finish(item, output):
        at = ranges[item]
        field = field_in[:, at] + (gate_in[:, at] * output + output)
        out_ref[at, :] = field.astype(BF16).T
        if item % 3 == 0 or item == len(ranges) - 1:
            rows = pl.ds(done[0], at.stop - done[0])
            done[0] = at.stop
            copies.append(pltpu.make_async_copy(out_ref.at[rows], out_hbm.at[rows], sems.at[len(copies)]))
            copies[-1].start()

    staged(len(ranges), (outgoing, finish))
    for copy in copies:
        copy.wait()


def moved(source, moves, count):
    shape = None
    lane = None
    targets = [[] for _ in range(count)]
    for row, begin, length, target in moves:
        shift = (target - begin) % LANES
        while length > 0:
            size = min(length, LANES - begin % LANES, LANES - target % LANES)
            targets[target // LANES].append((target % LANES, row, begin // LANES, shift))
            begin, target, length = begin + size, target + size, length - size
    rolled = {}
    registers = []
    for pieces in targets:
        value = None
        for start, row, register, shift in sorted(pieces, key=lambda piece: piece[0]):
            key = (row, register, shift)
            if key not in rolled:
                tile = source(row, register)
                rolled[key] = pltpu.roll(tile, shift, 1) if shift else tile
            if value is None:
                value = rolled[key]
            else:
                if lane is None:
                    shape = value.shape
                    lane = lax.broadcasted_iota(jnp.int32, shape, 1)
                value = jnp.where(lane < start, value, rolled[key])
        registers.append(value)
    return registers


def wide_steps(tiles):
    place_step = tiles + 1 - tiles % 2
    return place_step, SUB * place_step + 1


def row_order(groups, row_devices, rows, width):
    line = lax.broadcasted_iota(jnp.int32, (groups * SUB * row_devices, 1), 0)
    row, rest = line % row_devices, line // row_devices
    paired = groups // 2 * 2
    pair, inside = rest // (2 * SUB), rest % (2 * SUB)
    of_pair = (2 * pair + inside % 2) * SUB + inside // 2
    place = jnp.where(rest < paired * SUB, of_pair, rest)
    lane = lax.broadcasted_iota(jnp.int32, (groups * SUB * row_devices, width), 1)
    return jnp.where(lane == row * rows + place, 1.0, 0.0).astype(BF16)


def stacked(low, high):
    return jnp.concatenate([low, high], axis=0).astype(BF16)


def triangle_kernel(direction, share, rows, cols, row_devices, col_devices, line, got_ref, sent_ref,
                    wide, left_ref, right_ref, even_ref, result_ref, packed):
    groups = rows // SUB
    pieces = SUB * cols // LANES
    total = row_devices * rows
    blocks = -(-total // LANES)
    pairs = -(-groups // 2)
    rest = total - (blocks - 1) * LANES
    tail = lax.broadcasted_iota(jnp.int32, (2 * SUB, LANES), 1) < rest
    place_step, row_step = wide_steps(col_devices * groups * pieces)
    pick = row_order(groups, row_devices, rows, blocks * LANES) if direction == 1 else None

    def spot(tile):
        device, number = divmod(tile, groups * pieces)
        col, row = divmod(device, row_devices)
        return row * row_step + col * groups * pieces + number

    def widen(pair):
        for unit in range(got_ref.shape[0] // (2 * SUB)):
            owners = [tile % (groups * pieces) // pieces // 2 for tile in (2 * unit, 2 * unit + 1)]
            if min(owners) != pair:
                continue
            both = got_ref[unit * 2 * SUB : (unit + 1) * 2 * SUB, :].astype(F32)
            for half in range(2):
                at = pl.ds(spot(2 * unit + half), SUB, stride=place_step)
                wide[at, :] = both[half * SUB : (half + 1) * SUB]

    def loaded(place, group, col, piece):
        start = place * place_step + (col * groups + group) * pieces + piece
        return wide[pl.ds(start, row_devices, stride=row_step), :]

    def spread(tiles, step, cleared):
        moves = [(col, step * cols, cols, col * cols) for col in range(col_devices)]
        registers = moved(lambda col, piece: tiles[col, piece], moves, blocks)
        if cleared:
            registers[-1] = jnp.where(tail, registers[-1], jnp.zeros_like(registers[-1]))
        return registers

    def put(target, spare, start, block, value):
        target[spare, start : start + 2 * SUB, block * LANES : (block + 1) * LANES] = value

    def put_even(spare, group, step, block, value):
        even_ref[spare, block, pl.ds(group * SUB + step, row_devices, stride=rows), :] = value

    def unpack(channel, only=range(pairs)):
        spare = channel % 2
        for pair in only:
            if 2 * pair + 1 < groups:
                unpack_pair(channel, spare, pair)
            else:
                unpack_last(channel, spare, 2 * pair)

    def unpack_pair(channel, spare, pair):
        for is_right, place in ((False, channel), (True, share + channel)):
            tiles = {}
            for col in range(col_devices):
                for piece in range(pieces):
                    tiles[col, piece] = stacked(
                        loaded(place, 2 * pair, col, piece), loaded(place, 2 * pair + 1, col, piece)
                    )
            for step in range(SUB):
                for block, register in enumerate(spread(tiles, step, direction == 0 and not is_right)):
                    if is_right and direction == 0:
                        both = register.astype(F32)
                        for half in range(2):
                            put_even(spare, 2 * pair + half, step, block, both[half * SUB : (half + 1) * SUB])
                    else:
                        target = right_ref if is_right else left_ref
                        put(target, spare, (pair * SUB + step) * 2 * SUB, block, register)

    def unpack_last(channel, spare, group):
        tiles = {}
        for col in range(col_devices):
            for piece in range(pieces):
                tiles[col, piece] = stacked(
                    loaded(channel, group, col, piece), loaded(share + channel, group, col, piece)
                )
        before = None
        for step in range(SUB):
            now = [register.astype(F32) for register in spread(tiles, step, direction == 0)]
            for block in range(blocks):
                if direction == 0:
                    put_even(spare, group, step, block, now[block][SUB:])
                if step % 2:
                    start = (group * SUB + step - 1) * SUB
                    put(left_ref, spare, start, block, stacked(before[block][:SUB], now[block][:SUB]))
                    if direction == 1:
                        put(right_ref, spare, start, block, stacked(before[block][SUB:], now[block][SUB:]))
            before = now

    def product(channel):
        spare = channel % 2
        if direction == 0:
            right = [even_ref[spare, block, 0:total].astype(BF16) for block in range(blocks)]
            right = jnp.concatenate(right, axis=1)
            summed = matmul(left_ref[spare], right, ((1,), (1,)))
        else:
            turned = matmul(pick, left_ref[spare], ((1,), (1,))).astype(BF16)
            summed = matmul(turned, right_ref[spare], ((1,), (0,)))
        for block in range(blocks):
            size = min(LANES, total - block * LANES)
            part = summed[:, block * LANES : block * LANES + size].astype(BF16)
            result_ref[channel, block, :, 0:size] = part

    def send(tiles, targets):
        for col in range(col_devices):
            moves = [(step, col * cols, cols, step * cols) for step in range(SUB)]
            registers = moved(lambda step, block: tiles[step, block], moves, pieces)
            for piece in range(pieces):
                both = registers[piece].astype(F32)
                for half, (channel, group) in enumerate(targets):
                    start = (col * row_devices * share + channel) * line + group * pieces + piece
                    packed[pl.ds(start, row_devices, stride=share * line), :] = (
                        both[half * SUB : (half + 1) * SUB]
                    )
        missing.difference_update(targets)

    missing = set((channel, group) for channel in range(share) for group in range(groups))
    waiting = list(range(sent_ref.shape[0] // (2 * SUB)))

    def finish():
        for unit in list(waiting):
            lines = range(unit * 2 * SUB, (unit + 1) * 2 * SUB)
            if any((at // line % share, at % line // pieces) in missing for at in lines):
                continue
            waiting.remove(unit)
            at = slice(unit * 2 * SUB, (unit + 1) * 2 * SUB)
            sent_ref[at, :] = packed[at, :].astype(BF16)

    def pack(channel):
        for pair in range(groups // 2):
            tiles = {}
            for step in range(SUB):
                for block in range(blocks):
                    start = (pair * SUB + step) * 2 * SUB
                    tiles[step, block] = result_ref[channel, block, start : start + 2 * SUB, :]
            send(tiles, [(channel, 2 * pair), (channel, 2 * pair + 1)])
        if groups % 2 and channel % 2:
            group = groups - 1
            tiles = {}
            for block in range(blocks):
                for step in range(0, SUB, 2):
                    start = (group * SUB + step) * SUB
                    low, high = [
                        result_ref[one, block, start : start + 2 * SUB, :].astype(F32)
                        for one in (channel - 1, channel)
                    ]
                    tiles[step, block] = stacked(low[:SUB], high[:SUB])
                    tiles[step + 1, block] = stacked(low[SUB:], high[SUB:])
            send(tiles, [(channel - 1, group), (channel, group)])

    widen(0)
    for pair in range(pairs):
        if pair + 1 < pairs:
            widen(pair + 1)
        unpack(0, [pair])
    for channel in range(share):
        product(channel)
        if channel > 0:
            pack(channel - 1)
        if channel + 1 < share:
            unpack(channel + 1)
        else:
            finish()
    pack(share - 1)
    finish()


def by_channels(pair, token_mask, chain_ids, chain_bias, in_weights, out_weights, row_devices, col_devices):
    rows, cols, width = pair.shape
    devices = row_devices * col_devices
    share = width // devices
    lanes = SUB * cols
    pieces = lanes // LANES
    groups = rows // SUB
    chunk = groups * pieces * SUB
    spots = rows * cols
    line = groups * pieces
    total = row_devices * rows
    blocks = -(-total // LANES)
    tall = groups * SUB * row_devices
    params = pltpu.CompilerParams(vmem_limit_bytes=40 * 1024 * 1024)
    whole = pl.BlockSpec(memory_space=pltpu.VMEM)
    far = pl.BlockSpec(memory_space=pltpu.HBM)

    sent_shape = jax.ShapeDtypeStruct((devices, chunk, LANES), BF16)
    sum_shape = jax.ShapeDtypeStruct((devices * share * line, LANES), BF16)
    state_shape = jax.ShapeDtypeStruct((width, spots), F32)
    mask_shape = jax.ShapeDtypeStruct((1, spots), F32)
    padded_sum = pltpu.VMEM((-(-(devices + 1) * share * line // SUB) * SUB, LANES), F32)

    def exchange(array, rows):
        shape = (devices, rows) if rows % SUB == 0 else (devices, rows * 2 // SUB, SUB // 2)
        split = array.reshape(*shape, LANES)
        return lax.all_to_all(split, ("col", "row"), 0, 0, tiled=True).reshape(devices * rows, LANES)

    def triangle(direction, sent):
        wide_rows = (row_devices + 1) * wide_steps(col_devices * groups * pieces)[1]
        summed = pl.pallas_call(
            functools.partial(
                triangle_kernel, direction, share, rows, cols, row_devices, col_devices, line
            ),
            out_shape=sum_shape,
            in_specs=[whole],
            out_specs=whole,
            scratch_shapes=[
                pltpu.VMEM((-(-wide_rows // SUB) * SUB, LANES), F32),
                pltpu.VMEM((2, tall, blocks * LANES), BF16),
                pltpu.VMEM((2, tall, blocks * LANES), BF16),
                pltpu.VMEM((2, blocks, total + rows, LANES), F32),
                pltpu.VMEM((share, blocks, tall, LANES), BF16),
                padded_sum,
            ],
            compiler_params=params,
            name="triangle",
        )(exchange(sent, chunk))
        return exchange(summed, share * line)

    flat_pair = pair.reshape(spots, width)
    sent, gate, field, mask = pl.pallas_call(
        functools.partial(start_kernel, share, rows, cols),
        out_shape=[sent_shape, state_shape, state_shape, mask_shape],
        in_specs=[far] * 5,
        out_specs=[whole] * 4,
        scratch_shapes=[
            pltpu.VMEM(mask_shape.shape, F32),
            pltpu.VMEM((spots, width), BF16),
            pltpu.VMEM(in_weights.shape[1:], BF16),
            pltpu.VMEM((1, width), F32),
            pltpu.VMEM((1,) + token_mask.shape, jnp.int32),
            pltpu.VMEM((1,) + chain_ids.shape, jnp.int32),
            pltpu.SemaphoreType.DMA((6,)),
        ],
        compiler_params=params,
        name="start",
    )(*[
        pltpu.with_memory_space_constraint(array, pltpu.HBM)
        for array in (token_mask, chain_ids, flat_pair, chain_bias, in_weights)
    ])
    got = triangle(0, sent)
    sent, gate, field = pl.pallas_call(
        functools.partial(middle_kernel, share, line),
        out_shape=[sent_shape, state_shape, state_shape],
        in_specs=[whole] * 6,
        out_specs=[whole] * 3,
        scratch_shapes=[padded_sum],
        compiler_params=params,
        name="middle",
    )(mask, got, field, gate, out_weights, in_weights)
    got = triangle(1, sent)
    out = pl.pallas_call(
        functools.partial(end_kernel, line),
        out_shape=jax.ShapeDtypeStruct((spots, width), BF16),
        in_specs=[whole] * 4,
        out_specs=far,
        scratch_shapes=[
            padded_sum,
            pltpu.VMEM((spots, width), BF16),
            pltpu.SemaphoreType.DMA((len(spans(spots)),)),
        ],
        compiler_params=params,
        name="end",
    )(got, field, gate, out_weights)
    return out.reshape(pair.shape)


def gated_inputs(field, weights, pair_mask):
    width = weights.shape[0]
    normed = layer_norm(field).astype(BF16)
    projected = jnp.einsum("ijc,cd->ijd", normed, weights, preferred_element_type=F32)
    first = (
        jax.nn.sigmoid(projected[..., :width])
        * projected[..., width : 2 * width]
        * pair_mask[:, :, None]
    ).astype(BF16)
    second = (
        jax.nn.sigmoid(projected[..., 2 * width : 3 * width])
        * projected[..., 3 * width : 4 * width]
        * pair_mask[:, :, None]
    ).astype(BF16)
    gate_value = jax.nn.sigmoid(projected[..., 4 * width :])
    return (first, second, gate_value)


def update(field, summed, gate_value, weights):
    normed_sum = layer_norm(summed).astype(BF16)
    output = jnp.einsum("ijc,cd->ijd", normed_sum, weights, preferred_element_type=F32)
    return field + gate_value * output


def by_blocks(pair, token_mask, chain_ids, chain_bias, in_weights, out_weights):
    row_count = pair.shape[0]
    col_count = pair.shape[1]
    row_start = lax.axis_index("row") * row_count
    col_start = lax.axis_index("col") * col_count
    valid_rows = lax.dynamic_slice_in_dim(token_mask, row_start, row_count).astype(F32)
    valid_cols = lax.dynamic_slice_in_dim(token_mask, col_start, col_count).astype(F32)
    chain_rows = lax.dynamic_slice_in_dim(chain_ids, row_start, row_count)
    chain_cols = lax.dynamic_slice_in_dim(chain_ids, col_start, col_count)
    pair_mask = valid_rows[:, None] * valid_cols[None, :]
    same_chain = (chain_rows[:, None] == chain_cols[None, :]).astype(F32)
    field = pair.astype(F32) + same_chain[:, :, None] * chain_bias
    first, second, gate_value = gated_inputs(field, in_weights[0], pair_mask)
    second_rows = lax.all_gather(second, "row", axis=0, tiled=True)
    part = jnp.einsum("jkc,ikc->jic", second_rows, first, preferred_element_type=F32).astype(BF16)
    summed = lax.psum_scatter(part, "col", scatter_dimension=0, tiled=True).astype(F32)
    summed = jnp.transpose(summed, (1, 0, 2))
    field = update(field, summed, gate_value, out_weights[0])
    first, second, gate_value = gated_inputs(field, in_weights[1], pair_mask)
    first_cols = lax.all_gather(first, "col", axis=1, tiled=True)
    part = jnp.einsum("kic,kjc->ijc", first_cols, second, preferred_element_type=F32).astype(BF16)
    summed = lax.psum_scatter(part, "row", scatter_dimension=0, tiled=True).astype(F32)
    field = update(field, summed, gate_value, out_weights[1])
    return field.astype(BF16)


def solution(mesh):
    row_devices, col_devices = mesh.shape["row"], mesh.shape["col"]

    def per_device(pair, *rest):
        rows, cols, width = pair.shape
        devices = row_devices * col_devices
        fits = (
            width % devices == 0
            and 2 * (width // devices) == SUB
            and row_devices == SUB
            and rows % SUB == 0
            and rows >= 3 * SUB
            and (SUB * cols) % LANES == 0
            and max(rows, cols) <= LANES
        )
        if fits:
            return by_channels(pair, *rest, row_devices, col_devices)
        return by_blocks(pair, *rest)

    return jax.shard_map(
        per_device,
        mesh=mesh,
        in_specs=(P("row", "col", None), P(), P(), P(), P(), P()),
        out_specs=P("row", "col", None),
        check_vma=False,
    )
```

```python
import functools

import jax
import jax.numpy as jnp
from jax import lax
from jax.experimental import pallas as pl
from jax.experimental.pallas import tpu as pltpu
from jax.sharding import PartitionSpec as P

LANES = 128
SUB = 8
SPAN = 1280
F32 = jnp.float32
BF16 = jnp.bfloat16


def layer_norm(values, axis=-1):
    center = values - jnp.mean(values, axis=axis, keepdims=True)
    spread = jnp.mean(center * center, axis=axis, keepdims=True)
    return center * lax.rsqrt(spread + 1e-05)


def matmul(left, right, dims):
    return lax.dot_general(left, right, (dims, ((), ())), preferred_element_type=F32)


def identity(size, scale):
    row = lax.broadcasted_iota(jnp.int32, (size, size), 0)
    col = lax.broadcasted_iota(jnp.int32, (size, size), 1)
    return jnp.where(row == col, scale, 0.0).astype(BF16)


def column(row_ref):
    width = row_ref.shape[1]
    return jnp.broadcast_to(row_ref[...], (width, width)).T[:, 0:1]


def transposed(weights, scale):
    eye = identity(weights.shape[1], scale)
    return matmul(eye, weights, ((1,), (1,))).astype(BF16)


def interleaved(first, second, share):
    width = first.shape[1]
    both = jnp.concatenate([first, second], axis=1)
    row = lax.broadcasted_iota(jnp.int32, (2 * width, 1), 0)
    col = lax.broadcasted_iota(jnp.int32, (2 * width, 2 * width), 1)
    owner, place = row // (2 * share), row % (2 * share)
    source = owner * share + place % share + jnp.where(place >= share, width, 0)
    pick = jnp.where(col == source, 0.5, 0.0).astype(BF16)
    return matmul(pick, both, ((1,), (1,))).astype(BF16)


def load_in_weights(weights, share):
    width = weights.shape[0]
    blocks = [weights[:, k * width : (k + 1) * width] for k in range(5)]
    return (
        interleaved(blocks[0], blocks[2], share),
        interleaved(blocks[1], blocks[3], share),
        transposed(blocks[4], 0.5),
    )


def token_vectors(tokens, row_start, col_start, rows, cols):
    groups = rows // SUB
    wide = tokens.shape[1]
    many = jnp.broadcast_to(tokens.astype(F32), (SUB, wide))
    lane = lax.broadcasted_iota(jnp.int32, (1, SUB * cols), 1)
    at_row = jnp.zeros_like(lane)
    for step in range(1, SUB):
        at_row = at_row + jnp.where(lane >= step * cols, 1, 0)
    at_col = lane - at_row * cols
    key = lax.broadcasted_iota(jnp.int32, (LANES, SUB * cols), 0)
    pick_row = jnp.where(key == at_row, 1.0, 0.0).astype(BF16)
    pick_col = jnp.where(key == at_col, 1.0, 0.0).astype(BF16)

    def window(start):
        return pltpu.roll(many, wide - start, 1)[:, :LANES]

    by_col = matmul(window(col_start).astype(BF16), pick_col, ((1,), (0,)))[0:1]
    windows = [window(row_start + group * SUB)[0:1] for group in range(groups)]
    windows.append(jnp.zeros((-groups % SUB, LANES), F32))
    by_row = matmul(jnp.concatenate(windows, axis=0).astype(BF16), pick_row, ((1,), (0,)))
    by_row = by_row.astype(jnp.int32)
    by_col = by_col.astype(jnp.int32)
    masks = (by_row & by_col & 1).astype(F32)
    sames = jnp.where((by_row >> 1) == (by_col >> 1), 1.0, 0.0)
    return masks, sames


def staged(count, stages):
    held = {}
    for step in range(count + len(stages) - 1):
        for number, stage in enumerate(stages):
            item = step - number
            if 0 <= item < count:
                held[item] = stage(item, held.get(item))


def spans(total):
    return [slice(at, min(at + SPAN, total)) for at in range(0, total, SPAN)]


def projected(field, in_t):
    normed = layer_norm(field, 0).astype(BF16)
    return [matmul(weights, normed, ((1,), (0,))) for weights in in_t]


def gated(products, mask, at, share, sent_ref, gate_ref):
    gates, values, gate = products
    width, lanes = gate.shape
    sent = (jnp.tanh(gates) * values + values) * mask
    lines = slice(at.start // LANES * SUB, at.stop // LANES * SUB)
    for owner in range(width // share):
        block = sent[owner * 2 * share : (owner + 1) * 2 * share]
        tiles = [block[:, lane : lane + LANES] for lane in range(0, lanes, LANES)]
        sent_ref[owner, lines, :] = jnp.concatenate(tiles, axis=0).astype(BF16)
    gate_ref[:, at] = jnp.tanh(gate)


def start_kernel(share, rows, cols, valid_hbm, chain_hbm, pair_hbm, bias_hbm, w_hbm,
                 sent_ref, gate_ref, field_ref, mask_ref,
                 same_ref, pair_ref, w_ref, bias_ref, valid_ref, chain_ref, sems):
    lanes = SUB * cols
    groups = rows // SUB
    spots, width = pair_ref.shape
    count = valid_hbm.shape[0]
    ranges = spans(spots)
    first = ranges[len(ranges) // 3].start
    started = []

    def copy(near, far):
        started.append(pltpu.make_async_copy(near, far, sems.at[len(started)]))
        started[-1].start()

    copy(w_hbm.at[0], w_ref)
    copy(valid_hbm, valid_ref.at[0])
    copy(chain_hbm, chain_ref.at[0])
    copy(bias_hbm, bias_ref.at[0])
    for at in (pl.ds(0, first), pl.ds(first, spots - first)):
        copy(pair_hbm.at[at], pair_ref.at[at])
    eye = identity(width, 1.0)
    row_start = lax.axis_index("row") * rows
    col_start = lax.axis_index("col") * cols
    started[0].wait()
    in_t = load_in_weights(w_ref[...], share)
    for number in range(1, len(started) - 1):
        started[number].wait()

    def lift(item):
        if ranges[item].start == first:
            started[-1].wait()
        return matmul(eye, pair_ref[ranges[item], :], ((1,), (1,)))

    lifted = {0: lift(0)}
    tokens = chain_ref[...] * 2 + valid_ref[...]
    tokens = jnp.concatenate([tokens, jnp.zeros((1, -count % LANES), jnp.int32)], axis=1)
    masks, sames = token_vectors(tokens, row_start, col_start, rows, cols)
    for group in range(groups):
        at = slice(group * lanes, (group + 1) * lanes)
        mask_ref[:, at] = masks[group : group + 1]
        same_ref[:, at] = sames[group : group + 1]
    bias_col = column(bias_ref)

    def make_field(item, _):
        if item + 1 < len(ranges):
            lifted[item + 1] = lift(item + 1)
        field = lifted.pop(item) + bias_col * same_ref[:, ranges[item]]
        field_ref[:, ranges[item]] = field
        return field

    def project(item, field):
        return projected(field, in_t)

    def finish(item, products):
        at = ranges[item]
        gated(products, mask_ref[:, at], at, share, sent_ref, gate_ref)

    staged(len(ranges), (make_field, project, finish))


def output_of(wide, out_t, at, line):
    width = out_t.shape[1]
    parts = []
    for piece in range(at.start // LANES, at.stop // LANES):
        parts.append(wide[pl.ds(piece, width, stride=line), :])
    normed = layer_norm(jnp.concatenate(parts, axis=1), 0).astype(BF16)
    return matmul(out_t, normed, ((1,), (0,)))


def middle_kernel(share, line, mask_ref, got_ref, field_in, gate_in, wo_ref, w_ref,
                  sent_ref, gate_ref, field_ref, wide):
    ranges = spans(field_in.shape[1])
    count = got_ref.shape[0]
    half = count // 2
    wide[:half, :] = got_ref[:half, :].astype(F32)
    out_t = transposed(wo_ref[0], 0.5)
    wide[half:count, :] = got_ref[half:, :].astype(F32)
    in_t = load_in_weights(w_ref[1], share)

    def outgoing(item, _):
        return output_of(wide, out_t, ranges[item], line)

    def project(item, output):
        at = ranges[item]
        field = field_in[:, at] + (gate_in[:, at] * output + output)
        field_ref[:, at] = field
        return projected(field, in_t)

    def finish(item, products):
        at = ranges[item]
        gated(products, mask_ref[:, at], at, share, sent_ref, gate_ref)

    staged(len(ranges), (outgoing, project, finish))


def end_kernel(line, got_ref, field_in, gate_in, wo_ref, out_hbm, wide, out_ref, sems):
    ranges = spans(field_in.shape[1])
    out_t = transposed(wo_ref[1], 0.5)
    wide[: got_ref.shape[0], :] = got_ref[...].astype(F32)
    copies = []
    done = [0]

    def outgoing(item, _):
        return output_of(wide, out_t, ranges[item], line)

    def finish(item, output):
        at = ranges[item]
        field = field_in[:, at] + (gate_in[:, at] * output + output)
        out_ref[at, :] = field.astype(BF16).T
        if item % 3 == 0 or item == len(ranges) - 1:
            rows = pl.ds(done[0], at.stop - done[0])
            done[0] = at.stop
            copies.append(pltpu.make_async_copy(out_ref.at[rows], out_hbm.at[rows], sems.at[len(copies)]))
            copies[-1].start()

    staged(len(ranges), (outgoing, finish))
    for copy in copies:
        copy.wait()


def moved(source, moves, count):
    shape = None
    lane = None
    targets = [[] for _ in range(count)]
    for row, begin, length, target in moves:
        shift = (target - begin) % LANES
        while length > 0:
            size = min(length, LANES - begin % LANES, LANES - target % LANES)
            targets[target // LANES].append((target % LANES, row, begin // LANES, shift))
            begin, target, length = begin + size, target + size, length - size
    rolled = {}
    registers = []
    for pieces in targets:
        value = None
        for start, row, register, shift in sorted(pieces, key=lambda piece: piece[0]):
            key = (row, register, shift)
            if key not in rolled:
                tile = source(row, register)
                rolled[key] = pltpu.roll(tile, shift, 1) if shift else tile
            if value is None:
                value = rolled[key]
            else:
                if lane is None:
                    shape = value.shape
                    lane = lax.broadcasted_iota(jnp.int32, shape, 1)
                value = jnp.where(lane < start, value, rolled[key])
        registers.append(value)
    return registers


def wide_steps(tiles):
    place_step = tiles + 1 - tiles % 2
    return place_step, SUB * place_step + 1


def row_order(groups, row_devices, rows, width):
    line = lax.broadcasted_iota(jnp.int32, (groups * SUB * row_devices, 1), 0)
    row, rest = line % row_devices, line // row_devices
    paired = groups // 2 * 2
    pair, inside = rest // (2 * SUB), rest % (2 * SUB)
    of_pair = (2 * pair + inside % 2) * SUB + inside // 2
    place = jnp.where(rest < paired * SUB, of_pair, rest)
    lane = lax.broadcasted_iota(jnp.int32, (groups * SUB * row_devices, width), 1)
    return jnp.where(lane == row * rows + place, 1.0, 0.0).astype(BF16)


def stacked(low, high):
    return jnp.concatenate([low, high], axis=0).astype(BF16)


def triangle_kernel(direction, share, rows, cols, row_devices, col_devices, line, got_ref, sent_ref,
                    wide, left_ref, right_ref, even_ref, result_ref, packed):
    groups = rows // SUB
    pieces = SUB * cols // LANES
    total = row_devices * rows
    blocks = -(-total // LANES)
    pairs = -(-groups // 2)
    rest = total - (blocks - 1) * LANES
    tail = lax.broadcasted_iota(jnp.int32, (2 * SUB, LANES), 1) < rest
    place_step, row_step = wide_steps(col_devices * groups * pieces)
    pick = row_order(groups, row_devices, rows, blocks * LANES) if direction == 1 else None

    def spot(tile):
        device, number = divmod(tile, groups * pieces)
        col, row = divmod(device, row_devices)
        return row * row_step + col * groups * pieces + number

    def widen(pair):
        for unit in range(got_ref.shape[0] // (2 * SUB)):
            owners = [tile % (groups * pieces) // pieces // 2 for tile in (2 * unit, 2 * unit + 1)]
            if min(owners) != pair:
                continue
            both = got_ref[unit * 2 * SUB : (unit + 1) * 2 * SUB, :].astype(F32)
            for half in range(2):
                at = pl.ds(spot(2 * unit + half), SUB, stride=place_step)
                wide[at, :] = both[half * SUB : (half + 1) * SUB]

    def loaded(place, group, col, piece):
        start = place * place_step + (col * groups + group) * pieces + piece
        return wide[pl.ds(start, row_devices, stride=row_step), :]

    def spread(tiles, step, cleared):
        moves = [(col, step * cols, cols, col * cols) for col in range(col_devices)]
        registers = moved(lambda col, piece: tiles[col, piece], moves, blocks)
        if cleared:
            registers[-1] = jnp.where(tail, registers[-1], jnp.zeros_like(registers[-1]))
        return registers

    def put(target, spare, start, block, value):
        target[spare, start : start + 2 * SUB, block * LANES : (block + 1) * LANES] = value

    def put_even(spare, group, step, block, value):
        even_ref[spare, block, pl.ds(group * SUB + step, row_devices, stride=rows), :] = value

    def unpack(channel, only=range(pairs)):
        spare = channel % 2
        for pair in only:
            if 2 * pair + 1 < groups:
                unpack_pair(channel, spare, pair)
            else:
                unpack_last(channel, spare, 2 * pair)

    def unpack_pair(channel, spare, pair):
        for is_right, place in ((False, channel), (True, share + channel)):
            tiles = {}
            for col in range(col_devices):
                for piece in range(pieces):
                    tiles[col, piece] = stacked(
                        loaded(place, 2 * pair, col, piece), loaded(place, 2 * pair + 1, col, piece)
                    )
            for step in range(SUB):
                for block, register in enumerate(spread(tiles, step, direction == 0 and not is_right)):
                    if is_right and direction == 0:
                        both = register.astype(F32)
                        for half in range(2):
                            put_even(spare, 2 * pair + half, step, block, both[half * SUB : (half + 1) * SUB])
                    else:
                        target = right_ref if is_right else left_ref
                        put(target, spare, (pair * SUB + step) * 2 * SUB, block, register)

    def unpack_last(channel, spare, group):
        tiles = {}
        for col in range(col_devices):
            for piece in range(pieces):
                tiles[col, piece] = stacked(
                    loaded(channel, group, col, piece), loaded(share + channel, group, col, piece)
                )
        before = None
        for step in range(SUB):
            now = [register.astype(F32) for register in spread(tiles, step, direction == 0)]
            for block in range(blocks):
                if direction == 0:
                    put_even(spare, group, step, block, now[block][SUB:])
                if step % 2:
                    start = (group * SUB + step - 1) * SUB
                    put(left_ref, spare, start, block, stacked(before[block][:SUB], now[block][:SUB]))
                    if direction == 1:
                        put(right_ref, spare, start, block, stacked(before[block][SUB:], now[block][SUB:]))
            before = now

    def product(channel):
        spare = channel % 2
        if direction == 0:
            right = [even_ref[spare, block, 0:total].astype(BF16) for block in range(blocks)]
            right = jnp.concatenate(right, axis=1)
            summed = matmul(left_ref[spare], right, ((1,), (1,)))
        else:
            turned = matmul(pick, left_ref[spare], ((1,), (1,))).astype(BF16)
            summed = matmul(turned, right_ref[spare], ((1,), (0,)))
        for block in range(blocks):
            size = min(LANES, total - block * LANES)
            part = summed[:, block * LANES : block * LANES + size].astype(BF16)
            result_ref[channel, block, :, 0:size] = part

    def send(tiles, targets):
        for col in range(col_devices):
            moves = [(step, col * cols, cols, step * cols) for step in range(SUB)]
            registers = moved(lambda step, block: tiles[step, block], moves, pieces)
            for piece in range(pieces):
                both = registers[piece].astype(F32)
                for half, (channel, group) in enumerate(targets):
                    start = (col * row_devices * share + channel) * line + group * pieces + piece
                    packed[pl.ds(start, row_devices, stride=share * line), :] = (
                        both[half * SUB : (half + 1) * SUB]
                    )
        missing.difference_update(targets)

    missing = set((channel, group) for channel in range(share) for group in range(groups))
    waiting = list(range(sent_ref.shape[0] // (2 * SUB)))

    def finish():
        for unit in list(waiting):
            lines = range(unit * 2 * SUB, (unit + 1) * 2 * SUB)
            if any((at // line % share, at % line // pieces) in missing for at in lines):
                continue
            waiting.remove(unit)
            at = slice(unit * 2 * SUB, (unit + 1) * 2 * SUB)
            sent_ref[at, :] = packed[at, :].astype(BF16)

    def pack(channel):
        for pair in range(groups // 2):
            tiles = {}
            for step in range(SUB):
                for block in range(blocks):
                    start = (pair * SUB + step) * 2 * SUB
                    tiles[step, block] = result_ref[channel, block, start : start + 2 * SUB, :]
            send(tiles, [(channel, 2 * pair), (channel, 2 * pair + 1)])
        if groups % 2 and channel % 2:
            group = groups - 1
            tiles = {}
            for block in range(blocks):
                for step in range(0, SUB, 2):
                    start = (group * SUB + step) * SUB
                    low, high = [
                        result_ref[one, block, start : start + 2 * SUB, :].astype(F32)
                        for one in (channel - 1, channel)
                    ]
                    tiles[step, block] = stacked(low[:SUB], high[:SUB])
                    tiles[step + 1, block] = stacked(low[SUB:], high[SUB:])
            send(tiles, [(channel - 1, group), (channel, group)])

    widen(0)
    for pair in range(pairs):
        if pair + 1 < pairs:
            widen(pair + 1)
        unpack(0, [pair])
    for channel in range(share):
        product(channel)
        if channel > 0:
            pack(channel - 1)
        if channel + 1 < share:
            unpack(channel + 1)
        else:
            finish()
    pack(share - 1)
    finish()


def by_channels(pair, token_mask, chain_ids, chain_bias, in_weights, out_weights, row_devices, col_devices):
    rows, cols, width = pair.shape
    devices = row_devices * col_devices
    share = width // devices
    lanes = SUB * cols
    pieces = lanes // LANES
    groups = rows // SUB
    chunk = groups * pieces * SUB
    spots = rows * cols
    line = groups * pieces
    total = row_devices * rows
    blocks = -(-total // LANES)
    tall = groups * SUB * row_devices
    params = pltpu.CompilerParams(vmem_limit_bytes=40 * 1024 * 1024)
    whole = pl.BlockSpec(memory_space=pltpu.VMEM)
    far = pl.BlockSpec(memory_space=pltpu.HBM)

    sent_shape = jax.ShapeDtypeStruct((devices, chunk, LANES), BF16)
    sum_shape = jax.ShapeDtypeStruct((devices * share * line, LANES), BF16)
    state_shape = jax.ShapeDtypeStruct((width, spots), F32)
    mask_shape = jax.ShapeDtypeStruct((1, spots), F32)
    padded_sum = pltpu.VMEM((-(-(devices + 1) * share * line // SUB) * SUB, LANES), F32)

    def exchange(array, rows):
        shape = (devices, rows) if rows % SUB == 0 else (devices, rows * 2 // SUB, SUB // 2)
        split = array.reshape(*shape, LANES)
        return lax.all_to_all(split, ("col", "row"), 0, 0, tiled=True).reshape(devices * rows, LANES)

    def triangle(direction, sent):
        wide_rows = (row_devices + 1) * wide_steps(col_devices * groups * pieces)[1]
        summed = pl.pallas_call(
            functools.partial(
                triangle_kernel, direction, share, rows, cols, row_devices, col_devices, line
            ),
            out_shape=sum_shape,
            in_specs=[whole],
            out_specs=whole,
            scratch_shapes=[
                pltpu.VMEM((-(-wide_rows // SUB) * SUB, LANES), F32),
                pltpu.VMEM((2, tall, blocks * LANES), BF16),
                pltpu.VMEM((2, tall, blocks * LANES), BF16),
                pltpu.VMEM((2, blocks, total + rows, LANES), F32),
                pltpu.VMEM((share, blocks, tall, LANES), BF16),
                padded_sum,
            ],
            compiler_params=params,
            name="triangle",
        )(exchange(sent, chunk))
        return exchange(summed, share * line)

    flat_pair = pair.reshape(spots, width)
    sent, gate, field, mask = pl.pallas_call(
        functools.partial(start_kernel, share, rows, cols),
        out_shape=[sent_shape, state_shape, state_shape, mask_shape],
        in_specs=[far] * 5,
        out_specs=[whole] * 4,
        scratch_shapes=[
            pltpu.VMEM(mask_shape.shape, F32),
            pltpu.VMEM((spots, width), BF16),
            pltpu.VMEM(in_weights.shape[1:], BF16),
            pltpu.VMEM((1, width), F32),
            pltpu.VMEM((1,) + token_mask.shape, jnp.int32),
            pltpu.VMEM((1,) + chain_ids.shape, jnp.int32),
            pltpu.SemaphoreType.DMA((6,)),
        ],
        compiler_params=params,
        name="start",
    )(*[
        pltpu.with_memory_space_constraint(array, pltpu.HBM)
        for array in (token_mask, chain_ids, flat_pair, chain_bias, in_weights)
    ])
    got = triangle(0, sent)
    sent, gate, field = pl.pallas_call(
        functools.partial(middle_kernel, share, line),
        out_shape=[sent_shape, state_shape, state_shape],
        in_specs=[whole] * 6,
        out_specs=[whole] * 3,
        scratch_shapes=[padded_sum],
        compiler_params=params,
        name="middle",
    )(mask, got, field, gate, out_weights, in_weights)
    got = triangle(1, sent)
    out = pl.pallas_call(
        functools.partial(end_kernel, line),
        out_shape=jax.ShapeDtypeStruct((spots, width), BF16),
        in_specs=[whole] * 4,
        out_specs=far,
        scratch_shapes=[
            padded_sum,
            pltpu.VMEM((spots, width), BF16),
            pltpu.SemaphoreType.DMA((len(spans(spots)),)),
        ],
        compiler_params=params,
        name="end",
    )(got, field, gate, out_weights)
    return out.reshape(pair.shape)


def gated_inputs(field, weights, pair_mask):
    width = weights.shape[0]
    normed = layer_norm(field).astype(BF16)
    projected = jnp.einsum("ijc,cd->ijd", normed, weights, preferred_element_type=F32)
    first = (
        jax.nn.sigmoid(projected[..., :width])
        * projected[..., width : 2 * width]
        * pair_mask[:, :, None]
    ).astype(BF16)
    second = (
        jax.nn.sigmoid(projected[..., 2 * width : 3 * width])
        * projected[..., 3 * width : 4 * width]
        * pair_mask[:, :, None]
    ).astype(BF16)
    gate_value = jax.nn.sigmoid(projected[..., 4 * width :])
    return (first, second, gate_value)


def update(field, summed, gate_value, weights):
    normed_sum = layer_norm(summed).astype(BF16)
    output = jnp.einsum("ijc,cd->ijd", normed_sum, weights, preferred_element_type=F32)
    return field + gate_value * output


def by_blocks(pair, token_mask, chain_ids, chain_bias, in_weights, out_weights):
    row_count = pair.shape[0]
    col_count = pair.shape[1]
    row_start = lax.axis_index("row") * row_count
    col_start = lax.axis_index("col") * col_count
    valid_rows = lax.dynamic_slice_in_dim(token_mask, row_start, row_count).astype(F32)
    valid_cols = lax.dynamic_slice_in_dim(token_mask, col_start, col_count).astype(F32)
    chain_rows = lax.dynamic_slice_in_dim(chain_ids, row_start, row_count)
    chain_cols = lax.dynamic_slice_in_dim(chain_ids, col_start, col_count)
    pair_mask = valid_rows[:, None] * valid_cols[None, :]
    same_chain = (chain_rows[:, None] == chain_cols[None, :]).astype(F32)
    field = pair.astype(F32) + same_chain[:, :, None] * chain_bias
    first, second, gate_value = gated_inputs(field, in_weights[0], pair_mask)
    second_rows = lax.all_gather(second, "row", axis=0, tiled=True)
    part = jnp.einsum("jkc,ikc->jic", second_rows, first, preferred_element_type=F32).astype(BF16)
    summed = lax.psum_scatter(part, "col", scatter_dimension=0, tiled=True).astype(F32)
    summed = jnp.transpose(summed, (1, 0, 2))
    field = update(field, summed, gate_value, out_weights[0])
    first, second, gate_value = gated_inputs(field, in_weights[1], pair_mask)
    first_cols = lax.all_gather(first, "col", axis=1, tiled=True)
    part = jnp.einsum("kic,kjc->ijc", first_cols, second, preferred_element_type=F32).astype(BF16)
    summed = lax.psum_scatter(part, "row", scatter_dimension=0, tiled=True).astype(F32)
    field = update(field, summed, gate_value, out_weights[1])
    return field.astype(BF16)


def solution(mesh):
    row_devices, col_devices = mesh.shape["row"], mesh.shape["col"]

    def per_device(pair, *rest):
        rows, cols, width = pair.shape
        devices = row_devices * col_devices
        fits = (
            width % devices == 0
            and 2 * (width // devices) == SUB
            and row_devices == SUB
            and rows % SUB == 0
            and rows >= 3 * SUB
            and (SUB * cols) % LANES == 0
            and max(rows, cols) <= LANES
        )
        if fits:
            return by_channels(pair, *rest, row_devices, col_devices)
        return by_blocks(pair, *rest)

    return jax.shard_map(
        per_device,
        mesh=mesh,
        in_specs=(P("row", "col", None), P(), P(), P(), P(), P()),
        out_specs=P("row", "col", None),
        check_vma=False,
    )
```

```python
import functools

import jax
import jax.numpy as jnp
from jax import lax
from jax.experimental import pallas as pl
from jax.experimental.pallas import tpu as pltpu
from jax.sharding import PartitionSpec as P

LANES = 128
SUB = 8
F32 = jnp.float32
BF16 = jnp.bfloat16


def layer_norm(values, axis=-1):
    center = values - jnp.mean(values, axis=axis, keepdims=True)
    spread = jnp.mean(center * center, axis=axis, keepdims=True)
    return center * lax.rsqrt(spread + 1e-05)


def matmul(left, right, dims):
    return lax.dot_general(left, right, (dims, ((), ())), preferred_element_type=F32)


def identity(size, scale):
    row = lax.broadcasted_iota(jnp.int32, (size, size), 0)
    col = lax.broadcasted_iota(jnp.int32, (size, size), 1)
    return jnp.where(row == col, scale, 0.0).astype(BF16)


def column(row_ref):
    width = row_ref.shape[1]
    return jnp.broadcast_to(row_ref[...], (width, width)).T[:, 0:1]


def transposed(weights, scale):
    eye = identity(weights.shape[1], scale)
    return matmul(eye, weights, ((1,), (1,))).astype(BF16)


def interleaved(first, second, share):
    width = first.shape[1]
    both = jnp.concatenate([first, second], axis=1)
    row = lax.broadcasted_iota(jnp.int32, (2 * width, 1), 0)
    col = lax.broadcasted_iota(jnp.int32, (2 * width, 2 * width), 1)
    owner, place = row // (2 * share), row % (2 * share)
    source = owner * share + place % share + jnp.where(place >= share, width, 0)
    pick = jnp.where(col == source, 0.5, 0.0).astype(BF16)
    return matmul(pick, both, ((1,), (1,))).astype(BF16)


def load_in_weights(weights, share):
    width = weights.shape[0]
    blocks = [weights[:, k * width : (k + 1) * width] for k in range(5)]
    return (
        interleaved(blocks[0], blocks[2], share),
        interleaved(blocks[1], blocks[3], share),
        transposed(blocks[4], 0.5),
    )


def token_vectors(tokens, row_start, col_start, rows, cols):
    groups = rows // SUB
    wide = tokens.shape[1]
    many = jnp.broadcast_to(tokens.astype(F32), (SUB, wide))
    lane = lax.broadcasted_iota(jnp.int32, (1, SUB * cols), 1)
    at_row = jnp.zeros_like(lane)
    for step in range(1, SUB):
        at_row = at_row + jnp.where(lane >= step * cols, 1, 0)
    at_col = lane - at_row * cols
    key = lax.broadcasted_iota(jnp.int32, (LANES, SUB * cols), 0)
    pick_row = jnp.where(key == at_row, 1.0, 0.0).astype(BF16)
    pick_col = jnp.where(key == at_col, 1.0, 0.0).astype(BF16)

    def window(start):
        return pltpu.roll(many, wide - start, 1)[:, :LANES]

    by_col = matmul(window(col_start).astype(BF16), pick_col, ((1,), (0,)))[0:1]
    windows = [window(row_start + group * SUB)[0:1] for group in range(groups)]
    windows.append(jnp.zeros((-groups % SUB, LANES), F32))
    by_row = matmul(jnp.concatenate(windows, axis=0).astype(BF16), pick_row, ((1,), (0,)))
    by_row = by_row.astype(jnp.int32)
    by_col = by_col.astype(jnp.int32)
    masks = (by_row & by_col & 1).astype(F32)
    sames = jnp.where((by_row >> 1) == (by_col >> 1), 1.0, 0.0)
    return masks, sames


def staged(count, stages):
    held = {}
    for step in range(count + len(stages) - 1):
        for number, stage in enumerate(stages):
            item = step - number
            if 0 <= item < count:
                held[item] = stage(item, held.get(item))


def projected(field, in_t):
    normed = layer_norm(field, 0).astype(BF16)
    return [matmul(weights, normed, ((1,), (0,))) for weights in in_t]


def gated(products, mask, group, share, sent_ref, gate_ref):
    gates, values, gate = products
    width, lanes = gate.shape
    sent = (jnp.tanh(gates) * values + values) * mask
    for owner in range(width // share):
        block = sent[owner * 2 * share : (owner + 1) * 2 * share]
        lines = [block[:, at : at + LANES] for at in range(0, lanes, LANES)]
        sent_ref[owner, group] = jnp.concatenate(lines, axis=0).astype(BF16)
    gate_ref[:, group * lanes : (group + 1) * lanes] = jnp.tanh(gate)


def start_kernel(share, rows, cols, valid_hbm, chain_hbm, pair_hbm, bias_hbm, w_hbm,
                 sent_ref, gate_ref, field_ref, mask_ref,
                 pair_ref, w_ref, bias_ref, valid_ref, chain_ref, sems):
    lanes = SUB * cols
    groups = rows // SUB
    width = pair_ref.shape[1]
    count = valid_hbm.shape[0]
    started = []

    def copy(near, far):
        started.append(pltpu.make_async_copy(near, far, sems.at[len(started)]))
        started[-1].start()

    copy(w_hbm.at[0], w_ref)
    copy(valid_hbm, valid_ref.at[0])
    copy(chain_hbm, chain_ref.at[0])
    copy(bias_hbm, bias_ref.at[0])
    for at in (pl.ds(0, 2 * lanes), pl.ds(2 * lanes, (groups - 2) * lanes)):
        copy(pair_hbm.at[at], pair_ref.at[at])
    arriving = len(started)
    eye = identity(width, 1.0)
    row_start = lax.axis_index("row") * rows
    col_start = lax.axis_index("col") * cols
    started[0].wait()
    in_t = load_in_weights(w_ref[...], share)
    for number in range(1, arriving - 1):
        started[number].wait()

    def lift(group):
        if group == 2:
            started[arriving - 1].wait()
        rows_of = pair_ref[group * lanes : (group + 1) * lanes, :]
        return matmul(eye, rows_of, ((1,), (1,)))

    lifted = {0: lift(0)}
    tokens = chain_ref[...] * 2 + valid_ref[...]
    tokens = jnp.concatenate([tokens, jnp.zeros((1, -count % LANES), jnp.int32)], axis=1)
    masks, sames = token_vectors(tokens, row_start, col_start, rows, cols)
    bias_col = column(bias_ref)

    def make_field(group, _):
        at = slice(group * lanes, (group + 1) * lanes)
        if group + 1 < groups:
            lifted[group + 1] = lift(group + 1)
        field = lifted.pop(group) + bias_col * sames[group : group + 1]
        field_ref[:, at] = field
        mask_ref[:, at] = masks[group : group + 1]
        return field

    def project(group, field):
        return projected(field, in_t)

    def finish(group, products):
        gated(products, masks[group : group + 1], group, share, sent_ref, gate_ref)

    staged(groups, (make_field, project, finish))


def output_of(wide, out_t, group, lanes, line):
    width = out_t.shape[1]
    pieces = lanes // LANES
    parts = []
    for piece in range(pieces):
        parts.append(wide[pl.ds(group * pieces + piece, width, stride=line), :])
    normed = layer_norm(jnp.concatenate(parts, axis=1), 0).astype(BF16)
    return matmul(out_t, normed, ((1,), (0,)))


def middle_kernel(share, rows, cols, line, mask_ref, got_ref, field_in, gate_in, prepared,
                  sent_ref, gate_ref, field_ref, wide):
    lanes = SUB * cols
    *in_t, out_t, _ = prepared_parts(prepared)
    wide[: got_ref.shape[0], :] = got_ref[...].astype(F32)

    def span(group):
        return slice(group * lanes, (group + 1) * lanes)

    def outgoing(group, _):
        return output_of(wide, out_t, group, lanes, line)

    def project(group, output):
        at = span(group)
        field = field_in[:, at] + (gate_in[:, at] * output + output)
        field_ref[:, at] = field
        return projected(field, in_t)

    def finish(group, products):
        gated(products, mask_ref[:, span(group)], group, share, sent_ref, gate_ref)

    staged(rows // SUB, (outgoing, project, finish))


def end_kernel(rows, cols, line, got_ref, field_in, gate_in, prepared, out_hbm, wide, out_ref, sems):
    lanes = SUB * cols
    out_t = prepared_parts(prepared)[-1]
    wide[: got_ref.shape[0], :] = got_ref[...].astype(F32)
    copies = []

    def outgoing(group, _):
        return output_of(wide, out_t, group, lanes, line)

    def finish(group, output):
        at = slice(group * lanes, (group + 1) * lanes)
        field = field_in[:, at] + (gate_in[:, at] * output + output)
        out_ref[at, :] = field.astype(BF16).T
        at = pl.ds(group * lanes, lanes)
        copies.append(pltpu.make_async_copy(out_ref.at[at], out_hbm.at[at], sems.at[group]))
        copies[-1].start()

    staged(rows // SUB, (outgoing, finish))
    for copy in copies:
        copy.wait()


def moved(source, moves, count):
    shape = None
    lane = None
    targets = [[] for _ in range(count)]
    for row, begin, length, target in moves:
        shift = (target - begin) % LANES
        while length > 0:
            size = min(length, LANES - begin % LANES, LANES - target % LANES)
            targets[target // LANES].append((target % LANES, row, begin // LANES, shift))
            begin, target, length = begin + size, target + size, length - size
    rolled = {}
    registers = []
    for pieces in targets:
        value = None
        for start, row, register, shift in sorted(pieces, key=lambda piece: piece[0]):
            key = (row, register, shift)
            if key not in rolled:
                tile = source(row, register)
                rolled[key] = pltpu.roll(tile, shift, 1) if shift else tile
            if value is None:
                value = rolled[key]
            else:
                if lane is None:
                    shape = value.shape
                    lane = lax.broadcasted_iota(jnp.int32, shape, 1)
                value = jnp.where(lane < start, value, rolled[key])
        registers.append(value)
    return registers


def wide_steps(tiles):
    place_step = tiles + 1 - tiles % 2
    return place_step, SUB * place_step + 1


def row_order(groups, row_devices, rows, width):
    line = lax.broadcasted_iota(jnp.int32, (groups * SUB * row_devices, 1), 0)
    row, rest = line % row_devices, line // row_devices
    paired = groups // 2 * 2
    pair, inside = rest // (2 * SUB), rest % (2 * SUB)
    of_pair = (2 * pair + inside % 2) * SUB + inside // 2
    place = jnp.where(rest < paired * SUB, of_pair, rest)
    lane = lax.broadcasted_iota(jnp.int32, (groups * SUB * row_devices, width), 1)
    return jnp.where(lane == row * rows + place, 1.0, 0.0).astype(BF16)


def stacked(low, high):
    return jnp.concatenate([low, high], axis=0).astype(BF16)


def prepare_weights(w_ref, wo_ref, share, prepared):
    parts = [*load_in_weights(w_ref[1], share), transposed(wo_ref[0], 0.5), transposed(wo_ref[1], 0.5)]
    prepared[...] = jnp.concatenate(parts, axis=0)


def prepared_parts(prepared):
    width = prepared.shape[1]
    cuts = [0, 2, 4, 5, 6, 7]
    return [prepared[low * width : high * width, :] for low, high in zip(cuts, cuts[1:])]


def triangle_kernel(direction, share, rows, cols, row_devices, col_devices, line, *refs):
    if direction == 0:
        got_ref, w_ref, wo_ref, sent_ref, prepared, *refs = refs
    else:
        got_ref, sent_ref, *refs = refs
    wide, left_ref, right_ref, even_ref, result_ref, packed = refs
    groups = rows // SUB
    pieces = SUB * cols // LANES
    total = row_devices * rows
    blocks = -(-total // LANES)
    pairs = -(-groups // 2)
    rest = total - (blocks - 1) * LANES
    tail = lax.broadcasted_iota(jnp.int32, (2 * SUB, LANES), 1) < rest
    place_step, row_step = wide_steps(col_devices * groups * pieces)
    pick = row_order(groups, row_devices, rows, blocks * LANES) if direction == 1 else None

    def spot(tile):
        device, number = divmod(tile, groups * pieces)
        col, row = divmod(device, row_devices)
        return row * row_step + col * groups * pieces + number

    def widen(pair):
        for unit in range(got_ref.shape[0] // (2 * SUB)):
            owners = [tile % (groups * pieces) // pieces // 2 for tile in (2 * unit, 2 * unit + 1)]
            if min(owners) != pair:
                continue
            both = got_ref[unit * 2 * SUB : (unit + 1) * 2 * SUB, :].astype(F32)
            for half in range(2):
                at = pl.ds(spot(2 * unit + half), SUB, stride=place_step)
                wide[at, :] = both[half * SUB : (half + 1) * SUB]

    def loaded(place, group, col, piece):
        start = place * place_step + (col * groups + group) * pieces + piece
        return wide[pl.ds(start, row_devices, stride=row_step), :]

    def spread(tiles, step, cleared):
        moves = [(col, step * cols, cols, col * cols) for col in range(col_devices)]
        registers = moved(lambda col, piece: tiles[col, piece], moves, blocks)
        if cleared:
            registers[-1] = jnp.where(tail, registers[-1], jnp.zeros_like(registers[-1]))
        return registers

    def put(target, spare, start, block, value):
        target[spare, start : start + 2 * SUB, block * LANES : (block + 1) * LANES] = value

    def put_even(spare, group, step, block, value):
        even_ref[spare, block, pl.ds(group * SUB + step, row_devices, stride=rows), :] = value

    def unpack(channel, only=range(pairs)):
        spare = channel % 2
        for pair in only:
            if 2 * pair + 1 < groups:
                unpack_pair(channel, spare, pair)
            else:
                unpack_last(channel, spare, 2 * pair)

    def unpack_pair(channel, spare, pair):
        for is_right, place in ((False, channel), (True, share + channel)):
            tiles = {}
            for col in range(col_devices):
                for piece in range(pieces):
                    tiles[col, piece] = stacked(
                        loaded(place, 2 * pair, col, piece), loaded(place, 2 * pair + 1, col, piece)
                    )
            for step in range(SUB):
                for block, register in enumerate(spread(tiles, step, direction == 0 and not is_right)):
                    if is_right and direction == 0:
                        both = register.astype(F32)
                        for half in range(2):
                            put_even(spare, 2 * pair + half, step, block, both[half * SUB : (half + 1) * SUB])
                    else:
                        target = right_ref if is_right else left_ref
                        put(target, spare, (pair * SUB + step) * 2 * SUB, block, register)

    def unpack_last(channel, spare, group):
        tiles = {}
        for col in range(col_devices):
            for piece in range(pieces):
                tiles[col, piece] = stacked(
                    loaded(channel, group, col, piece), loaded(share + channel, group, col, piece)
                )
        before = None
        for step in range(SUB):
            now = [register.astype(F32) for register in spread(tiles, step, direction == 0)]
            for block in range(blocks):
                if direction == 0:
                    put_even(spare, group, step, block, now[block][SUB:])
                if step % 2:
                    start = (group * SUB + step - 1) * SUB
                    put(left_ref, spare, start, block, stacked(before[block][:SUB], now[block][:SUB]))
                    if direction == 1:
                        put(right_ref, spare, start, block, stacked(before[block][SUB:], now[block][SUB:]))
            before = now

    def product(channel):
        spare = channel % 2
        if direction == 0:
            right = [even_ref[spare, block, 0:total].astype(BF16) for block in range(blocks)]
            right = jnp.concatenate(right, axis=1)
            summed = matmul(left_ref[spare], right, ((1,), (1,)))
        else:
            turned = matmul(pick, left_ref[spare], ((1,), (1,))).astype(BF16)
            summed = matmul(turned, right_ref[spare], ((1,), (0,)))
        for block in range(blocks):
            size = min(LANES, total - block * LANES)
            part = summed[:, block * LANES : block * LANES + size].astype(BF16)
            result_ref[channel, block, :, 0:size] = part

    def send(tiles, targets):
        for col in range(col_devices):
            moves = [(step, col * cols, cols, step * cols) for step in range(SUB)]
            registers = moved(lambda step, block: tiles[step, block], moves, pieces)
            for piece in range(pieces):
                both = registers[piece].astype(F32)
                for half, (channel, group) in enumerate(targets):
                    start = (col * row_devices * share + channel) * line + group * pieces + piece
                    packed[pl.ds(start, row_devices, stride=share * line), :] = (
                        both[half * SUB : (half + 1) * SUB]
                    )
        missing.difference_update(targets)

    missing = set((channel, group) for channel in range(share) for group in range(groups))
    waiting = list(range(sent_ref.shape[0] // (2 * SUB)))

    def finish():
        for unit in list(waiting):
            lines = range(unit * 2 * SUB, (unit + 1) * 2 * SUB)
            if any((at // line % share, at % line // pieces) in missing for at in lines):
                continue
            waiting.remove(unit)
            at = slice(unit * 2 * SUB, (unit + 1) * 2 * SUB)
            sent_ref[at, :] = packed[at, :].astype(BF16)

    def pack(channel):
        for pair in range(groups // 2):
            tiles = {}
            for step in range(SUB):
                for block in range(blocks):
                    start = (pair * SUB + step) * 2 * SUB
                    tiles[step, block] = result_ref[channel, block, start : start + 2 * SUB, :]
            send(tiles, [(channel, 2 * pair), (channel, 2 * pair + 1)])
        if groups % 2 and channel % 2:
            group = groups - 1
            tiles = {}
            for block in range(blocks):
                for step in range(0, SUB, 2):
                    start = (group * SUB + step) * SUB
                    low, high = [
                        result_ref[one, block, start : start + 2 * SUB, :].astype(F32)
                        for one in (channel - 1, channel)
                    ]
                    tiles[step, block] = stacked(low[:SUB], high[:SUB])
                    tiles[step + 1, block] = stacked(low[SUB:], high[SUB:])
            send(tiles, [(channel - 1, group), (channel, group)])

    widen(0)
    for pair in range(pairs):
        if pair + 1 < pairs:
            widen(pair + 1)
        elif direction == 0:
            prepare_weights(w_ref, wo_ref, share, prepared)
        unpack(0, [pair])
    for channel in range(share):
        product(channel)
        if channel > 0:
            pack(channel - 1)
        if channel + 1 < share:
            unpack(channel + 1)
        else:
            finish()
    pack(share - 1)
    finish()


def by_channels(pair, token_mask, chain_ids, chain_bias, in_weights, out_weights, row_devices, col_devices):
    rows, cols, width = pair.shape
    devices = row_devices * col_devices
    share = width // devices
    lanes = SUB * cols
    pieces = lanes // LANES
    groups = rows // SUB
    chunk = groups * pieces * SUB
    spots = rows * cols
    line = groups * pieces
    total = row_devices * rows
    blocks = -(-total // LANES)
    tall = groups * SUB * row_devices
    params = pltpu.CompilerParams(vmem_limit_bytes=40 * 1024 * 1024)
    whole = pl.BlockSpec(memory_space=pltpu.VMEM)
    far = pl.BlockSpec(memory_space=pltpu.HBM)

    sent_shape = jax.ShapeDtypeStruct((devices, groups, pieces * SUB, LANES), BF16)
    sum_shape = jax.ShapeDtypeStruct((devices * share * line, LANES), BF16)
    state_shape = jax.ShapeDtypeStruct((width, spots), F32)
    mask_shape = jax.ShapeDtypeStruct((1, spots), F32)
    prepared_shape = jax.ShapeDtypeStruct((7 * width, width), BF16)
    padded_sum = pltpu.VMEM((-(-(devices + 1) * share * line // SUB) * SUB, LANES), F32)

    def exchange(array, rows):
        shape = (devices, rows) if rows % SUB == 0 else (devices, rows * 2 // SUB, SUB // 2)
        split = array.reshape(*shape, LANES)
        return lax.all_to_all(split, ("col", "row"), 0, 0, tiled=True).reshape(devices * rows, LANES)

    def triangle(direction, sent, *weights):
        wide_rows = (row_devices + 1) * wide_steps(col_devices * groups * pieces)[1]
        summed, *prepared = pl.pallas_call(
            functools.partial(
                triangle_kernel, direction, share, rows, cols, row_devices, col_devices, line
            ),
            out_shape=[sum_shape] + [prepared_shape] * (len(weights) // 2),
            in_specs=[whole] * (1 + len(weights)),
            out_specs=[whole] * (1 + len(weights) // 2),
            scratch_shapes=[
                pltpu.VMEM((-(-wide_rows // SUB) * SUB, LANES), F32),
                pltpu.VMEM((2, tall, blocks * LANES), BF16),
                pltpu.VMEM((2, tall, blocks * LANES), BF16),
                pltpu.VMEM((2, blocks, total + rows, LANES), F32),
                pltpu.VMEM((share, blocks, tall, LANES), BF16),
                padded_sum,
            ],
            compiler_params=params,
            name="triangle",
        )(exchange(sent, chunk), *weights)
        return exchange(summed, share * line), *prepared

    flat_pair = pair.reshape(spots, width)
    sent, gate, field, mask = pl.pallas_call(
        functools.partial(start_kernel, share, rows, cols),
        out_shape=[sent_shape, state_shape, state_shape, mask_shape],
        in_specs=[far] * 5,
        out_specs=[whole] * 4,
        scratch_shapes=[
            pltpu.VMEM((spots, width), BF16),
            pltpu.VMEM(in_weights.shape[1:], BF16),
            pltpu.VMEM((1, width), F32),
            pltpu.VMEM((1,) + token_mask.shape, jnp.int32),
            pltpu.VMEM((1,) + chain_ids.shape, jnp.int32),
            pltpu.SemaphoreType.DMA((6,)),
        ],
        compiler_params=params,
        name="start",
    )(*[
        pltpu.with_memory_space_constraint(array, pltpu.HBM)
        for array in (token_mask, chain_ids, flat_pair, chain_bias, in_weights)
    ])
    got, prepared = triangle(0, sent, in_weights, out_weights)
    sent, gate, field = pl.pallas_call(
        functools.partial(middle_kernel, share, rows, cols, line),
        out_shape=[sent_shape, state_shape, state_shape],
        in_specs=[whole] * 5,
        out_specs=[whole] * 3,
        scratch_shapes=[padded_sum],
        compiler_params=params,
        name="middle",
    )(mask, got, field, gate, prepared)
    (got,) = triangle(1, sent)
    out = pl.pallas_call(
        functools.partial(end_kernel, rows, cols, line),
        out_shape=jax.ShapeDtypeStruct((spots, width), BF16),
        in_specs=[whole] * 4,
        out_specs=far,
        scratch_shapes=[
            padded_sum,
            pltpu.VMEM((spots, width), BF16),
            pltpu.SemaphoreType.DMA((groups,)),
        ],
        compiler_params=params,
        name="end",
    )(got, field, gate, prepared)
    return out.reshape(pair.shape)


def gated_inputs(field, weights, pair_mask):
    width = weights.shape[0]
    normed = layer_norm(field).astype(BF16)
    projected = jnp.einsum("ijc,cd->ijd", normed, weights, preferred_element_type=F32)
    first = (
        jax.nn.sigmoid(projected[..., :width])
        * projected[..., width : 2 * width]
        * pair_mask[:, :, None]
    ).astype(BF16)
    second = (
        jax.nn.sigmoid(projected[..., 2 * width : 3 * width])
        * projected[..., 3 * width : 4 * width]
        * pair_mask[:, :, None]
    ).astype(BF16)
    gate_value = jax.nn.sigmoid(projected[..., 4 * width :])
    return (first, second, gate_value)


def update(field, summed, gate_value, weights):
    normed_sum = layer_norm(summed).astype(BF16)
    output = jnp.einsum("ijc,cd->ijd", normed_sum, weights, preferred_element_type=F32)
    return field + gate_value * output


def by_blocks(pair, token_mask, chain_ids, chain_bias, in_weights, out_weights):
    row_count = pair.shape[0]
    col_count = pair.shape[1]
    row_start = lax.axis_index("row") * row_count
    col_start = lax.axis_index("col") * col_count
    valid_rows = lax.dynamic_slice_in_dim(token_mask, row_start, row_count).astype(F32)
    valid_cols = lax.dynamic_slice_in_dim(token_mask, col_start, col_count).astype(F32)
    chain_rows = lax.dynamic_slice_in_dim(chain_ids, row_start, row_count)
    chain_cols = lax.dynamic_slice_in_dim(chain_ids, col_start, col_count)
    pair_mask = valid_rows[:, None] * valid_cols[None, :]
    same_chain = (chain_rows[:, None] == chain_cols[None, :]).astype(F32)
    field = pair.astype(F32) + same_chain[:, :, None] * chain_bias
    first, second, gate_value = gated_inputs(field, in_weights[0], pair_mask)
    second_rows = lax.all_gather(second, "row", axis=0, tiled=True)
    part = jnp.einsum("jkc,ikc->jic", second_rows, first, preferred_element_type=F32).astype(BF16)
    summed = lax.psum_scatter(part, "col", scatter_dimension=0, tiled=True).astype(F32)
    summed = jnp.transpose(summed, (1, 0, 2))
    field = update(field, summed, gate_value, out_weights[0])
    first, second, gate_value = gated_inputs(field, in_weights[1], pair_mask)
    first_cols = lax.all_gather(first, "col", axis=1, tiled=True)
    part = jnp.einsum("kic,kjc->ijc", first_cols, second, preferred_element_type=F32).astype(BF16)
    summed = lax.psum_scatter(part, "row", scatter_dimension=0, tiled=True).astype(F32)
    field = update(field, summed, gate_value, out_weights[1])
    return field.astype(BF16)


def solution(mesh):
    row_devices, col_devices = mesh.shape["row"], mesh.shape["col"]

    def per_device(pair, *rest):
        rows, cols, width = pair.shape
        devices = row_devices * col_devices
        fits = (
            width % devices == 0
            and 2 * (width // devices) == SUB
            and row_devices == SUB
            and rows % SUB == 0
            and rows >= 3 * SUB
            and (SUB * cols) % LANES == 0
            and max(rows, cols) <= LANES
        )
        if fits:
            return by_channels(pair, *rest, row_devices, col_devices)
        return by_blocks(pair, *rest)

    return jax.shard_map(
        per_device,
        mesh=mesh,
        in_specs=(P("row", "col", None), P(), P(), P(), P(), P()),
        out_specs=P("row", "col", None),
        check_vma=False,
    )
```

```python
import functools

import jax
import jax.numpy as jnp
from jax import lax
from jax.experimental import pallas as pl
from jax.experimental.pallas import tpu as pltpu
from jax.sharding import PartitionSpec as P

LANES = 128
SUB = 8
F32 = jnp.float32
BF16 = jnp.bfloat16


def layer_norm(values, axis=-1):
    center = values - jnp.mean(values, axis=axis, keepdims=True)
    spread = jnp.mean(center * center, axis=axis, keepdims=True)
    return center * lax.rsqrt(spread + 1e-05)


def matmul(left, right, dims):
    return lax.dot_general(left, right, (dims, ((), ())), preferred_element_type=F32)


def identity(size, scale):
    row = lax.broadcasted_iota(jnp.int32, (size, size), 0)
    col = lax.broadcasted_iota(jnp.int32, (size, size), 1)
    return jnp.where(row == col, scale, 0.0).astype(BF16)


def column(row_ref):
    width = row_ref.shape[1]
    return jnp.broadcast_to(row_ref[...], (width, width)).T[:, 0:1]


def transposed(weights, scale):
    eye = identity(weights.shape[1], scale)
    return matmul(eye, weights, ((1,), (1,))).astype(BF16)


def interleaved(first, second, share):
    width = first.shape[1]
    both = jnp.concatenate([first, second], axis=1)
    row = lax.broadcasted_iota(jnp.int32, (2 * width, 1), 0)
    col = lax.broadcasted_iota(jnp.int32, (2 * width, 2 * width), 1)
    owner, place = row // (2 * share), row % (2 * share)
    source = owner * share + place % share + jnp.where(place >= share, width, 0)
    pick = jnp.where(col == source, 0.5, 0.0).astype(BF16)
    return matmul(pick, both, ((1,), (1,))).astype(BF16)


def load_in_weights(weights, share):
    width = weights.shape[0]
    blocks = [weights[:, k * width : (k + 1) * width] for k in range(5)]
    return (
        interleaved(blocks[0], blocks[2], share),
        interleaved(blocks[1], blocks[3], share),
        transposed(blocks[4], 0.5),
    )


def token_vectors(tokens, row_start, col_start, rows, cols):
    groups = rows // SUB
    wide = tokens.shape[1]
    many = jnp.broadcast_to(tokens.astype(F32), (SUB, wide))
    lane = lax.broadcasted_iota(jnp.int32, (1, SUB * cols), 1)
    at_row = jnp.zeros_like(lane)
    for step in range(1, SUB):
        at_row = at_row + jnp.where(lane >= step * cols, 1, 0)
    at_col = lane - at_row * cols
    key = lax.broadcasted_iota(jnp.int32, (LANES, SUB * cols), 0)
    pick_row = jnp.where(key == at_row, 1.0, 0.0).astype(BF16)
    pick_col = jnp.where(key == at_col, 1.0, 0.0).astype(BF16)

    def window(start):
        return pltpu.roll(many, wide - start, 1)[:, :LANES]

    by_col = matmul(window(col_start).astype(BF16), pick_col, ((1,), (0,)))[0:1]
    windows = [window(row_start + group * SUB)[0:1] for group in range(groups)]
    windows.append(jnp.zeros((-groups % SUB, LANES), F32))
    by_row = matmul(jnp.concatenate(windows, axis=0).astype(BF16), pick_row, ((1,), (0,)))
    by_row = by_row.astype(jnp.int32)
    by_col = by_col.astype(jnp.int32)
    masks = (by_row & by_col & 1).astype(F32)
    sames = jnp.where((by_row >> 1) == (by_col >> 1), 1.0, 0.0)
    return masks, sames


def staged(count, stages):
    held = {}
    for step in range(count + len(stages) - 1):
        for number, stage in enumerate(stages):
            item = step - number
            if 0 <= item < count:
                held[item] = stage(item, held.get(item))


def statistics(values):
    center = values - jnp.mean(values, axis=0, keepdims=True)
    spread = jnp.mean(center * center, axis=0, keepdims=True)
    return center, lax.rsqrt(spread + 1e-05)


def normalised(halves):
    center, scale = halves
    return (center * scale).astype(BF16)


def projected(halves, in_t):
    normed = normalised(halves)
    return [matmul(weights, normed, ((1,), (0,))) for weights in in_t]


def gated(products, mask, group, share, sent_ref, gate_ref):
    gates, values, gate = products
    width, lanes = gate.shape
    sent = (jnp.tanh(gates) * values + values) * mask
    for owner in range(width // share):
        block = sent[owner * 2 * share : (owner + 1) * 2 * share]
        lines = [block[:, at : at + LANES] for at in range(0, lanes, LANES)]
        sent_ref[owner, group] = jnp.concatenate(lines, axis=0).astype(BF16)
    gate_ref[:, group * lanes : (group + 1) * lanes] = jnp.tanh(gate)


def start_kernel(share, rows, cols, valid_hbm, chain_hbm, pair_hbm, bias_hbm, w_hbm,
                 sent_ref, gate_ref, field_ref, mask_ref,
                 pair_ref, w_ref, bias_ref, valid_ref, chain_ref, sems):
    lanes = SUB * cols
    groups = rows // SUB
    width = pair_ref.shape[1]
    count = valid_hbm.shape[0]
    started = []

    def copy(near, far):
        started.append(pltpu.make_async_copy(near, far, sems.at[len(started)]))
        started[-1].start()

    copy(w_hbm.at[0], w_ref)
    copy(valid_hbm, valid_ref.at[0])
    copy(chain_hbm, chain_ref.at[0])
    copy(bias_hbm, bias_ref.at[0])
    for at in (pl.ds(0, 2 * lanes), pl.ds(2 * lanes, (groups - 2) * lanes)):
        copy(pair_hbm.at[at], pair_ref.at[at])
    arriving = len(started)
    eye = identity(width, 1.0)
    row_start = lax.axis_index("row") * rows
    col_start = lax.axis_index("col") * cols
    started[0].wait()
    in_t = load_in_weights(w_ref[...], share)
    for number in range(1, arriving - 1):
        started[number].wait()

    def lift(group):
        if group == 2:
            started[arriving - 1].wait()
        rows_of = pair_ref[group * lanes : (group + 1) * lanes, :]
        return matmul(eye, rows_of, ((1,), (1,)))

    lifted = {0: lift(0)}
    tokens = chain_ref[...] * 2 + valid_ref[...]
    tokens = jnp.concatenate([tokens, jnp.zeros((1, -count % LANES), jnp.int32)], axis=1)
    masks, sames = token_vectors(tokens, row_start, col_start, rows, cols)
    bias_col = column(bias_ref)

    def make_field(group, _):
        at = slice(group * lanes, (group + 1) * lanes)
        if group + 1 < groups:
            lifted[group + 1] = lift(group + 1)
        field = lifted.pop(group) + bias_col * sames[group : group + 1]
        field_ref[:, at] = field
        mask_ref[:, at] = masks[group : group + 1]
        return statistics(field)

    def project(group, halves):
        return projected(halves, in_t)

    def finish(group, products):
        gated(products, masks[group : group + 1], group, share, sent_ref, gate_ref)

    staged(groups, (make_field, project, finish))


def received(wide, width, group, lanes, line):
    pieces = lanes // LANES
    parts = []
    for piece in range(pieces):
        parts.append(wide[pl.ds(group * pieces + piece, width, stride=line), :])
    return statistics(jnp.concatenate(parts, axis=1))


def middle_kernel(share, rows, cols, line, mask_ref, got_ref, field_in, gate_in, prepared,
                  sent_ref, gate_ref, field_ref, wide):
    lanes = SUB * cols
    *in_t, out_t, _ = prepared_parts(prepared)
    wide[: got_ref.shape[0], :] = got_ref[...].astype(F32)

    def span(group):
        return slice(group * lanes, (group + 1) * lanes)

    def receive(group, _):
        return received(wide, out_t.shape[1], group, lanes, line)

    def outgoing(group, halves):
        return matmul(out_t, normalised(halves), ((1,), (0,)))

    def update_field(group, output):
        at = span(group)
        field = field_in[:, at] + (gate_in[:, at] * output + output)
        field_ref[:, at] = field
        return statistics(field)

    def project(group, halves):
        return projected(halves, in_t)

    def finish(group, products):
        gated(products, mask_ref[:, span(group)], group, share, sent_ref, gate_ref)

    staged(rows // SUB, (receive, outgoing, update_field, project, finish))


def end_kernel(rows, cols, line, got_ref, field_in, gate_in, prepared, out_hbm, wide, out_ref, sems):
    lanes = SUB * cols
    out_t = prepared_parts(prepared)[-1]
    wide[: got_ref.shape[0], :] = got_ref[...].astype(F32)
    copies = []

    def receive(group, _):
        return received(wide, out_t.shape[1], group, lanes, line)

    def outgoing(group, halves):
        return matmul(out_t, normalised(halves), ((1,), (0,)))

    def finish(group, output):
        at = slice(group * lanes, (group + 1) * lanes)
        field = field_in[:, at] + (gate_in[:, at] * output + output)
        out_ref[at, :] = field.astype(BF16).T
        at = pl.ds(group * lanes, lanes)
        copies.append(pltpu.make_async_copy(out_ref.at[at], out_hbm.at[at], sems.at[group]))
        copies[-1].start()

    staged(rows // SUB, (receive, outgoing, finish))
    for copy in copies:
        copy.wait()


def moved(source, moves, count):
    shape = None
    lane = None
    targets = [[] for _ in range(count)]
    for row, begin, length, target in moves:
        shift = (target - begin) % LANES
        while length > 0:
            size = min(length, LANES - begin % LANES, LANES - target % LANES)
            targets[target // LANES].append((target % LANES, row, begin // LANES, shift))
            begin, target, length = begin + size, target + size, length - size
    rolled = {}
    registers = []
    for pieces in targets:
        value = None
        for start, row, register, shift in sorted(pieces, key=lambda piece: piece[0]):
            key = (row, register, shift)
            if key not in rolled:
                tile = source(row, register)
                rolled[key] = pltpu.roll(tile, shift, 1) if shift else tile
            if value is None:
                value = rolled[key]
            else:
                if lane is None:
                    shape = value.shape
                    lane = lax.broadcasted_iota(jnp.int32, shape, 1)
                value = jnp.where(lane < start, value, rolled[key])
        registers.append(value)
    return registers


def wide_steps(tiles):
    place_step = tiles + 1 - tiles % 2
    return place_step, SUB * place_step + 1


def row_order(groups, row_devices, rows, width):
    line = lax.broadcasted_iota(jnp.int32, (groups * SUB * row_devices, 1), 0)
    row, rest = line % row_devices, line // row_devices
    paired = groups // 2 * 2
    pair, inside = rest // (2 * SUB), rest % (2 * SUB)
    of_pair = (2 * pair + inside % 2) * SUB + inside // 2
    place = jnp.where(rest < paired * SUB, of_pair, rest)
    lane = lax.broadcasted_iota(jnp.int32, (groups * SUB * row_devices, width), 1)
    return jnp.where(lane == row * rows + place, 1.0, 0.0).astype(BF16)


def stacked(low, high):
    return jnp.concatenate([low, high], axis=0).astype(BF16)


def prepare_weights(w_ref, wo_ref, share, prepared):
    parts = [*load_in_weights(w_ref[1], share), transposed(wo_ref[0], 0.5), transposed(wo_ref[1], 0.5)]
    prepared[...] = jnp.concatenate(parts, axis=0)


def prepared_parts(prepared):
    width = prepared.shape[1]
    cuts = [0, 2, 4, 5, 6, 7]
    return [prepared[low * width : high * width, :] for low, high in zip(cuts, cuts[1:])]


def triangle_kernel(direction, share, rows, cols, row_devices, col_devices, line, *refs):
    if direction == 0:
        got_ref, w_ref, wo_ref, sent_ref, prepared, *refs = refs
    else:
        got_ref, sent_ref, *refs = refs
    wide, left_ref, right_ref, even_ref, result_ref, packed = refs
    groups = rows // SUB
    pieces = SUB * cols // LANES
    total = row_devices * rows
    blocks = -(-total // LANES)
    pairs = -(-groups // 2)
    rest = total - (blocks - 1) * LANES
    tail = lax.broadcasted_iota(jnp.int32, (2 * SUB, LANES), 1) < rest
    place_step, row_step = wide_steps(col_devices * groups * pieces)
    pick = row_order(groups, row_devices, rows, blocks * LANES) if direction == 1 else None

    def spot(tile):
        device, number = divmod(tile, groups * pieces)
        col, row = divmod(device, row_devices)
        return row * row_step + col * groups * pieces + number

    def widen(pair):
        for unit in range(got_ref.shape[0] // (2 * SUB)):
            owners = [tile % (groups * pieces) // pieces // 2 for tile in (2 * unit, 2 * unit + 1)]
            if min(owners) != pair:
                continue
            both = got_ref[unit * 2 * SUB : (unit + 1) * 2 * SUB, :].astype(F32)
            for half in range(2):
                at = pl.ds(spot(2 * unit + half), SUB, stride=place_step)
                wide[at, :] = both[half * SUB : (half + 1) * SUB]

    def loaded(place, group, col, piece):
        start = place * place_step + (col * groups + group) * pieces + piece
        return wide[pl.ds(start, row_devices, stride=row_step), :]

    def spread(tiles, step, cleared):
        moves = [(col, step * cols, cols, col * cols) for col in range(col_devices)]
        registers = moved(lambda col, piece: tiles[col, piece], moves, blocks)
        if cleared:
            registers[-1] = jnp.where(tail, registers[-1], jnp.zeros_like(registers[-1]))
        return registers

    def put(target, spare, start, block, value):
        target[spare, start : start + 2 * SUB, block * LANES : (block + 1) * LANES] = value

    def put_even(spare, group, step, block, value):
        even_ref[spare, block, pl.ds(group * SUB + step, row_devices, stride=rows), :] = value

    def unpack(channel, only=range(pairs)):
        spare = channel % 2
        for pair in only:
            if 2 * pair + 1 < groups:
                unpack_pair(channel, spare, pair)
            else:
                unpack_last(channel, spare, 2 * pair)

    def unpack_pair(channel, spare, pair):
        for is_right, place in ((False, channel), (True, share + channel)):
            tiles = {}
            for col in range(col_devices):
                for piece in range(pieces):
                    tiles[col, piece] = stacked(
                        loaded(place, 2 * pair, col, piece), loaded(place, 2 * pair + 1, col, piece)
                    )
            for step in range(SUB):
                for block, register in enumerate(spread(tiles, step, direction == 0 and not is_right)):
                    if is_right and direction == 0:
                        both = register.astype(F32)
                        for half in range(2):
                            put_even(spare, 2 * pair + half, step, block, both[half * SUB : (half + 1) * SUB])
                    else:
                        target = right_ref if is_right else left_ref
                        put(target, spare, (pair * SUB + step) * 2 * SUB, block, register)

    def unpack_last(channel, spare, group):
        tiles = {}
        for col in range(col_devices):
            for piece in range(pieces):
                tiles[col, piece] = stacked(
                    loaded(channel, group, col, piece), loaded(share + channel, group, col, piece)
                )
        before = None
        for step in range(SUB):
            now = [register.astype(F32) for register in spread(tiles, step, direction == 0)]
            for block in range(blocks):
                if direction == 0:
                    put_even(spare, group, step, block, now[block][SUB:])
                if step % 2:
                    start = (group * SUB + step - 1) * SUB
                    put(left_ref, spare, start, block, stacked(before[block][:SUB], now[block][:SUB]))
                    if direction == 1:
                        put(right_ref, spare, start, block, stacked(before[block][SUB:], now[block][SUB:]))
            before = now

    def product(channel):
        spare = channel % 2
        if direction == 0:
            right = [even_ref[spare, block, 0:total].astype(BF16) for block in range(blocks)]
            right = jnp.concatenate(right, axis=1)
            summed = matmul(left_ref[spare], right, ((1,), (1,)))
        else:
            turned = matmul(pick, left_ref[spare], ((1,), (1,))).astype(BF16)
            summed = matmul(turned, right_ref[spare], ((1,), (0,)))
        for block in range(blocks):
            size = min(LANES, total - block * LANES)
            part = summed[:, block * LANES : block * LANES + size].astype(BF16)
            result_ref[channel, block, :, 0:size] = part

    def send(tiles, targets):
        for col in range(col_devices):
            moves = [(step, col * cols, cols, step * cols) for step in range(SUB)]
            registers = moved(lambda step, block: tiles[step, block], moves, pieces)
            for piece in range(pieces):
                both = registers[piece].astype(F32)
                for half, (channel, group) in enumerate(targets):
                    start = (col * row_devices * share + channel) * line + group * pieces + piece
                    packed[pl.ds(start, row_devices, stride=share * line), :] = (
                        both[half * SUB : (half + 1) * SUB]
                    )
        missing.difference_update(targets)

    missing = set((channel, group) for channel in range(share) for group in range(groups))
    waiting = list(range(sent_ref.shape[0] // (2 * SUB)))

    def finish():
        for unit in list(waiting):
            lines = range(unit * 2 * SUB, (unit + 1) * 2 * SUB)
            if any((at // line % share, at % line // pieces) in missing for at in lines):
                continue
            waiting.remove(unit)
            at = slice(unit * 2 * SUB, (unit + 1) * 2 * SUB)
            sent_ref[at, :] = packed[at, :].astype(BF16)

    def pack(channel):
        for pair in range(groups // 2):
            tiles = {}
            for step in range(SUB):
                for block in range(blocks):
                    start = (pair * SUB + step) * 2 * SUB
                    tiles[step, block] = result_ref[channel, block, start : start + 2 * SUB, :]
            send(tiles, [(channel, 2 * pair), (channel, 2 * pair + 1)])
        if groups % 2 and channel % 2:
            group = groups - 1
            tiles = {}
            for block in range(blocks):
                for step in range(0, SUB, 2):
                    start = (group * SUB + step) * SUB
                    low, high = [
                        result_ref[one, block, start : start + 2 * SUB, :].astype(F32)
                        for one in (channel - 1, channel)
                    ]
                    tiles[step, block] = stacked(low[:SUB], high[:SUB])
                    tiles[step + 1, block] = stacked(low[SUB:], high[SUB:])
            send(tiles, [(channel - 1, group), (channel, group)])

    widen(0)
    for pair in range(pairs):
        if pair + 1 < pairs:
            widen(pair + 1)
        elif direction == 0:
            prepare_weights(w_ref, wo_ref, share, prepared)
        unpack(0, [pair])
    for channel in range(share):
        product(channel)
        if channel > 0:
            pack(channel - 1)
        if channel + 1 < share:
            unpack(channel + 1)
        else:
            finish()
    pack(share - 1)
    finish()


def by_channels(pair, token_mask, chain_ids, chain_bias, in_weights, out_weights, row_devices, col_devices):
    rows, cols, width = pair.shape
    devices = row_devices * col_devices
    share = width // devices
    lanes = SUB * cols
    pieces = lanes // LANES
    groups = rows // SUB
    chunk = groups * pieces * SUB
    spots = rows * cols
    line = groups * pieces
    total = row_devices * rows
    blocks = -(-total // LANES)
    tall = groups * SUB * row_devices
    params = pltpu.CompilerParams(vmem_limit_bytes=40 * 1024 * 1024)
    whole = pl.BlockSpec(memory_space=pltpu.VMEM)
    far = pl.BlockSpec(memory_space=pltpu.HBM)

    sent_shape = jax.ShapeDtypeStruct((devices, groups, pieces * SUB, LANES), BF16)
    sum_shape = jax.ShapeDtypeStruct((devices * share * line, LANES), BF16)
    state_shape = jax.ShapeDtypeStruct((width, spots), F32)
    mask_shape = jax.ShapeDtypeStruct((1, spots), F32)
    prepared_shape = jax.ShapeDtypeStruct((7 * width, width), BF16)
    padded_sum = pltpu.VMEM((-(-(devices + 1) * share * line // SUB) * SUB, LANES), F32)

    def exchange(array, rows):
        shape = (devices, rows) if rows % SUB == 0 else (devices, rows * 2 // SUB, SUB // 2)
        split = array.reshape(*shape, LANES)
        return lax.all_to_all(split, ("col", "row"), 0, 0, tiled=True).reshape(devices * rows, LANES)

    def triangle(direction, sent, *weights):
        wide_rows = (row_devices + 1) * wide_steps(col_devices * groups * pieces)[1]
        summed, *prepared = pl.pallas_call(
            functools.partial(
                triangle_kernel, direction, share, rows, cols, row_devices, col_devices, line
            ),
            out_shape=[sum_shape] + [prepared_shape] * (len(weights) // 2),
            in_specs=[whole] * (1 + len(weights)),
            out_specs=[whole] * (1 + len(weights) // 2),
            scratch_shapes=[
                pltpu.VMEM((-(-wide_rows // SUB) * SUB, LANES), F32),
                pltpu.VMEM((2, tall, blocks * LANES), BF16),
                pltpu.VMEM((2, tall, blocks * LANES), BF16),
                pltpu.VMEM((2, blocks, total + rows, LANES), F32),
                pltpu.VMEM((share, blocks, tall, LANES), BF16),
                padded_sum,
            ],
            compiler_params=params,
            name="triangle",
        )(exchange(sent, chunk), *weights)
        return exchange(summed, share * line), *prepared

    flat_pair = pair.reshape(spots, width)
    sent, gate, field, mask = pl.pallas_call(
        functools.partial(start_kernel, share, rows, cols),
        out_shape=[sent_shape, state_shape, state_shape, mask_shape],
        in_specs=[far] * 5,
        out_specs=[whole] * 4,
        scratch_shapes=[
            pltpu.VMEM((spots, width), BF16),
            pltpu.VMEM(in_weights.shape[1:], BF16),
            pltpu.VMEM((1, width), F32),
            pltpu.VMEM((1,) + token_mask.shape, jnp.int32),
            pltpu.VMEM((1,) + chain_ids.shape, jnp.int32),
            pltpu.SemaphoreType.DMA((6,)),
        ],
        compiler_params=params,
        name="start",
    )(*[
        pltpu.with_memory_space_constraint(array, pltpu.HBM)
        for array in (token_mask, chain_ids, flat_pair, chain_bias, in_weights)
    ])
    got, prepared = triangle(0, sent, in_weights, out_weights)
    sent, gate, field = pl.pallas_call(
        functools.partial(middle_kernel, share, rows, cols, line),
        out_shape=[sent_shape, state_shape, state_shape],
        in_specs=[whole] * 5,
        out_specs=[whole] * 3,
        scratch_shapes=[padded_sum],
        compiler_params=params,
        name="middle",
    )(mask, got, field, gate, prepared)
    (got,) = triangle(1, sent)
    out = pl.pallas_call(
        functools.partial(end_kernel, rows, cols, line),
        out_shape=jax.ShapeDtypeStruct((spots, width), BF16),
        in_specs=[whole] * 4,
        out_specs=far,
        scratch_shapes=[
            padded_sum,
            pltpu.VMEM((spots, width), BF16),
            pltpu.SemaphoreType.DMA((groups,)),
        ],
        compiler_params=params,
        name="end",
    )(got, field, gate, prepared)
    return out.reshape(pair.shape)


def gated_inputs(field, weights, pair_mask):
    width = weights.shape[0]
    normed = layer_norm(field).astype(BF16)
    projected = jnp.einsum("ijc,cd->ijd", normed, weights, preferred_element_type=F32)
    first = (
        jax.nn.sigmoid(projected[..., :width])
        * projected[..., width : 2 * width]
        * pair_mask[:, :, None]
    ).astype(BF16)
    second = (
        jax.nn.sigmoid(projected[..., 2 * width : 3 * width])
        * projected[..., 3 * width : 4 * width]
        * pair_mask[:, :, None]
    ).astype(BF16)
    gate_value = jax.nn.sigmoid(projected[..., 4 * width :])
    return (first, second, gate_value)


def update(field, summed, gate_value, weights):
    normed_sum = layer_norm(summed).astype(BF16)
    output = jnp.einsum("ijc,cd->ijd", normed_sum, weights, preferred_element_type=F32)
    return field + gate_value * output


def by_blocks(pair, token_mask, chain_ids, chain_bias, in_weights, out_weights):
    row_count = pair.shape[0]
    col_count = pair.shape[1]
    row_start = lax.axis_index("row") * row_count
    col_start = lax.axis_index("col") * col_count
    valid_rows = lax.dynamic_slice_in_dim(token_mask, row_start, row_count).astype(F32)
    valid_cols = lax.dynamic_slice_in_dim(token_mask, col_start, col_count).astype(F32)
    chain_rows = lax.dynamic_slice_in_dim(chain_ids, row_start, row_count)
    chain_cols = lax.dynamic_slice_in_dim(chain_ids, col_start, col_count)
    pair_mask = valid_rows[:, None] * valid_cols[None, :]
    same_chain = (chain_rows[:, None] == chain_cols[None, :]).astype(F32)
    field = pair.astype(F32) + same_chain[:, :, None] * chain_bias
    first, second, gate_value = gated_inputs(field, in_weights[0], pair_mask)
    second_rows = lax.all_gather(second, "row", axis=0, tiled=True)
    part = jnp.einsum("jkc,ikc->jic", second_rows, first, preferred_element_type=F32).astype(BF16)
    summed = lax.psum_scatter(part, "col", scatter_dimension=0, tiled=True).astype(F32)
    summed = jnp.transpose(summed, (1, 0, 2))
    field = update(field, summed, gate_value, out_weights[0])
    first, second, gate_value = gated_inputs(field, in_weights[1], pair_mask)
    first_cols = lax.all_gather(first, "col", axis=1, tiled=True)
    part = jnp.einsum("kic,kjc->ijc", first_cols, second, preferred_element_type=F32).astype(BF16)
    summed = lax.psum_scatter(part, "row", scatter_dimension=0, tiled=True).astype(F32)
    field = update(field, summed, gate_value, out_weights[1])
    return field.astype(BF16)


def solution(mesh):
    row_devices, col_devices = mesh.shape["row"], mesh.shape["col"]

    def per_device(pair, *rest):
        rows, cols, width = pair.shape
        devices = row_devices * col_devices
        fits = (
            width % devices == 0
            and 2 * (width // devices) == SUB
            and row_devices == SUB
            and rows % SUB == 0
            and rows >= 3 * SUB
            and (SUB * cols) % LANES == 0
            and max(rows, cols) <= LANES
        )
        if fits:
            return by_channels(pair, *rest, row_devices, col_devices)
        return by_blocks(pair, *rest)

    return jax.shard_map(
        per_device,
        mesh=mesh,
        in_specs=(P("row", "col", None), P(), P(), P(), P(), P()),
        out_specs=P("row", "col", None),
        check_vma=False,
    )
```

```python
import functools

import jax
import jax.numpy as jnp
from jax import lax
from jax.experimental import pallas as pl
from jax.experimental.pallas import tpu as pltpu
from jax.sharding import PartitionSpec as P

LANES = 128
SUB = 8
F32 = jnp.float32
BF16 = jnp.bfloat16


def layer_norm(values, axis=-1):
    center = values - jnp.mean(values, axis=axis, keepdims=True)
    spread = jnp.mean(center * center, axis=axis, keepdims=True)
    return center * lax.rsqrt(spread + 1e-05)


def matmul(left, right, dims):
    return lax.dot_general(left, right, (dims, ((), ())), preferred_element_type=F32)


def identity(size, scale):
    row = lax.broadcasted_iota(jnp.int32, (size, size), 0)
    col = lax.broadcasted_iota(jnp.int32, (size, size), 1)
    return jnp.where(row == col, scale, 0.0).astype(BF16)


def column(row_ref):
    width = row_ref.shape[1]
    return jnp.broadcast_to(row_ref[...], (width, width)).T[:, 0:1]


def transposed(weights, scale):
    eye = identity(weights.shape[1], scale)
    return matmul(eye, weights, ((1,), (1,))).astype(BF16)


def interleaved(first, second, share):
    width = first.shape[1]
    both = jnp.concatenate([first, second], axis=1)
    row = lax.broadcasted_iota(jnp.int32, (2 * width, 1), 0)
    col = lax.broadcasted_iota(jnp.int32, (2 * width, 2 * width), 1)
    owner, place = row // (2 * share), row % (2 * share)
    source = owner * share + place % share + jnp.where(place >= share, width, 0)
    pick = jnp.where(col == source, 0.5, 0.0).astype(BF16)
    return matmul(pick, both, ((1,), (1,))).astype(BF16)


def load_in_weights(weights, share):
    width = weights.shape[0]
    blocks = [weights[:, k * width : (k + 1) * width] for k in range(5)]
    return (
        interleaved(blocks[0], blocks[2], share),
        interleaved(blocks[1], blocks[3], share),
        transposed(blocks[4], 0.5),
    )


def token_vectors(tokens, row_start, col_start, rows, cols):
    groups = rows // SUB
    wide = tokens.shape[1]
    many = jnp.broadcast_to(tokens.astype(F32), (SUB, wide))
    lane = lax.broadcasted_iota(jnp.int32, (1, SUB * cols), 1)
    at_row = jnp.zeros_like(lane)
    for step in range(1, SUB):
        at_row = at_row + jnp.where(lane >= step * cols, 1, 0)
    at_col = lane - at_row * cols
    key = lax.broadcasted_iota(jnp.int32, (LANES, SUB * cols), 0)
    pick_row = jnp.where(key == at_row, 1.0, 0.0).astype(BF16)
    pick_col = jnp.where(key == at_col, 1.0, 0.0).astype(BF16)

    def window(start):
        return pltpu.roll(many, wide - start, 1)[:, :LANES]

    by_col = matmul(window(col_start).astype(BF16), pick_col, ((1,), (0,)))[0:1]
    windows = [window(row_start + group * SUB)[0:1] for group in range(groups)]
    windows.append(jnp.zeros((-groups % SUB, LANES), F32))
    by_row = matmul(jnp.concatenate(windows, axis=0).astype(BF16), pick_row, ((1,), (0,)))
    by_row = by_row.astype(jnp.int32)
    by_col = by_col.astype(jnp.int32)
    masks = (by_row & by_col & 1).astype(F32)
    sames = jnp.where((by_row >> 1) == (by_col >> 1), 1.0, 0.0)
    return masks, sames


def staged(count, stages):
    held = {}
    for step in range(count + len(stages) - 1):
        for number, stage in enumerate(stages):
            item = step - number
            if 0 <= item < count:
                held[item] = stage(item, held.get(item))


def projected(field, in_t):
    normed = layer_norm(field, 0).astype(BF16)
    return [matmul(weights, normed, ((1,), (0,))) for weights in in_t]


def gated(products, mask, group, share, sent_ref, gate_ref):
    gates, values, gate = products
    width, lanes = gate.shape
    sent = (jnp.tanh(gates) * values + values) * mask
    for owner in range(width // share):
        block = sent[owner * 2 * share : (owner + 1) * 2 * share]
        lines = [block[:, at : at + LANES] for at in range(0, lanes, LANES)]
        sent_ref[owner, group] = jnp.concatenate(lines, axis=0).astype(BF16)
    gate_ref[:, group * lanes : (group + 1) * lanes] = jnp.tanh(gate)


def start_kernel(share, rows, cols, valid_hbm, chain_hbm, pair_hbm, bias_hbm, w_hbm,
                 sent_ref, gate_ref, field_ref, mask_ref,
                 pair_ref, w_ref, bias_ref, valid_ref, chain_ref, sems):
    lanes = SUB * cols
    groups = rows // SUB
    width = pair_ref.shape[1]
    count = valid_hbm.shape[0]
    started = []

    def copy(near, far):
        started.append(pltpu.make_async_copy(near, far, sems.at[len(started)]))
        started[-1].start()

    copy(w_hbm.at[0], w_ref)
    copy(valid_hbm, valid_ref.at[0])
    copy(chain_hbm, chain_ref.at[0])
    copy(bias_hbm, bias_ref.at[0])
    for at in (pl.ds(0, 2 * lanes), pl.ds(2 * lanes, (groups - 2) * lanes)):
        copy(pair_hbm.at[at], pair_ref.at[at])
    arriving = len(started)
    eye = identity(width, 1.0)
    row_start = lax.axis_index("row") * rows
    col_start = lax.axis_index("col") * cols
    started[0].wait()
    in_t = load_in_weights(w_ref[...], share)
    for number in range(1, arriving - 1):
        started[number].wait()

    def lift(group):
        if group == 2:
            started[arriving - 1].wait()
        rows_of = pair_ref[group * lanes : (group + 1) * lanes, :]
        return matmul(eye, rows_of, ((1,), (1,)))

    lifted = {0: lift(0)}
    tokens = chain_ref[...] * 2 + valid_ref[...]
    tokens = jnp.concatenate([tokens, jnp.zeros((1, -count % LANES), jnp.int32)], axis=1)
    masks, sames = token_vectors(tokens, row_start, col_start, rows, cols)
    bias_col = column(bias_ref)

    def make_field(group, _):
        at = slice(group * lanes, (group + 1) * lanes)
        if group + 1 < groups:
            lifted[group + 1] = lift(group + 1)
        field = lifted.pop(group) + bias_col * sames[group : group + 1]
        field_ref[:, at] = field
        mask_ref[:, at] = masks[group : group + 1]
        return field

    def project(group, field):
        return projected(field, in_t)

    def finish(group, products):
        gated(products, masks[group : group + 1], group, share, sent_ref, gate_ref)

    staged(groups, (make_field, project, finish))


def output_of(wide, out_t, group, lanes, line):
    width = out_t.shape[1]
    pieces = lanes // LANES
    parts = []
    for piece in range(pieces):
        parts.append(wide[pl.ds(group * pieces + piece, width, stride=line), :])
    normed = layer_norm(jnp.concatenate(parts, axis=1), 0).astype(BF16)
    return matmul(out_t, normed, ((1,), (0,)))


def middle_kernel(share, rows, cols, line, mask_ref, got_ref, field_in, gate_in, prepared,
                  sent_ref, gate_ref, field_ref, wide):
    lanes = SUB * cols
    *in_t, out_t, _ = prepared_parts(prepared)
    wide[: got_ref.shape[0], :] = got_ref[...].astype(F32)

    def span(group):
        return slice(group * lanes, (group + 1) * lanes)

    def outgoing(group, _):
        return output_of(wide, out_t, group, lanes, line)

    def project(group, output):
        at = span(group)
        field = field_in[:, at] + (gate_in[:, at] * output + output)
        field_ref[:, at] = field
        return projected(field, in_t)

    def finish(group, products):
        gated(products, mask_ref[:, span(group)], group, share, sent_ref, gate_ref)

    staged(rows // SUB, (outgoing, project, finish))


def end_kernel(rows, cols, line, got_ref, field_in, gate_in, prepared, out_hbm, wide, out_ref, sems):
    lanes = SUB * cols
    out_t = prepared_parts(prepared)[-1]
    wide[: got_ref.shape[0], :] = got_ref[...].astype(F32)
    copies = []

    def outgoing(group, _):
        return output_of(wide, out_t, group, lanes, line)

    def finish(group, output):
        at = slice(group * lanes, (group + 1) * lanes)
        field = field_in[:, at] + (gate_in[:, at] * output + output)
        out_ref[at, :] = field.astype(BF16).T
        at = pl.ds(group * lanes, lanes)
        copies.append(pltpu.make_async_copy(out_ref.at[at], out_hbm.at[at], sems.at[group]))
        copies[-1].start()

    staged(rows // SUB, (outgoing, finish))
    for copy in copies:
        copy.wait()


def moved(source, moves, count):
    shape = None
    lane = None
    targets = [[] for _ in range(count)]
    for row, begin, length, target in moves:
        shift = (target - begin) % LANES
        while length > 0:
            size = min(length, LANES - begin % LANES, LANES - target % LANES)
            targets[target // LANES].append((target % LANES, row, begin // LANES, shift))
            begin, target, length = begin + size, target + size, length - size
    rolled = {}
    registers = []
    for pieces in targets:
        value = None
        for start, row, register, shift in sorted(pieces, key=lambda piece: piece[0]):
            key = (row, register, shift)
            if key not in rolled:
                tile = source(row, register)
                rolled[key] = pltpu.roll(tile, shift, 1) if shift else tile
            if value is None:
                value = rolled[key]
            else:
                if lane is None:
                    shape = value.shape
                    lane = lax.broadcasted_iota(jnp.int32, shape, 1)
                value = jnp.where(lane < start, value, rolled[key])
        registers.append(value)
    return registers


def wide_steps(tiles):
    place_step = tiles + 1 - tiles % 2
    return place_step, SUB * place_step + 1


def row_order(groups, row_devices, rows, width):
    line = lax.broadcasted_iota(jnp.int32, (groups * SUB * row_devices, 1), 0)
    row, rest = line % row_devices, line // row_devices
    paired = groups // 2 * 2
    pair, inside = rest // (2 * SUB), rest % (2 * SUB)
    of_pair = (2 * pair + inside % 2) * SUB + inside // 2
    place = jnp.where(rest < paired * SUB, of_pair, rest)
    lane = lax.broadcasted_iota(jnp.int32, (groups * SUB * row_devices, width), 1)
    return jnp.where(lane == row * rows + place, 1.0, 0.0).astype(BF16)


def stacked(low, high):
    return jnp.concatenate([low, high], axis=0).astype(BF16)


def prepare_weights(w_ref, wo_ref, share, prepared):
    parts = [*load_in_weights(w_ref[1], share), transposed(wo_ref[0], 0.5), transposed(wo_ref[1], 0.5)]
    prepared[...] = jnp.concatenate(parts, axis=0)


def prepared_parts(prepared):
    width = prepared.shape[1]
    cuts = [0, 2, 4, 5, 6, 7]
    return [prepared[low * width : high * width, :] for low, high in zip(cuts, cuts[1:])]


def triangle_kernel(direction, share, rows, cols, row_devices, col_devices, line, *refs):
    if direction == 0:
        got_ref, w_ref, wo_ref, sent_ref, prepared, *refs = refs
    else:
        got_ref, sent_ref, *refs = refs
    wide, left_ref, right_ref, even_ref, result_ref, packed = refs
    groups = rows // SUB
    pieces = SUB * cols // LANES
    total = row_devices * rows
    blocks = -(-total // LANES)
    pairs = -(-groups // 2)
    rest = total - (blocks - 1) * LANES
    tail = lax.broadcasted_iota(jnp.int32, (2 * SUB, LANES), 1) < rest
    place_step, row_step = wide_steps(col_devices * groups * pieces)
    pick = row_order(groups, row_devices, rows, blocks * LANES) if direction == 1 else None

    def spot(tile):
        device, number = divmod(tile, groups * pieces)
        col, row = divmod(device, row_devices)
        return row * row_step + col * groups * pieces + number

    def widen(pair):
        for unit in range(got_ref.shape[0] // (2 * SUB)):
            owners = [tile % (groups * pieces) // pieces // 2 for tile in (2 * unit, 2 * unit + 1)]
            if min(owners) != pair:
                continue
            both = got_ref[unit * 2 * SUB : (unit + 1) * 2 * SUB, :].astype(F32)
            for half in range(2):
                at = pl.ds(spot(2 * unit + half), SUB, stride=place_step)
                wide[at, :] = both[half * SUB : (half + 1) * SUB]

    def loaded(place, group, col, piece):
        start = place * place_step + (col * groups + group) * pieces + piece
        return wide[pl.ds(start, row_devices, stride=row_step), :]

    def spread(tiles, step, cleared):
        moves = [(col, step * cols, cols, col * cols) for col in range(col_devices)]
        registers = moved(lambda col, piece: tiles[col, piece], moves, blocks)
        if cleared:
            registers[-1] = jnp.where(tail, registers[-1], jnp.zeros_like(registers[-1]))
        return registers

    def put(target, spare, start, block, value):
        target[spare, start : start + 2 * SUB, block * LANES : (block + 1) * LANES] = value

    def put_even(spare, group, step, block, value):
        even_ref[spare, block, pl.ds(group * SUB + step, row_devices, stride=rows), :] = value

    def unpack(channel, only=range(pairs)):
        spare = channel % 2
        for pair in only:
            if 2 * pair + 1 < groups:
                unpack_pair(channel, spare, pair)
            else:
                unpack_last(channel, spare, 2 * pair)

    def unpack_pair(channel, spare, pair):
        for is_right, place in ((False, channel), (True, share + channel)):
            tiles = {}
            for col in range(col_devices):
                for piece in range(pieces):
                    tiles[col, piece] = stacked(
                        loaded(place, 2 * pair, col, piece), loaded(place, 2 * pair + 1, col, piece)
                    )
            for step in range(SUB):
                for block, register in enumerate(spread(tiles, step, direction == 0 and not is_right)):
                    if is_right and direction == 0:
                        both = register.astype(F32)
                        for half in range(2):
                            put_even(spare, 2 * pair + half, step, block, both[half * SUB : (half + 1) * SUB])
                    else:
                        target = right_ref if is_right else left_ref
                        put(target, spare, (pair * SUB + step) * 2 * SUB, block, register)

    def unpack_last(channel, spare, group):
        tiles = {}
        for col in range(col_devices):
            for piece in range(pieces):
                tiles[col, piece] = stacked(
                    loaded(channel, group, col, piece), loaded(share + channel, group, col, piece)
                )
        before = None
        for step in range(SUB):
            now = [register.astype(F32) for register in spread(tiles, step, direction == 0)]
            for block in range(blocks):
                if direction == 0:
                    put_even(spare, group, step, block, now[block][SUB:])
                if step % 2:
                    start = (group * SUB + step - 1) * SUB
                    put(left_ref, spare, start, block, stacked(before[block][:SUB], now[block][:SUB]))
                    if direction == 1:
                        put(right_ref, spare, start, block, stacked(before[block][SUB:], now[block][SUB:]))
            before = now

    rights = {}

    def product(channel, pair):
        spare = channel % 2
        start = pair * 2 * SUB * row_devices
        at = slice(start, min(start + 2 * SUB * row_devices, groups * SUB * row_devices))
        if direction == 0:
            if pair == 0:
                right = [even_ref[spare, block, 0:total].astype(BF16) for block in range(blocks)]
                rights[channel] = jnp.concatenate(right, axis=1)
            summed = matmul(left_ref[spare, at, :], rights[channel], ((1,), (1,)))
        else:
            turned = matmul(pick[at], left_ref[spare], ((1,), (1,))).astype(BF16)
            summed = matmul(turned, right_ref[spare], ((1,), (0,)))
        for block in range(blocks):
            size = min(LANES, total - block * LANES)
            part = summed[:, block * LANES : block * LANES + size].astype(BF16)
            result_ref[channel, block, at, 0:size] = part

    def send(tiles, targets):
        for col in range(col_devices):
            moves = [(step, col * cols, cols, step * cols) for step in range(SUB)]
            registers = moved(lambda step, block: tiles[step, block], moves, pieces)
            for piece in range(pieces):
                both = registers[piece].astype(F32)
                for half, (channel, group) in enumerate(targets):
                    start = (col * row_devices * share + channel) * line + group * pieces + piece
                    packed[pl.ds(start, row_devices, stride=share * line), :] = (
                        both[half * SUB : (half + 1) * SUB]
                    )
        missing.difference_update(targets)

    missing = set((channel, group) for channel in range(share) for group in range(groups))
    waiting = list(range(sent_ref.shape[0] // (2 * SUB)))

    def finish():
        for unit in list(waiting):
            lines = range(unit * 2 * SUB, (unit + 1) * 2 * SUB)
            if any((at // line % share, at % line // pieces) in missing for at in lines):
                continue
            waiting.remove(unit)
            at = slice(unit * 2 * SUB, (unit + 1) * 2 * SUB)
            sent_ref[at, :] = packed[at, :].astype(BF16)

    def pack(channel, pair):
        if 2 * pair + 1 < groups:
            tiles = {}
            for step in range(SUB):
                for block in range(blocks):
                    start = (pair * SUB + step) * 2 * SUB
                    tiles[step, block] = result_ref[channel, block, start : start + 2 * SUB, :]
            send(tiles, [(channel, 2 * pair), (channel, 2 * pair + 1)])
        elif channel % 2:
            group = groups - 1
            tiles = {}
            for block in range(blocks):
                for step in range(0, SUB, 2):
                    start = (group * SUB + step) * SUB
                    low, high = [
                        result_ref[one, block, start : start + 2 * SUB, :].astype(F32)
                        for one in (channel - 1, channel)
                    ]
                    tiles[step, block] = stacked(low[:SUB], high[:SUB])
                    tiles[step + 1, block] = stacked(low[SUB:], high[SUB:])
            send(tiles, [(channel - 1, group), (channel, group)])

    widen(0)
    for pair in range(pairs):
        if pair + 1 < pairs:
            widen(pair + 1)
        elif direction == 0:
            prepare_weights(w_ref, wo_ref, share, prepared)
        unpack(0, [pair])
    for channel in range(share):
        for pair in range(pairs):
            product(channel, pair)
            if channel > 0:
                pack(channel - 1, pair)
            if channel + 1 < share:
                unpack(channel + 1, [pair])
            elif pair > 0:
                pack(channel, pair - 1)
    finish()
    pack(share - 1, pairs - 1)
    finish()


def by_channels(pair, token_mask, chain_ids, chain_bias, in_weights, out_weights, row_devices, col_devices):
    rows, cols, width = pair.shape
    devices = row_devices * col_devices
    share = width // devices
    lanes = SUB * cols
    pieces = lanes // LANES
    groups = rows // SUB
    chunk = groups * pieces * SUB
    spots = rows * cols
    line = groups * pieces
    total = row_devices * rows
    blocks = -(-total // LANES)
    tall = groups * SUB * row_devices
    params = pltpu.CompilerParams(vmem_limit_bytes=40 * 1024 * 1024)
    whole = pl.BlockSpec(memory_space=pltpu.VMEM)
    far = pl.BlockSpec(memory_space=pltpu.HBM)

    sent_shape = jax.ShapeDtypeStruct((devices, groups, pieces * SUB, LANES), BF16)
    sum_shape = jax.ShapeDtypeStruct((devices * share * line, LANES), BF16)
    state_shape = jax.ShapeDtypeStruct((width, spots), F32)
    mask_shape = jax.ShapeDtypeStruct((1, spots), F32)
    prepared_shape = jax.ShapeDtypeStruct((7 * width, width), BF16)
    padded_sum = pltpu.VMEM((-(-(devices + 1) * share * line // SUB) * SUB, LANES), F32)

    def exchange(array, rows):
        shape = (devices, rows) if rows % SUB == 0 else (devices, rows * 2 // SUB, SUB // 2)
        split = array.reshape(*shape, LANES)
        return lax.all_to_all(split, ("col", "row"), 0, 0, tiled=True).reshape(devices * rows, LANES)

    def triangle(direction, sent, *weights):
        wide_rows = (row_devices + 1) * wide_steps(col_devices * groups * pieces)[1]
        summed, *prepared = pl.pallas_call(
            functools.partial(
                triangle_kernel, direction, share, rows, cols, row_devices, col_devices, line
            ),
            out_shape=[sum_shape] + [prepared_shape] * (len(weights) // 2),
            in_specs=[whole] * (1 + len(weights)),
            out_specs=[whole] * (1 + len(weights) // 2),
            scratch_shapes=[
                pltpu.VMEM((-(-wide_rows // SUB) * SUB, LANES), F32),
                pltpu.VMEM((2, tall, blocks * LANES), BF16),
                pltpu.VMEM((2, tall, blocks * LANES), BF16),
                pltpu.VMEM((2, blocks, total + rows, LANES), F32),
                pltpu.VMEM((share, blocks, tall, LANES), BF16),
                padded_sum,
            ],
            compiler_params=params,
            name="triangle",
        )(exchange(sent, chunk), *weights)
        return exchange(summed, share * line), *prepared

    flat_pair = pair.reshape(spots, width)
    sent, gate, field, mask = pl.pallas_call(
        functools.partial(start_kernel, share, rows, cols),
        out_shape=[sent_shape, state_shape, state_shape, mask_shape],
        in_specs=[far] * 5,
        out_specs=[whole] * 4,
        scratch_shapes=[
            pltpu.VMEM((spots, width), BF16),
            pltpu.VMEM(in_weights.shape[1:], BF16),
            pltpu.VMEM((1, width), F32),
            pltpu.VMEM((1,) + token_mask.shape, jnp.int32),
            pltpu.VMEM((1,) + chain_ids.shape, jnp.int32),
            pltpu.SemaphoreType.DMA((6,)),
        ],
        compiler_params=params,
        name="start",
    )(*[
        pltpu.with_memory_space_constraint(array, pltpu.HBM)
        for array in (token_mask, chain_ids, flat_pair, chain_bias, in_weights)
    ])
    got, prepared = triangle(0, sent, in_weights, out_weights)
    sent, gate, field = pl.pallas_call(
        functools.partial(middle_kernel, share, rows, cols, line),
        out_shape=[sent_shape, state_shape, state_shape],
        in_specs=[whole] * 5,
        out_specs=[whole] * 3,
        scratch_shapes=[padded_sum],
        compiler_params=params,
        name="middle",
    )(mask, got, field, gate, prepared)
    (got,) = triangle(1, sent)
    out = pl.pallas_call(
        functools.partial(end_kernel, rows, cols, line),
        out_shape=jax.ShapeDtypeStruct((spots, width), BF16),
        in_specs=[whole] * 4,
        out_specs=far,
        scratch_shapes=[
            padded_sum,
            pltpu.VMEM((spots, width), BF16),
            pltpu.SemaphoreType.DMA((groups,)),
        ],
        compiler_params=params,
        name="end",
    )(got, field, gate, prepared)
    return out.reshape(pair.shape)


def gated_inputs(field, weights, pair_mask):
    width = weights.shape[0]
    normed = layer_norm(field).astype(BF16)
    projected = jnp.einsum("ijc,cd->ijd", normed, weights, preferred_element_type=F32)
    first = (
        jax.nn.sigmoid(projected[..., :width])
        * projected[..., width : 2 * width]
        * pair_mask[:, :, None]
    ).astype(BF16)
    second = (
        jax.nn.sigmoid(projected[..., 2 * width : 3 * width])
        * projected[..., 3 * width : 4 * width]
        * pair_mask[:, :, None]
    ).astype(BF16)
    gate_value = jax.nn.sigmoid(projected[..., 4 * width :])
    return (first, second, gate_value)


def update(field, summed, gate_value, weights):
    normed_sum = layer_norm(summed).astype(BF16)
    output = jnp.einsum("ijc,cd->ijd", normed_sum, weights, preferred_element_type=F32)
    return field + gate_value * output


def by_blocks(pair, token_mask, chain_ids, chain_bias, in_weights, out_weights):
    row_count = pair.shape[0]
    col_count = pair.shape[1]
    row_start = lax.axis_index("row") * row_count
    col_start = lax.axis_index("col") * col_count
    valid_rows = lax.dynamic_slice_in_dim(token_mask, row_start, row_count).astype(F32)
    valid_cols = lax.dynamic_slice_in_dim(token_mask, col_start, col_count).astype(F32)
    chain_rows = lax.dynamic_slice_in_dim(chain_ids, row_start, row_count)
    chain_cols = lax.dynamic_slice_in_dim(chain_ids, col_start, col_count)
    pair_mask = valid_rows[:, None] * valid_cols[None, :]
    same_chain = (chain_rows[:, None] == chain_cols[None, :]).astype(F32)
    field = pair.astype(F32) + same_chain[:, :, None] * chain_bias
    first, second, gate_value = gated_inputs(field, in_weights[0], pair_mask)
    second_rows = lax.all_gather(second, "row", axis=0, tiled=True)
    part = jnp.einsum("jkc,ikc->jic", second_rows, first, preferred_element_type=F32).astype(BF16)
    summed = lax.psum_scatter(part, "col", scatter_dimension=0, tiled=True).astype(F32)
    summed = jnp.transpose(summed, (1, 0, 2))
    field = update(field, summed, gate_value, out_weights[0])
    first, second, gate_value = gated_inputs(field, in_weights[1], pair_mask)
    first_cols = lax.all_gather(first, "col", axis=1, tiled=True)
    part = jnp.einsum("kic,kjc->ijc", first_cols, second, preferred_element_type=F32).astype(BF16)
    summed = lax.psum_scatter(part, "row", scatter_dimension=0, tiled=True).astype(F32)
    field = update(field, summed, gate_value, out_weights[1])
    return field.astype(BF16)


def solution(mesh):
    row_devices, col_devices = mesh.shape["row"], mesh.shape["col"]

    def per_device(pair, *rest):
        rows, cols, width = pair.shape
        devices = row_devices * col_devices
        fits = (
            width % devices == 0
            and 2 * (width // devices) == SUB
            and row_devices == SUB
            and rows % SUB == 0
            and rows >= 3 * SUB
            and (SUB * cols) % LANES == 0
            and max(rows, cols) <= LANES
        )
        if fits:
            return by_channels(pair, *rest, row_devices, col_devices)
        return by_blocks(pair, *rest)

    return jax.shard_map(
        per_device,
        mesh=mesh,
        in_specs=(P("row", "col", None), P(), P(), P(), P(), P()),
        out_specs=P("row", "col", None),
        check_vma=False,
    )
```

```python
import functools

import jax
import jax.numpy as jnp
from jax import lax
from jax.experimental import pallas as pl
from jax.experimental.pallas import tpu as pltpu
from jax.sharding import PartitionSpec as P

LANES = 128
SUB = 8
F32 = jnp.float32
BF16 = jnp.bfloat16


def layer_norm(values, axis=-1):
    center = values - jnp.mean(values, axis=axis, keepdims=True)
    spread = jnp.mean(center * center, axis=axis, keepdims=True)
    return center * lax.rsqrt(spread + 1e-05)


def matmul(left, right, dims):
    return lax.dot_general(left, right, (dims, ((), ())), preferred_element_type=F32)


def identity(size, scale):
    row = lax.broadcasted_iota(jnp.int32, (size, size), 0)
    col = lax.broadcasted_iota(jnp.int32, (size, size), 1)
    return jnp.where(row == col, scale, 0.0).astype(BF16)


def column(row_ref):
    width = row_ref.shape[1]
    return jnp.broadcast_to(row_ref[...], (width, width)).T[:, 0:1]


def transposed(weights, scale):
    eye = identity(weights.shape[1], scale)
    return matmul(eye, weights, ((1,), (1,))).astype(BF16)


def interleaved(first, second, share):
    width = first.shape[1]
    both = jnp.concatenate([first, second], axis=1)
    row = lax.broadcasted_iota(jnp.int32, (2 * width, 1), 0)
    col = lax.broadcasted_iota(jnp.int32, (2 * width, 2 * width), 1)
    owner, place = row // (2 * share), row % (2 * share)
    source = owner * share + place % share + jnp.where(place >= share, width, 0)
    pick = jnp.where(col == source, 0.5, 0.0).astype(BF16)
    return matmul(pick, both, ((1,), (1,))).astype(BF16)


def load_in_weights(weights, share):
    width = weights.shape[0]
    blocks = [weights[:, k * width : (k + 1) * width] for k in range(5)]
    return (
        interleaved(blocks[0], blocks[2], share),
        interleaved(blocks[1], blocks[3], share),
        transposed(blocks[4], 0.5),
    )


def token_vectors(tokens, row_start, col_start, rows, cols):
    groups = rows // SUB
    wide = tokens.shape[1]
    many = jnp.broadcast_to(tokens.astype(F32), (SUB, wide))
    lane = lax.broadcasted_iota(jnp.int32, (1, SUB * cols), 1)
    at_row = jnp.zeros_like(lane)
    for step in range(1, SUB):
        at_row = at_row + jnp.where(lane >= step * cols, 1, 0)
    at_col = lane - at_row * cols
    key = lax.broadcasted_iota(jnp.int32, (LANES, SUB * cols), 0)
    pick_row = jnp.where(key == at_row, 1.0, 0.0).astype(BF16)
    pick_col = jnp.where(key == at_col, 1.0, 0.0).astype(BF16)

    def window(start):
        return pltpu.roll(many, wide - start, 1)[:, :LANES]

    by_col = matmul(window(col_start).astype(BF16), pick_col, ((1,), (0,)))[0:1]
    windows = [window(row_start + group * SUB)[0:1] for group in range(groups)]
    windows.append(jnp.zeros((-groups % SUB, LANES), F32))
    by_row = matmul(jnp.concatenate(windows, axis=0).astype(BF16), pick_row, ((1,), (0,)))
    by_row = by_row.astype(jnp.int32)
    by_col = by_col.astype(jnp.int32)
    masks = (by_row & by_col & 1).astype(F32)
    sames = jnp.where((by_row >> 1) == (by_col >> 1), 1.0, 0.0)
    return masks, sames


def staged(count, stages):
    held = {}
    for step in range(count + len(stages) - 1):
        for number, stage in enumerate(stages):
            item = step - number
            if 0 <= item < count:
                held[item] = stage(item, held.get(item))


def statistics(values):
    center = values - jnp.mean(values, axis=0, keepdims=True)
    spread = jnp.mean(center * center, axis=0, keepdims=True)
    return center, lax.rsqrt(spread + 1e-05)


def normalised(halves):
    center, scale = halves
    return (center * scale).astype(BF16)


def projected(halves, in_t):
    normed = normalised(halves)
    return [matmul(weights, normed, ((1,), (0,))) for weights in in_t]


def gated(products, mask, group, share, sent_ref, gate_ref):
    gates, values, gate = products
    width, lanes = gate.shape
    sent = (jnp.tanh(gates) * values + values) * mask
    for owner in range(width // share):
        block = sent[owner * 2 * share : (owner + 1) * 2 * share]
        lines = [block[:, at : at + LANES] for at in range(0, lanes, LANES)]
        sent_ref[owner, group] = jnp.concatenate(lines, axis=0).astype(BF16)
    gate_ref[:, group * lanes : (group + 1) * lanes] = jnp.tanh(gate)


def start_kernel(share, rows, cols, valid_hbm, chain_hbm, pair_hbm, bias_hbm, w_hbm,
                 sent_ref, gate_ref, field_ref, mask_ref,
                 pair_ref, w_ref, bias_ref, valid_ref, chain_ref, sems):
    lanes = SUB * cols
    groups = rows // SUB
    width = pair_ref.shape[1]
    count = valid_hbm.shape[0]
    started = []

    def copy(near, far):
        started.append(pltpu.make_async_copy(near, far, sems.at[len(started)]))
        started[-1].start()

    copy(w_hbm.at[0], w_ref)
    copy(valid_hbm, valid_ref.at[0])
    copy(chain_hbm, chain_ref.at[0])
    copy(bias_hbm, bias_ref.at[0])
    for at in (pl.ds(0, 2 * lanes), pl.ds(2 * lanes, (groups - 2) * lanes)):
        copy(pair_hbm.at[at], pair_ref.at[at])
    arriving = len(started)
    eye = identity(width, 1.0)
    row_start = lax.axis_index("row") * rows
    col_start = lax.axis_index("col") * cols
    started[0].wait()
    in_t = load_in_weights(w_ref[...], share)
    for number in range(1, arriving - 1):
        started[number].wait()

    def lift(group):
        if group == 2:
            started[arriving - 1].wait()
        rows_of = pair_ref[group * lanes : (group + 1) * lanes, :]
        return matmul(eye, rows_of, ((1,), (1,)))

    lifted = {0: lift(0)}
    tokens = chain_ref[...] * 2 + valid_ref[...]
    tokens = jnp.concatenate([tokens, jnp.zeros((1, -count % LANES), jnp.int32)], axis=1)
    masks, sames = token_vectors(tokens, row_start, col_start, rows, cols)
    bias_col = column(bias_ref)

    def make_field(group, _):
        at = slice(group * lanes, (group + 1) * lanes)
        if group + 1 < groups:
            lifted[group + 1] = lift(group + 1)
        field = lifted.pop(group) + bias_col * sames[group : group + 1]
        field_ref[:, at] = field
        mask_ref[:, at] = masks[group : group + 1]
        return statistics(field)

    def project(group, halves):
        return projected(halves, in_t)

    def finish(group, products):
        gated(products, masks[group : group + 1], group, share, sent_ref, gate_ref)

    staged(groups, (make_field, project, finish))


def received(wide, width, group, lanes, line):
    pieces = lanes // LANES
    parts = []
    for piece in range(pieces):
        parts.append(wide[pl.ds(group * pieces + piece, width, stride=line), :])
    return statistics(jnp.concatenate(parts, axis=1))


def middle_kernel(share, rows, cols, line, mask_ref, got_ref, field_in, gate_in, prepared,
                  sent_ref, gate_ref, field_ref, wide):
    lanes = SUB * cols
    *in_t, out_t, _ = prepared_parts(prepared)
    wide[: got_ref.shape[0], :] = got_ref[...].astype(F32)

    def span(group):
        return slice(group * lanes, (group + 1) * lanes)

    def receive(group, _):
        return received(wide, out_t.shape[1], group, lanes, line)

    def outgoing(group, halves):
        return matmul(out_t, normalised(halves), ((1,), (0,)))

    def update_field(group, output):
        at = span(group)
        field = field_in[:, at] + (gate_in[:, at] * output + output)
        field_ref[:, at] = field
        return statistics(field)

    def project(group, halves):
        return projected(halves, in_t)

    def finish(group, products):
        gated(products, mask_ref[:, span(group)], group, share, sent_ref, gate_ref)

    staged(rows // SUB, (receive, outgoing, update_field, project, finish))


def end_kernel(rows, cols, line, got_ref, field_in, gate_in, prepared, out_hbm, wide, out_ref, sems):
    lanes = SUB * cols
    out_t = prepared_parts(prepared)[-1]
    wide[: got_ref.shape[0], :] = got_ref[...].astype(F32)
    copies = []

    def receive(group, _):
        return received(wide, out_t.shape[1], group, lanes, line)

    def outgoing(group, halves):
        return matmul(out_t, normalised(halves), ((1,), (0,)))

    def finish(group, output):
        at = slice(group * lanes, (group + 1) * lanes)
        field = field_in[:, at] + (gate_in[:, at] * output + output)
        out_ref[at, :] = field.astype(BF16).T
        at = pl.ds(group * lanes, lanes)
        copies.append(pltpu.make_async_copy(out_ref.at[at], out_hbm.at[at], sems.at[group]))
        copies[-1].start()

    staged(rows // SUB, (receive, outgoing, finish))
    for copy in copies:
        copy.wait()


def moved(source, moves, count):
    shape = None
    lane = None
    targets = [[] for _ in range(count)]
    for row, begin, length, target in moves:
        shift = (target - begin) % LANES
        while length > 0:
            size = min(length, LANES - begin % LANES, LANES - target % LANES)
            targets[target // LANES].append((target % LANES, row, begin // LANES, shift))
            begin, target, length = begin + size, target + size, length - size
    rolled = {}
    registers = []
    for pieces in targets:
        value = None
        for start, row, register, shift in sorted(pieces, key=lambda piece: piece[0]):
            key = (row, register, shift)
            if key not in rolled:
                tile = source(row, register)
                rolled[key] = pltpu.roll(tile, shift, 1) if shift else tile
            if value is None:
                value = rolled[key]
            else:
                if lane is None:
                    shape = value.shape
                    lane = lax.broadcasted_iota(jnp.int32, shape, 1)
                value = jnp.where(lane < start, value, rolled[key])
        registers.append(value)
    return registers


def wide_steps(tiles):
    place_step = tiles + 1 - tiles % 2
    return place_step, SUB * place_step + 1


def row_order(groups, row_devices, rows, width):
    line = lax.broadcasted_iota(jnp.int32, (groups * SUB * row_devices, 1), 0)
    row, rest = line % row_devices, line // row_devices
    paired = groups // 2 * 2
    pair, inside = rest // (2 * SUB), rest % (2 * SUB)
    of_pair = (2 * pair + inside % 2) * SUB + inside // 2
    place = jnp.where(rest < paired * SUB, of_pair, rest)
    lane = lax.broadcasted_iota(jnp.int32, (groups * SUB * row_devices, width), 1)
    return jnp.where(lane == row * rows + place, 1.0, 0.0).astype(BF16)


def stacked(low, high):
    return jnp.concatenate([low, high], axis=0).astype(BF16)


def prepare_weights(w_ref, wo_ref, share, prepared):
    parts = [*load_in_weights(w_ref[1], share), transposed(wo_ref[0], 0.5), transposed(wo_ref[1], 0.5)]
    prepared[...] = jnp.concatenate(parts, axis=0)


def prepared_parts(prepared):
    width = prepared.shape[1]
    cuts = [0, 2, 4, 5, 6, 7]
    return [prepared[low * width : high * width, :] for low, high in zip(cuts, cuts[1:])]


def triangle_kernel(direction, share, rows, cols, row_devices, col_devices, line, *refs):
    if direction == 0:
        got_ref, w_ref, wo_ref, sent_ref, prepared, *refs = refs
    else:
        got_ref, sent_ref, *refs = refs
    wide, left_ref, right_ref, even_ref, turned_ref, result_ref, packed = refs
    groups = rows // SUB
    pieces = SUB * cols // LANES
    total = row_devices * rows
    blocks = -(-total // LANES)
    pairs = -(-groups // 2)
    rest = total - (blocks - 1) * LANES
    tail = lax.broadcasted_iota(jnp.int32, (2 * SUB, LANES), 1) < rest
    place_step, row_step = wide_steps(col_devices * groups * pieces)
    pick = row_order(groups, row_devices, rows, blocks * LANES) if direction == 1 else None

    def spot(tile):
        device, number = divmod(tile, groups * pieces)
        col, row = divmod(device, row_devices)
        return row * row_step + col * groups * pieces + number

    def widen(pair):
        for unit in range(got_ref.shape[0] // (2 * SUB)):
            owners = [tile % (groups * pieces) // pieces // 2 for tile in (2 * unit, 2 * unit + 1)]
            if min(owners) != pair:
                continue
            both = got_ref[unit * 2 * SUB : (unit + 1) * 2 * SUB, :].astype(F32)
            for half in range(2):
                at = pl.ds(spot(2 * unit + half), SUB, stride=place_step)
                wide[at, :] = both[half * SUB : (half + 1) * SUB]

    def loaded(place, group, col, piece):
        start = place * place_step + (col * groups + group) * pieces + piece
        return wide[pl.ds(start, row_devices, stride=row_step), :]

    def spread(tiles, step, cleared):
        moves = [(col, step * cols, cols, col * cols) for col in range(col_devices)]
        registers = moved(lambda col, piece: tiles[col, piece], moves, blocks)
        if cleared:
            registers[-1] = jnp.where(tail, registers[-1], jnp.zeros_like(registers[-1]))
        return registers

    def put(target, spare, start, block, value):
        target[spare, start : start + 2 * SUB, block * LANES : (block + 1) * LANES] = value

    def put_even(spare, group, step, block, value):
        even_ref[spare, block, pl.ds(group * SUB + step, row_devices, stride=rows), :] = value

    def unpack(channel, only=range(pairs)):
        spare = channel % 2
        for pair in only:
            if 2 * pair + 1 < groups:
                unpack_pair(channel, spare, pair)
            else:
                unpack_last(channel, spare, 2 * pair)

    def unpack_pair(channel, spare, pair):
        for is_right, place in ((False, channel), (True, share + channel)):
            tiles = {}
            for col in range(col_devices):
                for piece in range(pieces):
                    tiles[col, piece] = stacked(
                        loaded(place, 2 * pair, col, piece), loaded(place, 2 * pair + 1, col, piece)
                    )
            for step in range(SUB):
                for block, register in enumerate(spread(tiles, step, direction == 0 and not is_right)):
                    if is_right and direction == 0:
                        both = register.astype(F32)
                        for half in range(2):
                            put_even(spare, 2 * pair + half, step, block, both[half * SUB : (half + 1) * SUB])
                    else:
                        target = right_ref if is_right else left_ref
                        put(target, spare, (pair * SUB + step) * 2 * SUB, block, register)

    def unpack_last(channel, spare, group):
        tiles = {}
        for col in range(col_devices):
            for piece in range(pieces):
                tiles[col, piece] = stacked(
                    loaded(channel, group, col, piece), loaded(share + channel, group, col, piece)
                )
        before = None
        for step in range(SUB):
            now = [register.astype(F32) for register in spread(tiles, step, direction == 0)]
            for block in range(blocks):
                if direction == 0:
                    put_even(spare, group, step, block, now[block][SUB:])
                if step % 2:
                    start = (group * SUB + step - 1) * SUB
                    put(left_ref, spare, start, block, stacked(before[block][:SUB], now[block][:SUB]))
                    if direction == 1:
                        put(right_ref, spare, start, block, stacked(before[block][SUB:], now[block][SUB:]))
            before = now

    rights = {}

    def turn(channel):
        spare = channel % 2
        if direction == 1:
            turned = matmul(pick, left_ref[spare], ((1,), (1,)))
            turned_ref[spare] = turned.astype(BF16)

    def product(channel, pair):
        spare = channel % 2
        start = pair * 2 * SUB * row_devices
        at = slice(start, min(start + 2 * SUB * row_devices, groups * SUB * row_devices))
        if direction == 0:
            if pair == 0:
                right = [even_ref[spare, block, 0:total].astype(BF16) for block in range(blocks)]
                rights[channel] = jnp.concatenate(right, axis=1)
            summed = matmul(left_ref[spare, at, :], rights[channel], ((1,), (1,)))
        else:
            summed = matmul(turned_ref[spare, at, :], right_ref[spare], ((1,), (0,)))
        for block in range(blocks):
            size = min(LANES, total - block * LANES)
            part = summed[:, block * LANES : block * LANES + size].astype(BF16)
            result_ref[channel, block, at, 0:size] = part

    def send(tiles, targets):
        for col in range(col_devices):
            moves = [(step, col * cols, cols, step * cols) for step in range(SUB)]
            registers = moved(lambda step, block: tiles[step, block], moves, pieces)
            for piece in range(pieces):
                both = registers[piece].astype(F32)
                for half, (channel, group) in enumerate(targets):
                    start = (col * row_devices * share + channel) * line + group * pieces + piece
                    packed[pl.ds(start, row_devices, stride=share * line), :] = (
                        both[half * SUB : (half + 1) * SUB]
                    )
        missing.difference_update(targets)

    missing = set((channel, group) for channel in range(share) for group in range(groups))
    waiting = list(range(sent_ref.shape[0] // (2 * SUB)))

    def finish():
        for unit in list(waiting):
            lines = range(unit * 2 * SUB, (unit + 1) * 2 * SUB)
            if any((at // line % share, at % line // pieces) in missing for at in lines):
                continue
            waiting.remove(unit)
            at = slice(unit * 2 * SUB, (unit + 1) * 2 * SUB)
            sent_ref[at, :] = packed[at, :].astype(BF16)

    def pack(channel, pair):
        if 2 * pair + 1 < groups:
            tiles = {}
            for step in range(SUB):
                for block in range(blocks):
                    start = (pair * SUB + step) * 2 * SUB
                    tiles[step, block] = result_ref[channel, block, start : start + 2 * SUB, :]
            send(tiles, [(channel, 2 * pair), (channel, 2 * pair + 1)])
        elif channel % 2:
            group = groups - 1
            tiles = {}
            for block in range(blocks):
                for step in range(0, SUB, 2):
                    start = (group * SUB + step) * SUB
                    low, high = [
                        result_ref[one, block, start : start + 2 * SUB, :].astype(F32)
                        for one in (channel - 1, channel)
                    ]
                    tiles[step, block] = stacked(low[:SUB], high[:SUB])
                    tiles[step + 1, block] = stacked(low[SUB:], high[SUB:])
            send(tiles, [(channel - 1, group), (channel, group)])

    widen(0)
    for pair in range(pairs):
        if pair + 1 < pairs:
            widen(pair + 1)
        elif direction == 0:
            prepare_weights(w_ref, wo_ref, share, prepared)
        unpack(0, [pair])
    turn(0)
    for channel in range(share):
        for pair in range(pairs):
            product(channel, pair)
            if channel > 0:
                pack(channel - 1, pair)
            if channel + 1 < share:
                unpack(channel + 1, [pair])
            elif pair > 0:
                pack(channel, pair - 1)
        if channel + 1 < share:
            turn(channel + 1)
    finish()
    pack(share - 1, pairs - 1)
    finish()


def by_channels(pair, token_mask, chain_ids, chain_bias, in_weights, out_weights, row_devices, col_devices):
    rows, cols, width = pair.shape
    devices = row_devices * col_devices
    share = width // devices
    lanes = SUB * cols
    pieces = lanes // LANES
    groups = rows // SUB
    chunk = groups * pieces * SUB
    spots = rows * cols
    line = groups * pieces
    total = row_devices * rows
    blocks = -(-total // LANES)
    tall = groups * SUB * row_devices
    params = pltpu.CompilerParams(vmem_limit_bytes=40 * 1024 * 1024)
    whole = pl.BlockSpec(memory_space=pltpu.VMEM)
    far = pl.BlockSpec(memory_space=pltpu.HBM)

    sent_shape = jax.ShapeDtypeStruct((devices, groups, pieces * SUB, LANES), BF16)
    sum_shape = jax.ShapeDtypeStruct((devices * share * line, LANES), BF16)
    state_shape = jax.ShapeDtypeStruct((width, spots), F32)
    mask_shape = jax.ShapeDtypeStruct((1, spots), F32)
    prepared_shape = jax.ShapeDtypeStruct((7 * width, width), BF16)
    padded_sum = pltpu.VMEM((-(-(devices + 1) * share * line // SUB) * SUB, LANES), F32)

    def exchange(array, rows):
        shape = (devices, rows) if rows % SUB == 0 else (devices, rows * 2 // SUB, SUB // 2)
        split = array.reshape(*shape, LANES)
        return lax.all_to_all(split, ("col", "row"), 0, 0, tiled=True).reshape(devices * rows, LANES)

    def triangle(direction, sent, *weights):
        wide_rows = (row_devices + 1) * wide_steps(col_devices * groups * pieces)[1]
        summed, *prepared = pl.pallas_call(
            functools.partial(
                triangle_kernel, direction, share, rows, cols, row_devices, col_devices, line
            ),
            out_shape=[sum_shape] + [prepared_shape] * (len(weights) // 2),
            in_specs=[whole] * (1 + len(weights)),
            out_specs=[whole] * (1 + len(weights) // 2),
            scratch_shapes=[
                pltpu.VMEM((-(-wide_rows // SUB) * SUB, LANES), F32),
                pltpu.VMEM((2, tall, blocks * LANES), BF16),
                pltpu.VMEM((2, tall, blocks * LANES), BF16),
                pltpu.VMEM((2, blocks, total + rows, LANES), F32),
                pltpu.VMEM((2, tall, tall), BF16),
                pltpu.VMEM((share, blocks, tall, LANES), BF16),
                padded_sum,
            ],
            compiler_params=params,
            name="triangle",
        )(exchange(sent, chunk), *weights)
        return exchange(summed, share * line), *prepared

    flat_pair = pair.reshape(spots, width)
    sent, gate, field, mask = pl.pallas_call(
        functools.partial(start_kernel, share, rows, cols),
        out_shape=[sent_shape, state_shape, state_shape, mask_shape],
        in_specs=[far] * 5,
        out_specs=[whole] * 4,
        scratch_shapes=[
            pltpu.VMEM((spots, width), BF16),
            pltpu.VMEM(in_weights.shape[1:], BF16),
            pltpu.VMEM((1, width), F32),
            pltpu.VMEM((1,) + token_mask.shape, jnp.int32),
            pltpu.VMEM((1,) + chain_ids.shape, jnp.int32),
            pltpu.SemaphoreType.DMA((6,)),
        ],
        compiler_params=params,
        name="start",
    )(*[
        pltpu.with_memory_space_constraint(array, pltpu.HBM)
        for array in (token_mask, chain_ids, flat_pair, chain_bias, in_weights)
    ])
    got, prepared = triangle(0, sent, in_weights, out_weights)
    sent, gate, field = pl.pallas_call(
        functools.partial(middle_kernel, share, rows, cols, line),
        out_shape=[sent_shape, state_shape, state_shape],
        in_specs=[whole] * 5,
        out_specs=[whole] * 3,
        scratch_shapes=[padded_sum],
        compiler_params=params,
        name="middle",
    )(mask, got, field, gate, prepared)
    (got,) = triangle(1, sent)
    out = pl.pallas_call(
        functools.partial(end_kernel, rows, cols, line),
        out_shape=jax.ShapeDtypeStruct((spots, width), BF16),
        in_specs=[whole] * 4,
        out_specs=far,
        scratch_shapes=[
            padded_sum,
            pltpu.VMEM((spots, width), BF16),
            pltpu.SemaphoreType.DMA((groups,)),
        ],
        compiler_params=params,
        name="end",
    )(got, field, gate, prepared)
    return out.reshape(pair.shape)


def gated_inputs(field, weights, pair_mask):
    width = weights.shape[0]
    normed = layer_norm(field).astype(BF16)
    projected = jnp.einsum("ijc,cd->ijd", normed, weights, preferred_element_type=F32)
    first = (
        jax.nn.sigmoid(projected[..., :width])
        * projected[..., width : 2 * width]
        * pair_mask[:, :, None]
    ).astype(BF16)
    second = (
        jax.nn.sigmoid(projected[..., 2 * width : 3 * width])
        * projected[..., 3 * width : 4 * width]
        * pair_mask[:, :, None]
    ).astype(BF16)
    gate_value = jax.nn.sigmoid(projected[..., 4 * width :])
    return (first, second, gate_value)


def update(field, summed, gate_value, weights):
    normed_sum = layer_norm(summed).astype(BF16)
    output = jnp.einsum("ijc,cd->ijd", normed_sum, weights, preferred_element_type=F32)
    return field + gate_value * output


def by_blocks(pair, token_mask, chain_ids, chain_bias, in_weights, out_weights):
    row_count = pair.shape[0]
    col_count = pair.shape[1]
    row_start = lax.axis_index("row") * row_count
    col_start = lax.axis_index("col") * col_count
    valid_rows = lax.dynamic_slice_in_dim(token_mask, row_start, row_count).astype(F32)
    valid_cols = lax.dynamic_slice_in_dim(token_mask, col_start, col_count).astype(F32)
    chain_rows = lax.dynamic_slice_in_dim(chain_ids, row_start, row_count)
    chain_cols = lax.dynamic_slice_in_dim(chain_ids, col_start, col_count)
    pair_mask = valid_rows[:, None] * valid_cols[None, :]
    same_chain = (chain_rows[:, None] == chain_cols[None, :]).astype(F32)
    field = pair.astype(F32) + same_chain[:, :, None] * chain_bias
    first, second, gate_value = gated_inputs(field, in_weights[0], pair_mask)
    second_rows = lax.all_gather(second, "row", axis=0, tiled=True)
    part = jnp.einsum("jkc,ikc->jic", second_rows, first, preferred_element_type=F32).astype(BF16)
    summed = lax.psum_scatter(part, "col", scatter_dimension=0, tiled=True).astype(F32)
    summed = jnp.transpose(summed, (1, 0, 2))
    field = update(field, summed, gate_value, out_weights[0])
    first, second, gate_value = gated_inputs(field, in_weights[1], pair_mask)
    first_cols = lax.all_gather(first, "col", axis=1, tiled=True)
    part = jnp.einsum("kic,kjc->ijc", first_cols, second, preferred_element_type=F32).astype(BF16)
    summed = lax.psum_scatter(part, "row", scatter_dimension=0, tiled=True).astype(F32)
    field = update(field, summed, gate_value, out_weights[1])
    return field.astype(BF16)


def solution(mesh):
    row_devices, col_devices = mesh.shape["row"], mesh.shape["col"]

    def per_device(pair, *rest):
        rows, cols, width = pair.shape
        devices = row_devices * col_devices
        fits = (
            width % devices == 0
            and 2 * (width // devices) == SUB
            and row_devices == SUB
            and rows % SUB == 0
            and rows >= 3 * SUB
            and (SUB * cols) % LANES == 0
            and max(rows, cols) <= LANES
        )
        if fits:
            return by_channels(pair, *rest, row_devices, col_devices)
        return by_blocks(pair, *rest)

    return jax.shard_map(
        per_device,
        mesh=mesh,
        in_specs=(P("row", "col", None), P(), P(), P(), P(), P()),
        out_specs=P("row", "col", None),
        check_vma=False,
    )
```

```python
import functools

import jax
import jax.numpy as jnp
from jax import lax
from jax.experimental import pallas as pl
from jax.experimental.pallas import tpu as pltpu
from jax.sharding import PartitionSpec as P

LANES = 128
SUB = 8
F32 = jnp.float32
BF16 = jnp.bfloat16


def layer_norm(values, axis=-1):
    center = values - jnp.mean(values, axis=axis, keepdims=True)
    spread = jnp.mean(center * center, axis=axis, keepdims=True)
    return center * lax.rsqrt(spread + 1e-05)


def matmul(left, right, dims):
    return lax.dot_general(left, right, (dims, ((), ())), preferred_element_type=F32)


def identity(size, scale):
    row = lax.broadcasted_iota(jnp.int32, (size, size), 0)
    col = lax.broadcasted_iota(jnp.int32, (size, size), 1)
    return jnp.where(row == col, scale, 0.0).astype(BF16)


def column(row_ref):
    width = row_ref.shape[1]
    return jnp.broadcast_to(row_ref[...], (width, width)).T[:, 0:1]


def transposed(weights, scale):
    eye = identity(weights.shape[1], scale)
    return matmul(eye, weights, ((1,), (1,))).astype(BF16)


def interleaved(first, second, share):
    width = first.shape[1]
    both = jnp.concatenate([first, second], axis=1)
    row = lax.broadcasted_iota(jnp.int32, (2 * width, 1), 0)
    col = lax.broadcasted_iota(jnp.int32, (2 * width, 2 * width), 1)
    owner, place = row // (2 * share), row % (2 * share)
    source = owner * share + place % share + jnp.where(place >= share, width, 0)
    pick = jnp.where(col == source, 0.5, 0.0).astype(BF16)
    return matmul(pick, both, ((1,), (1,))).astype(BF16)


def load_in_weights(weights, share):
    width = weights.shape[0]
    blocks = [weights[:, k * width : (k + 1) * width] for k in range(5)]
    return (
        interleaved(blocks[0], blocks[2], share),
        interleaved(blocks[1], blocks[3], share),
        transposed(blocks[4], 0.5),
    )


def token_vectors(tokens, row_start, col_start, rows, cols):
    groups = rows // SUB
    wide = tokens.shape[1]
    many = jnp.broadcast_to(tokens.astype(F32), (SUB, wide))
    lane = lax.broadcasted_iota(jnp.int32, (1, SUB * cols), 1)
    at_row = jnp.zeros_like(lane)
    for step in range(1, SUB):
        at_row = at_row + jnp.where(lane >= step * cols, 1, 0)
    at_col = lane - at_row * cols
    key = lax.broadcasted_iota(jnp.int32, (LANES, SUB * cols), 0)
    pick_row = jnp.where(key == at_row, 1.0, 0.0).astype(BF16)
    pick_col = jnp.where(key == at_col, 1.0, 0.0).astype(BF16)

    def window(start):
        return pltpu.roll(many, wide - start, 1)[:, :LANES]

    by_col = matmul(window(col_start).astype(BF16), pick_col, ((1,), (0,)))[0:1]
    windows = [window(row_start + group * SUB)[0:1] for group in range(groups)]
    windows.append(jnp.zeros((-groups % SUB, LANES), F32))
    by_row = matmul(jnp.concatenate(windows, axis=0).astype(BF16), pick_row, ((1,), (0,)))
    by_row = by_row.astype(jnp.int32)
    by_col = by_col.astype(jnp.int32)
    masks = (by_row & by_col & 1).astype(F32)
    sames = jnp.where((by_row >> 1) == (by_col >> 1), 1.0, 0.0)
    return masks, sames


def staged(count, stages):
    held = {}
    for step in range(count + len(stages) - 1):
        for number, stage in enumerate(stages):
            item = step - number
            if 0 <= item < count:
                held[item] = stage(item, held.get(item))


def statistics(values):
    center = values - jnp.mean(values, axis=0, keepdims=True)
    spread = jnp.mean(center * center, axis=0, keepdims=True)
    return center, lax.rsqrt(spread + 1e-05)


def normalised(halves):
    center, scale = halves
    return (center * scale).astype(BF16)


def projected(halves, in_t):
    normed = normalised(halves)
    return [matmul(weights, normed, ((1,), (0,))) for weights in in_t]


def gated(products, mask, group, share, sent_ref, gate_ref):
    gates, values, gate = products
    width, lanes = gate.shape
    sent = (jnp.tanh(gates) * values + values) * mask
    for owner in range(width // share):
        block = sent[owner * 2 * share : (owner + 1) * 2 * share]
        lines = [block[:, at : at + LANES] for at in range(0, lanes, LANES)]
        sent_ref[owner, group] = jnp.concatenate(lines, axis=0).astype(BF16)
    gate_ref[:, group * lanes : (group + 1) * lanes] = jnp.tanh(gate)


def start_kernel(share, rows, cols, valid_hbm, chain_hbm, pair_hbm, bias_hbm, w_hbm,
                 sent_ref, gate_ref, field_ref, mask_ref,
                 pair_ref, w_ref, bias_ref, valid_ref, chain_ref, sems):
    lanes = SUB * cols
    groups = rows // SUB
    width = pair_ref.shape[1]
    count = valid_hbm.shape[0]
    started = []

    def copy(near, far):
        started.append(pltpu.make_async_copy(near, far, sems.at[len(started)]))
        started[-1].start()

    copy(w_hbm.at[0], w_ref)
    copy(valid_hbm, valid_ref.at[0])
    copy(chain_hbm, chain_ref.at[0])
    copy(bias_hbm, bias_ref.at[0])
    for at in (pl.ds(0, 2 * lanes), pl.ds(2 * lanes, (groups - 2) * lanes)):
        copy(pair_hbm.at[at], pair_ref.at[at])
    arriving = len(started)
    eye = identity(width, 1.0)
    row_start = lax.axis_index("row") * rows
    col_start = lax.axis_index("col") * cols
    started[0].wait()
    in_t = load_in_weights(w_ref[...], share)
    for number in range(1, arriving - 1):
        started[number].wait()

    def lift(group):
        if group == 2:
            started[arriving - 1].wait()
        rows_of = pair_ref[group * lanes : (group + 1) * lanes, :]
        return matmul(eye, rows_of, ((1,), (1,)))

    lifted = {0: lift(0)}
    tokens = chain_ref[...] * 2 + valid_ref[...]
    tokens = jnp.concatenate([tokens, jnp.zeros((1, -count % LANES), jnp.int32)], axis=1)
    masks, sames = token_vectors(tokens, row_start, col_start, rows, cols)
    bias_col = column(bias_ref)

    def make_field(group, _):
        at = slice(group * lanes, (group + 1) * lanes)
        if group + 1 < groups:
            lifted[group + 1] = lift(group + 1)
        field = lifted.pop(group) + bias_col * sames[group : group + 1]
        field_ref[:, at] = field
        mask_ref[:, at] = masks[group : group + 1]
        return statistics(field)

    def project(group, halves):
        return projected(halves, in_t)

    def finish(group, products):
        gated(products, masks[group : group + 1], group, share, sent_ref, gate_ref)

    staged(groups, (make_field, project, finish))


def received(wide, width, group, lanes, line):
    pieces = lanes // LANES
    parts = []
    for piece in range(pieces):
        parts.append(wide[pl.ds(group * pieces + piece, width, stride=line), :])
    return statistics(jnp.concatenate(parts, axis=1))


def middle_kernel(share, rows, cols, line, mask_ref, got_ref, field_in, gate_in, prepared,
                  sent_ref, gate_ref, field_ref, wide):
    lanes = SUB * cols
    *in_t, out_t, _ = prepared_parts(prepared)
    wide[: got_ref.shape[0], :] = got_ref[...].astype(F32)

    def span(group):
        return slice(group * lanes, (group + 1) * lanes)

    def receive(group, _):
        return received(wide, out_t.shape[1], group, lanes, line)

    def outgoing(group, halves):
        return matmul(out_t, normalised(halves), ((1,), (0,)))

    def update_field(group, output):
        at = span(group)
        field = field_in[:, at] + (gate_in[:, at] * output + output)
        field_ref[:, at] = field
        return statistics(field)

    def project(group, halves):
        return projected(halves, in_t)

    def finish(group, products):
        gated(products, mask_ref[:, span(group)], group, share, sent_ref, gate_ref)

    staged(rows // SUB, (receive, outgoing, update_field, project, finish))


def end_kernel(rows, cols, line, got_ref, field_in, gate_in, prepared, out_hbm, wide, out_ref, sems):
    lanes = SUB * cols
    out_t = prepared_parts(prepared)[-1]
    wide[: got_ref.shape[0], :] = got_ref[...].astype(F32)
    copies = []

    def receive(group, _):
        return received(wide, out_t.shape[1], group, lanes, line)

    def outgoing(group, halves):
        return matmul(out_t, normalised(halves), ((1,), (0,)))

    def finish(group, output):
        at = slice(group * lanes, (group + 1) * lanes)
        field = field_in[:, at] + (gate_in[:, at] * output + output)
        out_ref[at, :] = field.astype(BF16).T
        at = pl.ds(group * lanes, lanes)
        copies.append(pltpu.make_async_copy(out_ref.at[at], out_hbm.at[at], sems.at[group]))
        copies[-1].start()

    staged(rows // SUB, (receive, outgoing, finish))
    for copy in copies:
        copy.wait()


def moved(source, moves, count):
    shape = None
    lane = None
    targets = [[] for _ in range(count)]
    for row, begin, length, target in moves:
        shift = (target - begin) % LANES
        while length > 0:
            size = min(length, LANES - begin % LANES, LANES - target % LANES)
            targets[target // LANES].append((target % LANES, row, begin // LANES, shift))
            begin, target, length = begin + size, target + size, length - size
    rolled = {}
    registers = []
    for pieces in targets:
        value = None
        for start, row, register, shift in sorted(pieces, key=lambda piece: piece[0]):
            key = (row, register, shift)
            if key not in rolled:
                tile = source(row, register)
                rolled[key] = pltpu.roll(tile, shift, 1) if shift else tile
            if value is None:
                value = rolled[key]
            else:
                if lane is None:
                    shape = value.shape
                    lane = lax.broadcasted_iota(jnp.int32, shape, 1)
                value = jnp.where(lane < start, value, rolled[key])
        registers.append(value)
    return registers


def wide_steps(tiles):
    place_step = tiles + 1 - tiles % 2
    return place_step, SUB * place_step + 1


def row_order(groups, row_devices, rows, width):
    line = lax.broadcasted_iota(jnp.int32, (groups * SUB * row_devices, 1), 0)
    row, rest = line % row_devices, line // row_devices
    paired = groups // 2 * 2
    pair, inside = rest // (2 * SUB), rest % (2 * SUB)
    of_pair = (2 * pair + inside % 2) * SUB + inside // 2
    place = jnp.where(rest < paired * SUB, of_pair, rest)
    lane = lax.broadcasted_iota(jnp.int32, (groups * SUB * row_devices, width), 1)
    return jnp.where(lane == row * rows + place, 1.0, 0.0).astype(BF16)


def stacked(low, high):
    return jnp.concatenate([low, high], axis=0).astype(BF16)


def prepare_weights(w_ref, wo_ref, share, prepared):
    parts = [*load_in_weights(w_ref[1], share), transposed(wo_ref[0], 0.5), transposed(wo_ref[1], 0.5)]
    prepared[...] = jnp.concatenate(parts, axis=0)


def prepared_parts(prepared):
    width = prepared.shape[1]
    cuts = [0, 2, 4, 5, 6, 7]
    return [prepared[low * width : high * width, :] for low, high in zip(cuts, cuts[1:])]


def triangle_kernel(direction, share, rows, cols, row_devices, col_devices, line, *refs):
    if direction == 0:
        got_ref, w_ref, wo_ref, sent_ref, prepared, *refs = refs
    else:
        got_ref, sent_ref, *refs = refs
    wide, left_ref, right_ref, even_ref, turned_ref, result_ref, packed = refs
    groups = rows // SUB
    pieces = SUB * cols // LANES
    total = row_devices * rows
    blocks = -(-total // LANES)
    pairs = -(-groups // 2)
    rest = total - (blocks - 1) * LANES
    tail = lax.broadcasted_iota(jnp.int32, (2 * SUB, LANES), 1) < rest
    place_step, row_step = wide_steps(col_devices * groups * pieces)
    pick = row_order(groups, row_devices, rows, blocks * LANES) if direction == 1 else None

    def spot(tile):
        device, number = divmod(tile, groups * pieces)
        col, row = divmod(device, row_devices)
        return row * row_step + col * groups * pieces + number

    def widen(pair):
        for unit in range(got_ref.shape[0] // (2 * SUB)):
            owners = [tile % (groups * pieces) // pieces // 2 for tile in (2 * unit, 2 * unit + 1)]
            if min(owners) != pair:
                continue
            both = got_ref[unit * 2 * SUB : (unit + 1) * 2 * SUB, :].astype(F32)
            for half in range(2):
                at = pl.ds(spot(2 * unit + half), SUB, stride=place_step)
                wide[at, :] = both[half * SUB : (half + 1) * SUB]

    def loaded(place, group, col, piece):
        start = place * place_step + (col * groups + group) * pieces + piece
        return wide[pl.ds(start, row_devices, stride=row_step), :]

    def spread(tiles, step, cleared):
        moves = [(col, step * cols, cols, col * cols) for col in range(col_devices)]
        registers = moved(lambda col, piece: tiles[col, piece], moves, blocks)
        if cleared:
            registers[-1] = jnp.where(tail, registers[-1], jnp.zeros_like(registers[-1]))
        return registers

    def put(target, spare, start, block, value):
        target[spare, start : start + 2 * SUB, block * LANES : (block + 1) * LANES] = value

    def put_even(spare, group, step, block, value):
        even_ref[spare, block, pl.ds(group * SUB + step, row_devices, stride=rows), :] = value

    def unpack(channel, only=range(pairs)):
        spare = channel % 2
        for pair in only:
            if 2 * pair + 1 < groups:
                unpack_pair(channel, spare, pair)
            else:
                unpack_last(channel, spare, 2 * pair)

    def unpack_pair(channel, spare, pair):
        for is_right, place in ((False, channel), (True, share + channel)):
            tiles = {}
            for col in range(col_devices):
                for piece in range(pieces):
                    tiles[col, piece] = stacked(
                        loaded(place, 2 * pair, col, piece), loaded(place, 2 * pair + 1, col, piece)
                    )
            for step in range(SUB):
                for block, register in enumerate(spread(tiles, step, direction == 0 and not is_right)):
                    if is_right and direction == 0:
                        both = register.astype(F32)
                        for half in range(2):
                            put_even(spare, 2 * pair + half, step, block, both[half * SUB : (half + 1) * SUB])
                    else:
                        target = right_ref if is_right else left_ref
                        put(target, spare, (pair * SUB + step) * 2 * SUB, block, register)

    def unpack_last(channel, spare, group):
        tiles = {}
        for col in range(col_devices):
            for piece in range(pieces):
                tiles[col, piece] = stacked(
                    loaded(channel, group, col, piece), loaded(share + channel, group, col, piece)
                )
        before = None
        for step in range(SUB):
            now = [register.astype(F32) for register in spread(tiles, step, direction == 0)]
            for block in range(blocks):
                if direction == 0:
                    put_even(spare, group, step, block, now[block][SUB:])
                if step % 2:
                    start = (group * SUB + step - 1) * SUB
                    put(left_ref, spare, start, block, stacked(before[block][:SUB], now[block][:SUB]))
                    if direction == 1:
                        put(right_ref, spare, start, block, stacked(before[block][SUB:], now[block][SUB:]))
            before = now

    rights = {}

    def turn(channel):
        spare = channel % 2
        if direction == 1:
            turned = matmul(pick, left_ref[spare], ((1,), (1,)))
            turned_ref[spare] = turned.astype(BF16)

    def product(channel, pair):
        spare = channel % 2
        start = pair * 2 * SUB * row_devices
        at = slice(start, min(start + 2 * SUB * row_devices, groups * SUB * row_devices))
        if direction == 1:
            if pair > 0:
                return
            at = slice(0, groups * SUB * row_devices)
        if direction == 0:
            if pair == 0:
                right = [even_ref[spare, block, 0:total].astype(BF16) for block in range(blocks)]
                rights[channel] = jnp.concatenate(right, axis=1)
            summed = matmul(left_ref[spare, at, :], rights[channel], ((1,), (1,)))
        else:
            summed = matmul(turned_ref[spare, at, :], right_ref[spare], ((1,), (0,)))
        for block in range(blocks):
            size = min(LANES, total - block * LANES)
            part = summed[:, block * LANES : block * LANES + size].astype(BF16)
            result_ref[channel, block, at, 0:size] = part

    def send(tiles, targets):
        for col in range(col_devices):
            moves = [(step, col * cols, cols, step * cols) for step in range(SUB)]
            registers = moved(lambda step, block: tiles[step, block], moves, pieces)
            for piece in range(pieces):
                both = registers[piece].astype(F32)
                for half, (channel, group) in enumerate(targets):
                    start = (col * row_devices * share + channel) * line + group * pieces + piece
                    packed[pl.ds(start, row_devices, stride=share * line), :] = (
                        both[half * SUB : (half + 1) * SUB]
                    )
        missing.difference_update(targets)

    missing = set((channel, group) for channel in range(share) for group in range(groups))
    waiting = list(range(sent_ref.shape[0] // (2 * SUB)))

    def finish():
        for unit in list(waiting):
            lines = range(unit * 2 * SUB, (unit + 1) * 2 * SUB)
            if any((at // line % share, at % line // pieces) in missing for at in lines):
                continue
            waiting.remove(unit)
            at = slice(unit * 2 * SUB, (unit + 1) * 2 * SUB)
            sent_ref[at, :] = packed[at, :].astype(BF16)

    def pack(channel, pair):
        if 2 * pair + 1 < groups:
            tiles = {}
            for step in range(SUB):
                for block in range(blocks):
                    start = (pair * SUB + step) * 2 * SUB
                    tiles[step, block] = result_ref[channel, block, start : start + 2 * SUB, :]
            send(tiles, [(channel, 2 * pair), (channel, 2 * pair + 1)])
        elif channel % 2:
            group = groups - 1
            tiles = {}
            for block in range(blocks):
                for step in range(0, SUB, 2):
                    start = (group * SUB + step) * SUB
                    low, high = [
                        result_ref[one, block, start : start + 2 * SUB, :].astype(F32)
                        for one in (channel - 1, channel)
                    ]
                    tiles[step, block] = stacked(low[:SUB], high[:SUB])
                    tiles[step + 1, block] = stacked(low[SUB:], high[SUB:])
            send(tiles, [(channel - 1, group), (channel, group)])

    widen(0)
    for pair in range(pairs):
        if pair + 1 < pairs:
            widen(pair + 1)
        elif direction == 0:
            prepare_weights(w_ref, wo_ref, share, prepared)
        unpack(0, [pair])
    turn(0)
    for channel in range(share):
        for pair in range(pairs):
            product(channel, pair)
            if channel > 0:
                pack(channel - 1, pair)
            if channel + 1 < share:
                unpack(channel + 1, [pair])
            elif pair > 0:
                pack(channel, pair - 1)
        if channel + 1 < share:
            turn(channel + 1)
    finish()
    pack(share - 1, pairs - 1)
    finish()


def by_channels(pair, token_mask, chain_ids, chain_bias, in_weights, out_weights, row_devices, col_devices):
    rows, cols, width = pair.shape
    devices = row_devices * col_devices
    share = width // devices
    lanes = SUB * cols
    pieces = lanes // LANES
    groups = rows // SUB
    chunk = groups * pieces * SUB
    spots = rows * cols
    line = groups * pieces
    total = row_devices * rows
    blocks = -(-total // LANES)
    tall = groups * SUB * row_devices
    params = pltpu.CompilerParams(vmem_limit_bytes=40 * 1024 * 1024)
    whole = pl.BlockSpec(memory_space=pltpu.VMEM)
    far = pl.BlockSpec(memory_space=pltpu.HBM)

    sent_shape = jax.ShapeDtypeStruct((devices, groups, pieces * SUB, LANES), BF16)
    sum_shape = jax.ShapeDtypeStruct((devices * share * line, LANES), BF16)
    state_shape = jax.ShapeDtypeStruct((width, spots), F32)
    mask_shape = jax.ShapeDtypeStruct((1, spots), F32)
    prepared_shape = jax.ShapeDtypeStruct((7 * width, width), BF16)
    padded_sum = pltpu.VMEM((-(-(devices + 1) * share * line // SUB) * SUB, LANES), F32)

    def exchange(array, rows):
        shape = (devices, rows) if rows % SUB == 0 else (devices, rows * 2 // SUB, SUB // 2)
        split = array.reshape(*shape, LANES)
        return lax.all_to_all(split, ("col", "row"), 0, 0, tiled=True).reshape(devices * rows, LANES)

    def triangle(direction, sent, *weights):
        wide_rows = (row_devices + 1) * wide_steps(col_devices * groups * pieces)[1]
        summed, *prepared = pl.pallas_call(
            functools.partial(
                triangle_kernel, direction, share, rows, cols, row_devices, col_devices, line
            ),
            out_shape=[sum_shape] + [prepared_shape] * (len(weights) // 2),
            in_specs=[whole] * (1 + len(weights)),
            out_specs=[whole] * (1 + len(weights) // 2),
            scratch_shapes=[
                pltpu.VMEM((-(-wide_rows // SUB) * SUB, LANES), F32),
                pltpu.VMEM((2, tall, blocks * LANES), BF16),
                pltpu.VMEM((2, tall, blocks * LANES), BF16),
                pltpu.VMEM((2, blocks, total + rows, LANES), F32),
                pltpu.VMEM((2, tall, tall), BF16),
                pltpu.VMEM((share, blocks, tall, LANES), BF16),
                padded_sum,
            ],
            compiler_params=params,
            name="triangle",
        )(exchange(sent, chunk), *weights)
        return exchange(summed, share * line), *prepared

    flat_pair = pair.reshape(spots, width)
    sent, gate, field, mask = pl.pallas_call(
        functools.partial(start_kernel, share, rows, cols),
        out_shape=[sent_shape, state_shape, state_shape, mask_shape],
        in_specs=[far] * 5,
        out_specs=[whole] * 4,
        scratch_shapes=[
            pltpu.VMEM((spots, width), BF16),
            pltpu.VMEM(in_weights.shape[1:], BF16),
            pltpu.VMEM((1, width), F32),
            pltpu.VMEM((1,) + token_mask.shape, jnp.int32),
            pltpu.VMEM((1,) + chain_ids.shape, jnp.int32),
            pltpu.SemaphoreType.DMA((6,)),
        ],
        compiler_params=params,
        name="start",
    )(*[
        pltpu.with_memory_space_constraint(array, pltpu.HBM)
        for array in (token_mask, chain_ids, flat_pair, chain_bias, in_weights)
    ])
    got, prepared = triangle(0, sent, in_weights, out_weights)
    sent, gate, field = pl.pallas_call(
        functools.partial(middle_kernel, share, rows, cols, line),
        out_shape=[sent_shape, state_shape, state_shape],
        in_specs=[whole] * 5,
        out_specs=[whole] * 3,
        scratch_shapes=[padded_sum],
        compiler_params=params,
        name="middle",
    )(mask, got, field, gate, prepared)
    (got,) = triangle(1, sent)
    out = pl.pallas_call(
        functools.partial(end_kernel, rows, cols, line),
        out_shape=jax.ShapeDtypeStruct((spots, width), BF16),
        in_specs=[whole] * 4,
        out_specs=far,
        scratch_shapes=[
            padded_sum,
            pltpu.VMEM((spots, width), BF16),
            pltpu.SemaphoreType.DMA((groups,)),
        ],
        compiler_params=params,
        name="end",
    )(got, field, gate, prepared)
    return out.reshape(pair.shape)


def gated_inputs(field, weights, pair_mask):
    width = weights.shape[0]
    normed = layer_norm(field).astype(BF16)
    projected = jnp.einsum("ijc,cd->ijd", normed, weights, preferred_element_type=F32)
    first = (
        jax.nn.sigmoid(projected[..., :width])
        * projected[..., width : 2 * width]
        * pair_mask[:, :, None]
    ).astype(BF16)
    second = (
        jax.nn.sigmoid(projected[..., 2 * width : 3 * width])
        * projected[..., 3 * width : 4 * width]
        * pair_mask[:, :, None]
    ).astype(BF16)
    gate_value = jax.nn.sigmoid(projected[..., 4 * width :])
    return (first, second, gate_value)


def update(field, summed, gate_value, weights):
    normed_sum = layer_norm(summed).astype(BF16)
    output = jnp.einsum("ijc,cd->ijd", normed_sum, weights, preferred_element_type=F32)
    return field + gate_value * output


def by_blocks(pair, token_mask, chain_ids, chain_bias, in_weights, out_weights):
    row_count = pair.shape[0]
    col_count = pair.shape[1]
    row_start = lax.axis_index("row") * row_count
    col_start = lax.axis_index("col") * col_count
    valid_rows = lax.dynamic_slice_in_dim(token_mask, row_start, row_count).astype(F32)
    valid_cols = lax.dynamic_slice_in_dim(token_mask, col_start, col_count).astype(F32)
    chain_rows = lax.dynamic_slice_in_dim(chain_ids, row_start, row_count)
    chain_cols = lax.dynamic_slice_in_dim(chain_ids, col_start, col_count)
    pair_mask = valid_rows[:, None] * valid_cols[None, :]
    same_chain = (chain_rows[:, None] == chain_cols[None, :]).astype(F32)
    field = pair.astype(F32) + same_chain[:, :, None] * chain_bias
    first, second, gate_value = gated_inputs(field, in_weights[0], pair_mask)
    second_rows = lax.all_gather(second, "row", axis=0, tiled=True)
    part = jnp.einsum("jkc,ikc->jic", second_rows, first, preferred_element_type=F32).astype(BF16)
    summed = lax.psum_scatter(part, "col", scatter_dimension=0, tiled=True).astype(F32)
    summed = jnp.transpose(summed, (1, 0, 2))
    field = update(field, summed, gate_value, out_weights[0])
    first, second, gate_value = gated_inputs(field, in_weights[1], pair_mask)
    first_cols = lax.all_gather(first, "col", axis=1, tiled=True)
    part = jnp.einsum("kic,kjc->ijc", first_cols, second, preferred_element_type=F32).astype(BF16)
    summed = lax.psum_scatter(part, "row", scatter_dimension=0, tiled=True).astype(F32)
    field = update(field, summed, gate_value, out_weights[1])
    return field.astype(BF16)


def solution(mesh):
    row_devices, col_devices = mesh.shape["row"], mesh.shape["col"]

    def per_device(pair, *rest):
        rows, cols, width = pair.shape
        devices = row_devices * col_devices
        fits = (
            width % devices == 0
            and 2 * (width // devices) == SUB
            and row_devices == SUB
            and rows % SUB == 0
            and rows >= 3 * SUB
            and (SUB * cols) % LANES == 0
            and max(rows, cols) <= LANES
        )
        if fits:
            return by_channels(pair, *rest, row_devices, col_devices)
        return by_blocks(pair, *rest)

    return jax.shard_map(
        per_device,
        mesh=mesh,
        in_specs=(P("row", "col", None), P(), P(), P(), P(), P()),
        out_specs=P("row", "col", None),
        check_vma=False,
    )
```
